32 devices in a mesh: ctx: 8 (over y, x, core), img: 4 (over z).
Axes of the slice: x: 2, y: 2, z: 4, core: 2. Of those that a mesh axis runs over, the one named last changes fastest.
Arguments:
- text: bfloat16 [1024, 4096], P('ctx'), may hold values from -6 to 6
- input_gain: float32 [4096], replicated, may hold values from 0.5 to 2
- q_weight: bfloat16 [4096, 4096], P('ctx', 'img'), may hold values from -0.09375 to 0.09375
- kv_weight: bfloat16 [4096, 2048], P('ctx'), may hold values from -0.09375 to 0.09375
- o_weight: bfloat16 [4096, 4096], P('img', 'ctx'), may hold values from -0.5 to 0.5
- q_gain: float32 [128], replicated, may hold values from 0.5 to 12, as said below
- k_gain: float32 [128], replicated, may hold values from 0.5 to 12, as said below
- attn_gate: float32 [1], replicated, may hold values from 0.3 to 1.5
- vision: bfloat16 [8, 64, 4096], P('img', 'ctx'), may hold values from -6 to 6
- segment_ids: int32 [1024], P('ctx'), may hold values from 0 to 31, as said below
- seg_images: int32 [32, 2], replicated, may hold values from 0 to 7, as said below
- image_slot: int32 [8], replicated, may hold values from 0 to 7, each once
Outputs:
- mixed: bfloat16 [1024, 4096], P('ctx', 'img')
The draws below stay inside these ranges and needn't reach their ends.
Inputs may be any that keep to these rules, and one draw needn't show every extreme that they name: `segment_ids`: numbers never fall along the tokens; block c of 128 tokens uses numbers from c * 4 on, 1 to 4 segments a block, and some block has 4. `seg_images`: each row names 2 different images; the tokens of one block of 128 see at most 8 different images, and some block sees exactly 8. `image_slot`: A permutation. `q_gain`: Positive. `k_gain`: Positive.
All inputs are finite; a program needn't handle non-finite values.
Results may differ from the reference program's by a relative error of at most 0.022.
The reference program's roundings to bfloat16 on the way (of `hidden`, `query` and `context`) count: a program that leaves them out, or rounds other values in their place, can miss the bound.
Values may be sent and summed in bfloat16 or wider, within the bound.
No kernel may reach another device: no remote copies, remote signals or barrier semaphores. Data moves between devices by JAX's collectives and lax.ppermute only.
A program may use at most 64 MiB of HBM per device.

```python
import math
import jax
import jax.numpy as jnp
from jax import lax

D = 4096
HEADS = 32
KVH = 8
HD = 128
TOK_DEV = 128
SEG_DEV = 4
VIS = 2
QD = 4096
TOKENS = 1024
IMAGES = 8
VT = 64
N_IMG = 4


def shared_layout(key):
    blocks = TOKENS // TOK_DEV
    key_count, key_force = jax.random.split(jax.random.fold_in(key, 7))
    counts = jax.random.randint(key_count, (blocks,), 1, SEG_DEV + 1)
    forced = jax.random.randint(key_force, (), 0, blocks)
    counts = jnp.where(jnp.arange(blocks) == forced, SEG_DEV, counts)
    return (counts, forced)


def draw_segment_ids(key, part):
    counts, forced = shared_layout(key)
    key = jax.random.fold_in(key, 11)
    blocks = TOKENS // TOK_DEV
    block_keys = jax.random.split(key, blocks)
    perms = jax.vmap(lambda single: jax.random.permutation(single, TOK_DEV - 1))(block_keys) + 1
    cuts = perms[:, :SEG_DEV - 1]
    used = jnp.arange(SEG_DEV - 1)[None, :] < counts[:, None] - 1
    cuts = jnp.where(used, cuts, TOK_DEV)
    positions = jnp.arange(TOK_DEV)
    local = jnp.sum((cuts[:, None, :] <= positions[None, :, None]).astype(jnp.int32), axis=2)
    numbers = local + jnp.arange(blocks)[:, None] * SEG_DEV
    return numbers.reshape(TOKENS).astype(jnp.int32)


def draw_seg_images(key, part):
    counts, forced = shared_layout(key)
    key = jax.random.fold_in(key, 13)
    blocks = TOKENS // TOK_DEV
    segments = blocks * SEG_DEV
    key_rows, key_force = jax.random.split(key)
    rows = jax.vmap(lambda single: jax.random.permutation(single, IMAGES)[:VIS])(jax.random.split(key_rows, segments))
    spread = jax.random.permutation(key_force, IMAGES)
    forced_rows = spread[jnp.arange(SEG_DEV * VIS) % IMAGES].reshape(SEG_DEV, VIS)
    owner = jnp.arange(segments) // SEG_DEV
    local = jnp.arange(segments) % SEG_DEV
    rows = jnp.where((owner == forced)[:, None], forced_rows[local], rows)
    return rows.astype(jnp.int32)


def draw_q_gain(key, part):
    key = jax.random.fold_in(key, 17)
    level = jax.random.uniform(key, (HD,), jnp.float32)
    return 0.5 * 5.0 ** level


def draw_k_gain(key, part):
    key = jax.random.fold_in(key, 19)
    level = jax.random.uniform(key, (HD,), jnp.float32)
    return 0.5 * 5.0 ** level


def steps_of(own_key, dims, cuts, low, largest):
    loudness = 1.0
    for dim, parts in cuts:
        steps = jax.random.uniform(jax.random.fold_in(jax.random.fold_in(own_key, 6), dim), (parts,), jnp.float32, low / len(cuts), largest / len(cuts))
        loudness = loudness * jnp.repeat(jnp.exp(steps), dims[dim] // parts).reshape((-1,) + (1,) * (len(dims) - 1 - dim))
    return loudness


def gaussian(stream_key, extent, deviation, most, cuts=(), kind=jnp.bfloat16):
    array = jax.random.normal(stream_key, extent, jnp.float32) * deviation
    if len(cuts) > 0:
        array = steps_of(stream_key, extent, cuts, -0.22, 0.18) * array
    return jnp.clip(array, min=-most, max=most).astype(kind)


def setup_inputs(seed: int = 0) -> dict:
    key_list = jax.random.split(jax.random.key(seed), 13)
    return {
        "text": gaussian(key_list[0], (TOKENS, D), 1.0, 6.0, ((0, 8),)),
        "input_gain": jnp.clip(jnp.exp(jax.random.uniform(key_list[1], (D,), jnp.float32, math.log(0.5), math.log(2.0))), 0.5, 2.0),
        "q_weight": gaussian(key_list[2], (D, QD), D ** -0.5, 0.09375, ((0, 8), (1, 4))),
        "kv_weight": gaussian(key_list[3], (D, 2 * KVH * HD), D ** -0.5, 0.09375, ((0, 8),)),
        "o_weight": gaussian(key_list[4], (QD, D), (QD // 32) ** -0.5, 0.5, ((0, 4), (1, 8))),
        "q_gain": draw_q_gain(jax.random.fold_in(key_list[12], 71), 0),
        "k_gain": draw_k_gain(jax.random.fold_in(key_list[12], 71), 0),
        "attn_gate": jnp.clip(jax.random.uniform(key_list[7], (1,), jnp.float32, 0.3, 1.5), 0.3, 1.5),
        "vision": gaussian(key_list[8], (IMAGES, VT, D), 1.0, 6.0, ((0, 4), (1, 8))),
        "segment_ids": draw_segment_ids(jax.random.fold_in(key_list[12], 71), 0),
        "seg_images": draw_seg_images(jax.random.fold_in(key_list[12], 71), 0),
        "image_slot": jax.random.permutation(key_list[11], IMAGES).astype(jnp.int32),
    }


EPS = 1e-05

def head_norm(values, gain):
    mean_sq = lax.optimization_barrier(jnp.mean(values * values, axis=-1, keepdims=True))
    return values * lax.rsqrt(mean_sq + EPS) * gain

def reference(text, input_gain, q_weight, kv_weight, o_weight, q_gain, k_gain, attn_gate, vision, segment_ids, seg_images, image_slot):
    hidden = head_norm(text.astype(jnp.float32), input_gain).astype(jnp.bfloat16)
    query = jnp.dot(hidden, q_weight, preferred_element_type=jnp.float32)
    query = head_norm(query.reshape(TOKENS, HEADS, HD), q_gain).astype(jnp.bfloat16)
    flat_vision = vision.reshape(IMAGES * VT, D)
    projected = jnp.dot(flat_vision, kv_weight, preferred_element_type=jnp.float32)
    projected = projected.reshape(IMAGES, VT, KVH, 2, HD)
    keys = head_norm(projected[:, :, :, 0], k_gain).astype(jnp.bfloat16)
    values = projected[:, :, :, 1].astype(jnp.bfloat16)
    slots = jnp.take(image_slot, jnp.take(seg_images, segment_ids, axis=0), axis=0).astype(jnp.int32)
    nblocks = TOKENS // TOK_DEV
    group = HEADS // KVH
    scale = HD ** (-0.5)

    def one_block(index):
        block = index // KVH
        head = index % KVH
        start = (block * TOK_DEV).astype(jnp.int32)
        q_block = lax.dynamic_slice_in_dim(query, start, TOK_DEV, 0)
        q_block = lax.dynamic_slice_in_dim(q_block, (head * group).astype(jnp.int32), group, 1).astype(jnp.float32)
        s_block = lax.dynamic_slice_in_dim(slots, start, TOK_DEV, 0)
        k_head = lax.dynamic_index_in_dim(keys, head, 2, keepdims=False)
        v_head = lax.dynamic_index_in_dim(values, head, 2, keepdims=False)
        k_sel = jnp.take(k_head, s_block, axis=0).reshape(TOK_DEV, VIS * VT, HD).astype(jnp.float32)
        v_sel = jnp.take(v_head, s_block, axis=0).reshape(TOK_DEV, VIS * VT, HD).astype(jnp.float32)
        scores = jnp.einsum('tgd,tkd->tgk', q_block, k_sel) * scale
        top = lax.optimization_barrier(jnp.max(scores, axis=-1, keepdims=True))
        weights = jnp.exp(scores - top)
        total = lax.optimization_barrier(jnp.sum(weights, axis=-1))
        rounded = lax.optimization_barrier(weights.astype(jnp.bfloat16)).astype(jnp.float32)
        context = jnp.einsum('tgk,tkd->tgd', rounded, v_sel) / total[..., None]
        return context.astype(jnp.bfloat16)
    outs = lax.map(one_block, jnp.arange(nblocks * KVH, dtype=jnp.int32))
    context = outs.reshape(nblocks, KVH, TOK_DEV, group, HD).transpose(0, 2, 1, 3, 4).reshape(TOKENS, QD)
    width_group = QD // N_IMG

    def add_group(index, total):
        part_context = lax.dynamic_slice_in_dim(context, index * width_group, width_group, 1)
        part_weight = lax.dynamic_slice_in_dim(o_weight, index * width_group, width_group, 0)
        part = jnp.dot(part_context, part_weight, preferred_element_type=jnp.float32).astype(jnp.bfloat16)
        return total + lax.optimization_barrier(part).astype(jnp.float32)
    update = lax.fori_loop(0, N_IMG, add_group, jnp.zeros((TOKENS, D), jnp.float32))
    return (text.astype(jnp.float32) + jnp.tanh(attn_gate[0]) * update).astype(jnp.bfloat16)
```

```python
import jax
import jax.numpy as jnp
from jax import lax
from jax.sharding import PartitionSpec as P

KVH = 8


EPS = 1e-05
NEG = -1e30


def head_norm(values, gain):
    mean_sq = jnp.mean(values * values, axis=-1, keepdims=True)
    return values * lax.rsqrt(mean_sq + EPS) * gain


def attend(query, keys, values, mask):
    scale = query.shape[-1] ** (-0.5)
    scores = jnp.einsum("tkgd,nkd->tkgn", query, keys, preferred_element_type=jnp.float32) * scale
    live = mask[:, None, None, :]
    scores = jnp.where(live, scores, NEG)
    top = jnp.max(scores, axis=-1)
    weights = jnp.where(live, jnp.exp(scores - top[..., None]), 0.0)
    total = jnp.sum(weights, axis=-1)
    acc = jnp.einsum(
        "tkgn,nkd->tkgd", weights.astype(jnp.bfloat16), values, preferred_element_type=jnp.float32
    )
    return acc / total[..., None]


def body(
    text,
    input_gain,
    q_weight,
    kv_weight,
    o_weight,
    q_gain,
    k_gain,
    attn_gate,
    vision,
    segment_ids,
    seg_images,
    image_slot,
):
    tokens_here = text.shape[0]
    head_dim = q_gain.shape[0]
    ctx_count = lax.axis_size("ctx")
    img_count = lax.axis_size("img")
    heads_here = q_weight.shape[1] // head_dim
    kv_heads = max(1, KVH // img_count)
    group = heads_here // kv_heads
    slots_here, vt_dev = vision.shape[:2]
    rows_here = slots_here * vt_dev

    o_full = lax.all_gather(o_weight, "ctx", axis=1, tiled=True)
    vision_cols = lax.all_to_all(
        vision.reshape(rows_here, -1), "ctx", split_axis=1, concat_axis=0, tiled=True
    )
    hidden = head_norm(text.astype(jnp.float32), input_gain).astype(jnp.bfloat16)
    hidden_cols = lax.all_to_all(hidden, "ctx", split_axis=1, concat_axis=0, tiled=True)

    kv_share = jnp.dot(vision_cols, kv_weight, preferred_element_type=jnp.float32)
    kv_shares = lax.all_to_all(
        kv_share.reshape(ctx_count, rows_here, -1), "ctx", split_axis=0, concat_axis=0, tiled=True
    )
    projected = jnp.sum(kv_shares, axis=0).reshape(rows_here, KVH, 2, head_dim)
    keys = head_norm(projected[:, :, 0], k_gain).astype(jnp.bfloat16)
    values = projected[:, :, 1].astype(jnp.bfloat16)
    kv_rows = jnp.stack((keys, values), axis=2)
    owners = jnp.arange(img_count)[:, None] * KVH // img_count + jnp.arange(kv_heads)[None, :]
    kv_out = jnp.take(kv_rows, owners, axis=1).transpose(1, 0, 2, 3, 4)
    kv_in = lax.all_to_all(kv_out, "img", split_axis=0, concat_axis=0, tiled=True)
    kv_all = lax.all_gather(kv_in, "ctx", axis=0, tiled=False)

    q_share = jnp.dot(hidden_cols, q_weight, preferred_element_type=jnp.float32)
    q_shares = lax.all_to_all(
        q_share.astype(jnp.bfloat16).reshape(ctx_count, tokens_here, -1),
        "ctx",
        split_axis=0,
        concat_axis=0,
        tiled=True,
    )
    query = jnp.sum(q_shares.astype(jnp.float32), axis=0)
    query = head_norm(query.reshape(tokens_here, kv_heads, group, head_dim), q_gain).astype(
        jnp.bfloat16
    )

    slots = img_count * slots_here
    own_slots = jnp.take(image_slot, jnp.take(seg_images, segment_ids, axis=0), axis=0)
    slot_ids = jnp.arange(slots, dtype=jnp.int32)
    sees = jnp.any(own_slots[:, :, None] == slot_ids[None, None, :], axis=1)
    flat = kv_all.reshape(ctx_count * slots * vt_dev, kv_heads, 2, head_dim)
    mask = jnp.broadcast_to(
        sees[:, None, :, None], (tokens_here, ctx_count, slots, vt_dev)
    ).reshape(tokens_here, -1)
    context = attend(query, flat[:, :, 0], flat[:, :, 1], mask)
    context = context.astype(jnp.bfloat16).reshape(tokens_here, heads_here * head_dim)
    partial_terms = jnp.dot(context, o_full, preferred_element_type=jnp.float32)
    width = partial_terms.shape[1] // img_count
    shares = lax.all_to_all(
        partial_terms.astype(jnp.bfloat16).reshape(tokens_here, img_count, width),
        "img",
        split_axis=1,
        concat_axis=1,
        tiled=True,
    )
    update = jnp.sum(shares.astype(jnp.float32), axis=1)
    own_text = lax.dynamic_slice_in_dim(text, lax.axis_index("img") * width, width, 1)
    return (own_text.astype(jnp.float32) + jnp.tanh(attn_gate[0]) * update).astype(jnp.bfloat16)


def solution(mesh):
    return jax.shard_map(
        body,
        mesh=mesh,
        in_specs=(
            P("ctx", None),
            P(),
            P("ctx", "img"),
            P("ctx", None),
            P("img", "ctx"),
            P(),
            P(),
            P(),
            P("img", "ctx", None),
            P("ctx"),
            P(),
            P(),
        ),
        out_specs=P("ctx", "img"),
        check_vma=False,
    )
```

```python
import jax
import jax.numpy as jnp
from jax import lax
from jax.sharding import PartitionSpec as P

KVH = 8


EPS = 1e-05
NEG = -1e30


def head_norm(values, gain):
    mean_sq = jnp.mean(values * values, axis=-1, keepdims=True)
    return values * lax.rsqrt(mean_sq + EPS) * gain


def attend(query, keys, values, mask):
    scale = query.shape[-1] ** (-0.5)
    scores = jnp.einsum("tkgd,nkd->tkgn", query, keys, preferred_element_type=jnp.float32) * scale
    live = mask[:, None, None, :]
    scores = jnp.where(live, scores, NEG)
    top = jnp.max(scores, axis=-1)
    weights = jnp.where(live, jnp.exp(scores - top[..., None]), 0.0)
    total = jnp.sum(weights, axis=-1)
    acc = jnp.einsum(
        "tkgn,nkd->tkgd", weights.astype(jnp.bfloat16), values, preferred_element_type=jnp.float32
    )
    return acc / total[..., None]


def general(
    text,
    input_gain,
    q_weight,
    kv_weight,
    o_weight,
    q_gain,
    k_gain,
    attn_gate,
    vision,
    segment_ids,
    seg_images,
    image_slot,
):
    tokens_here = text.shape[0]
    head_dim = q_gain.shape[0]
    ctx_count = lax.axis_size("ctx")
    img_count = lax.axis_size("img")
    heads_here = q_weight.shape[1] // head_dim
    kv_heads = max(1, KVH // img_count)
    group = heads_here // kv_heads
    slots_here, vt_dev = vision.shape[:2]
    rows_here = slots_here * vt_dev

    o_full = lax.all_gather(o_weight, "ctx", axis=1, tiled=True)
    vision_cols = lax.all_to_all(
        vision.reshape(rows_here, -1), "ctx", split_axis=1, concat_axis=0, tiled=True
    )
    hidden = head_norm(text.astype(jnp.float32), input_gain).astype(jnp.bfloat16)
    hidden_cols = lax.all_to_all(hidden, "ctx", split_axis=1, concat_axis=0, tiled=True)

    kv_share = jnp.dot(vision_cols, kv_weight, preferred_element_type=jnp.float32)
    kv_shares = lax.all_to_all(
        kv_share.reshape(ctx_count, rows_here, -1), "ctx", split_axis=0, concat_axis=0, tiled=True
    )
    projected = jnp.sum(kv_shares, axis=0).reshape(rows_here, KVH, 2, head_dim)
    keys = head_norm(projected[:, :, 0], k_gain).astype(jnp.bfloat16)
    values = projected[:, :, 1].astype(jnp.bfloat16)
    kv_rows = jnp.stack((keys, values), axis=2)
    owners = jnp.arange(img_count)[:, None] * KVH // img_count + jnp.arange(kv_heads)[None, :]
    kv_out = jnp.take(kv_rows, owners, axis=1).transpose(1, 0, 2, 3, 4)
    kv_in = lax.all_to_all(kv_out, "img", split_axis=0, concat_axis=0, tiled=True)
    kv_all = lax.all_gather(kv_in, "ctx", axis=0, tiled=False)

    q_share = jnp.dot(hidden_cols, q_weight, preferred_element_type=jnp.float32)
    q_shares = lax.all_to_all(
        q_share.astype(jnp.bfloat16).reshape(ctx_count, tokens_here, -1),
        "ctx",
        split_axis=0,
        concat_axis=0,
        tiled=True,
    )
    query = jnp.sum(q_shares.astype(jnp.float32), axis=0)
    query = head_norm(query.reshape(tokens_here, kv_heads, group, head_dim), q_gain).astype(
        jnp.bfloat16
    )

    slots = img_count * slots_here
    own_slots = jnp.take(image_slot, jnp.take(seg_images, segment_ids, axis=0), axis=0)
    slot_ids = jnp.arange(slots, dtype=jnp.int32)
    sees = jnp.any(own_slots[:, :, None] == slot_ids[None, None, :], axis=1)
    flat = kv_all.reshape(ctx_count * slots * vt_dev, kv_heads, 2, head_dim)
    mask = jnp.broadcast_to(
        sees[:, None, :, None], (tokens_here, ctx_count, slots, vt_dev)
    ).reshape(tokens_here, -1)
    context = attend(query, flat[:, :, 0], flat[:, :, 1], mask)
    context = context.astype(jnp.bfloat16).reshape(tokens_here, heads_here * head_dim)
    partial_terms = jnp.dot(context, o_full, preferred_element_type=jnp.float32)
    width = partial_terms.shape[1] // img_count
    shares = lax.all_to_all(
        partial_terms.astype(jnp.bfloat16).reshape(tokens_here, img_count, width),
        "img",
        split_axis=1,
        concat_axis=1,
        tiled=True,
    )
    update = jnp.sum(shares.astype(jnp.float32), axis=1)
    own_text = lax.dynamic_slice_in_dim(text, lax.axis_index("img") * width, width, 1)
    return (own_text.astype(jnp.float32) + jnp.tanh(attn_gate[0]) * update).astype(jnp.bfloat16)


def paired(
    text,
    input_gain,
    q_weight,
    kv_weight,
    o_weight,
    q_gain,
    k_gain,
    attn_gate,
    vision,
    segment_ids,
    seg_images,
    image_slot,
):
    bf16, f32 = jnp.bfloat16, jnp.float32
    ctx_count, chips = lax.axis_size("ctx"), lax.axis_size("img")
    place, plane = lax.axis_index("ctx"), lax.axis_index("img")
    chip, core = place // 2, place % 2
    tokens_here, width = text.shape
    head_dim = q_gain.shape[0]
    rows_dev, cols_plane = q_weight.shape
    half = cols_plane // 2
    group = half // head_dim
    chip_rows = 2 * rows_dev
    slots_here, vt_dev = vision.shape[:2]
    vis_here = slots_here * vt_dev

    def swap(x):
        return lax.ppermute(x, "ctx", [(k, k ^ 1) for k in range(ctx_count)])

    def peer(x, s):
        if s == 0:
            return x
        return lax.ppermute(x, "ctx", [(k, k ^ (2 * s)) for k in range(ctx_count)])

    def turn(x, s):
        moves = []
        for k in range(ctx_count):
            for z in range(chips):
                moves.append((k * chips + z, (2 * (z ^ s) + k % 2) * chips + k // 2))
        return lax.ppermute(x, ("ctx", "img"), moves)

    def cols(x, index, size):
        return lax.dynamic_slice_in_dim(x, index * size, size, 1)

    def join_rows(own, other):
        whole = jnp.zeros((2 * own.shape[0], own.shape[1]), own.dtype)
        whole = lax.dynamic_update_slice_in_dim(whole, own, core * own.shape[0], 0)
        return lax.dynamic_update_slice_in_dim(whole, other, (1 - core) * own.shape[0], 0)

    kv_pairs = kv_weight.reshape(rows_dev, chips, 2, -1)
    kv_keep = lax.dynamic_index_in_dim(kv_pairs, core, 2, keepdims=False).reshape(rows_dev, -1)
    kv_give = lax.dynamic_index_in_dim(kv_pairs, 1 - core, 2, keepdims=False).reshape(rows_dev, -1)
    q_rows = join_rows(cols(q_weight, core, half), swap(cols(q_weight, 1 - core, half)))
    kv_rows = join_rows(kv_keep, swap(kv_give))
    ids = jnp.concatenate((segment_ids, swap(segment_ids)))
    own_cols = 2 * plane + core
    pair_text = jnp.concatenate(
        (cols(text, own_cols, rows_dev), swap(cols(text, 2 * plane + 1 - core, rows_dev)))
    )
    o_rel = jnp.concatenate(
        (
            lax.dynamic_slice_in_dim(o_weight, core * half, half, 0),
            lax.dynamic_slice_in_dim(o_weight, (1 - core) * half, half, 0),
        )
    )

    hidden = head_norm(text.astype(f32), input_gain).astype(bf16)
    vis = vision.reshape(vis_here, width)
    sent = [
        peer(
            jnp.concatenate((cols(hidden, chip ^ s, chip_rows), cols(vis, chip ^ s, chip_rows))), s
        )
        for s in range(chips)
    ]
    pairs = [(x, swap(x)) for x in sent]

    vis_rel = jnp.stack([x[tokens_here:] for pair in pairs for x in pair])
    vis_all = jnp.take(vis_rel, jnp.arange(ctx_count) ^ place, axis=0).reshape(-1, chip_rows)
    kv_share = jnp.dot(vis_all, kv_rows, preferred_element_type=f32)
    kv_sum = 0.0
    for s in range(chips):
        kv_sum = kv_sum + peer(cols(kv_share, chip ^ s, 2 * head_dim), s)
    keys = head_norm(kv_sum[:, :head_dim], k_gain).astype(bf16)
    kv_own = jnp.concatenate((keys, kv_sum[:, head_dim:].astype(bf16)), axis=1)
    kv_all = jnp.concatenate([turn(kv_own, s) for s in range(chips)])

    query = 0.0
    for s, (own, other) in enumerate(pairs):
        rows = jnp.concatenate((own[:tokens_here], other[:tokens_here]))
        share = jnp.dot(rows, q_rows, preferred_element_type=f32)
        query = query + (share if s == 0 else peer(share.astype(bf16), s).astype(f32))
    query = head_norm(query.reshape(2 * tokens_here, group, head_dim), q_gain).astype(bf16)

    own_slots = jnp.take(image_slot, jnp.take(seg_images, ids, axis=0), axis=0)
    slot_ids = (chip ^ jnp.arange(chips))[:, None] * slots_here + jnp.arange(slots_here)[None, :]
    sees = jnp.any(own_slots[:, :, None, None] == slot_ids[None, None], axis=1)
    mask = jnp.broadcast_to(
        sees[:, :, None, :, None], (2 * tokens_here, chips, ctx_count, slots_here, vt_dev)
    ).reshape(2 * tokens_here, -1)
    context = attend(
        query[:, None], kv_all[:, None, :head_dim], kv_all[:, None, head_dim:], mask
    )
    context = context.astype(bf16).reshape(2, tokens_here, half)

    around = [peer(context, s) for s in range(chips)]
    full = jnp.stack(
        [jnp.concatenate((x, swap(x[::-1])), axis=-1).reshape(2 * tokens_here, -1) for x in around]
    )
    update = 0.0
    for s in range(chips):
        rows = lax.dynamic_index_in_dim(full, chip ^ plane ^ s, 0, keepdims=False)
        share = jnp.dot(rows, o_rel, preferred_element_type=f32).astype(bf16)
        update = update + turn(share, s).astype(f32)
    mixed = (pair_text.astype(f32) + jnp.tanh(attn_gate[0]) * update).astype(bf16)
    out = jnp.zeros((tokens_here, 2 * rows_dev), bf16)
    out = lax.dynamic_update_slice_in_dim(out, mixed[:tokens_here], core * rows_dev, 1)
    return lax.dynamic_update_slice_in_dim(
        out, swap(mixed[tokens_here:]), (1 - core) * rows_dev, 1
    )


def solution(mesh):
    fits = mesh.shape["img"] == 4 and mesh.shape["ctx"] == 8
    return jax.shard_map(
        paired if fits else general,
        mesh=mesh,
        in_specs=(
            P("ctx", None),
            P(),
            P("ctx", "img"),
            P("ctx", None),
            P("img", "ctx"),
            P(),
            P(),
            P(),
            P("img", "ctx", None),
            P("ctx"),
            P(),
            P(),
        ),
        out_specs=P("ctx", "img"),
        check_vma=False,
    )
```

```python
import functools

import jax
import jax.numpy as jnp
from jax import lax
from jax.experimental import pallas as pl
from jax.experimental.pallas import tpu as pltpu
from jax.sharding import PartitionSpec as P

KVH = 8


EPS = 1e-05
NEG = -1e30


def head_norm(values, gain):
    mean_sq = jnp.mean(values * values, axis=-1, keepdims=True)
    return values * lax.rsqrt(mean_sq + EPS) * gain


def attend(query, keys, values, mask):
    scale = query.shape[-1] ** (-0.5)
    scores = jnp.einsum("tkgd,nkd->tkgn", query, keys, preferred_element_type=jnp.float32) * scale
    live = mask[:, None, None, :]
    scores = jnp.where(live, scores, NEG)
    top = jnp.max(scores, axis=-1)
    weights = jnp.where(live, jnp.exp(scores - top[..., None]), 0.0)
    total = jnp.sum(weights, axis=-1)
    acc = jnp.einsum(
        "tkgn,nkd->tkgd", weights.astype(jnp.bfloat16), values, preferred_element_type=jnp.float32
    )
    return acc / total[..., None]


def general(
    text,
    input_gain,
    q_weight,
    kv_weight,
    o_weight,
    q_gain,
    k_gain,
    attn_gate,
    vision,
    segment_ids,
    seg_images,
    image_slot,
):
    tokens_here = text.shape[0]
    head_dim = q_gain.shape[0]
    ctx_count = lax.axis_size("ctx")
    img_count = lax.axis_size("img")
    heads_here = q_weight.shape[1] // head_dim
    kv_heads = max(1, KVH // img_count)
    group = heads_here // kv_heads
    slots_here, vt_dev = vision.shape[:2]
    rows_here = slots_here * vt_dev

    o_full = lax.all_gather(o_weight, "ctx", axis=1, tiled=True)
    vision_cols = lax.all_to_all(
        vision.reshape(rows_here, -1), "ctx", split_axis=1, concat_axis=0, tiled=True
    )
    hidden = head_norm(text.astype(jnp.float32), input_gain).astype(jnp.bfloat16)
    hidden_cols = lax.all_to_all(hidden, "ctx", split_axis=1, concat_axis=0, tiled=True)

    kv_share = jnp.dot(vision_cols, kv_weight, preferred_element_type=jnp.float32)
    kv_shares = lax.all_to_all(
        kv_share.reshape(ctx_count, rows_here, -1), "ctx", split_axis=0, concat_axis=0, tiled=True
    )
    projected = jnp.sum(kv_shares, axis=0).reshape(rows_here, KVH, 2, head_dim)
    keys = head_norm(projected[:, :, 0], k_gain).astype(jnp.bfloat16)
    values = projected[:, :, 1].astype(jnp.bfloat16)
    kv_rows = jnp.stack((keys, values), axis=2)
    owners = jnp.arange(img_count)[:, None] * KVH // img_count + jnp.arange(kv_heads)[None, :]
    kv_out = jnp.take(kv_rows, owners, axis=1).transpose(1, 0, 2, 3, 4)
    kv_in = lax.all_to_all(kv_out, "img", split_axis=0, concat_axis=0, tiled=True)
    kv_all = lax.all_gather(kv_in, "ctx", axis=0, tiled=False)

    q_share = jnp.dot(hidden_cols, q_weight, preferred_element_type=jnp.float32)
    q_shares = lax.all_to_all(
        q_share.astype(jnp.bfloat16).reshape(ctx_count, tokens_here, -1),
        "ctx",
        split_axis=0,
        concat_axis=0,
        tiled=True,
    )
    query = jnp.sum(q_shares.astype(jnp.float32), axis=0)
    query = head_norm(query.reshape(tokens_here, kv_heads, group, head_dim), q_gain).astype(
        jnp.bfloat16
    )

    slots = img_count * slots_here
    own_slots = jnp.take(image_slot, jnp.take(seg_images, segment_ids, axis=0), axis=0)
    slot_ids = jnp.arange(slots, dtype=jnp.int32)
    sees = jnp.any(own_slots[:, :, None] == slot_ids[None, None, :], axis=1)
    flat = kv_all.reshape(ctx_count * slots * vt_dev, kv_heads, 2, head_dim)
    mask = jnp.broadcast_to(
        sees[:, None, :, None], (tokens_here, ctx_count, slots, vt_dev)
    ).reshape(tokens_here, -1)
    context = attend(query, flat[:, :, 0], flat[:, :, 1], mask)
    context = context.astype(jnp.bfloat16).reshape(tokens_here, heads_here * head_dim)
    partial_terms = jnp.dot(context, o_full, preferred_element_type=jnp.float32)
    width = partial_terms.shape[1] // img_count
    shares = lax.all_to_all(
        partial_terms.astype(jnp.bfloat16).reshape(tokens_here, img_count, width),
        "img",
        split_axis=1,
        concat_axis=1,
        tiled=True,
    )
    update = jnp.sum(shares.astype(jnp.float32), axis=1)
    own_text = lax.dynamic_slice_in_dim(text, lax.axis_index("img") * width, width, 1)
    return (own_text.astype(jnp.float32) + jnp.tanh(attn_gate[0]) * update).astype(jnp.bfloat16)


BF16, F32 = jnp.bfloat16, jnp.float32
SMEM = pl.BlockSpec(memory_space=pltpu.SMEM)
VMEM = pl.BlockSpec(memory_space=pltpu.VMEM)
ANY = pl.BlockSpec(memory_space=pl.ANY)
CHIPS = 4


def call(kernel, args, specs, outs, out_specs=None, scratch=(), flops=0, size=0, name=None, grid=()):
    return pl.pallas_call(
        kernel,
        out_shape=outs,
        in_specs=specs,
        out_specs=[VMEM] * len(outs) if out_specs is None else out_specs,
        scratch_shapes=scratch,
        grid=grid,
        compiler_params=pltpu.CompilerParams(vmem_limit_bytes=24 * 2**20),
        cost_estimate=pl.CostEstimate(flops=flops, bytes_accessed=size, transcendentals=0),
        name=name,
    )(*args)


def block(index, size):
    return pl.ds(pl.multiple_of(index * size, size), size)


def spread_kernel(
    where, text, gain, vis, q_hbm, kv_hbm, *refs
):
    pieces, (q_give, kv_give, text_keep, text_give, scale, sems) = refs[:CHIPS], refs[CHIPS:]
    chip, core, plane = where[0], where[1], where[2]
    tokens, width = text.shape
    part = width // CHIPS
    half = q_give.shape[1]
    head = kv_give.shape[1] // CHIPS
    copies = [pltpu.make_async_copy(q_hbm.at[:, block(1 - core, half)], q_give, sems.at[0])]
    for j in range(CHIPS):
        copies.append(
            pltpu.make_async_copy(
                kv_hbm.at[:, block(2 * j + 1 - core, head)],
                kv_give.at[:, pl.ds(j * head, head)],
                sems.at[1 + j],
            )
        )
    for copy in copies:
        copy.start()
    step = 16
    for r in range(0, tokens, step):
        x = text[r : r + step, :].astype(F32)
        mean_sq = jnp.mean(x * x, axis=-1, keepdims=True)
        scale[r : r + step, :] = jnp.broadcast_to(lax.rsqrt(mean_sq + EPS), (step, 128))
    for s in range(CHIPS):
        cols = block(chip ^ s, part)
        row_gain = gain[:, cols]
        for r in range(0, tokens, step):
            x = text[r : r + step, cols].astype(F32)
            pieces[s][r : r + step, :] = (x * scale[r : r + step, 0:1] * row_gain).astype(BF16)
        pieces[s][tokens:, :] = vis[:, cols]
    text_keep[...] = text[:, block(2 * plane + core, half)]
    text_give[...] = text[:, block(2 * plane + 1 - core, half)]
    for copy in copies:
        copy.wait()


def query_kernel(where, own, other, q_own, q_other, out):
    core = where[1]
    tokens = out.shape[0] // 2
    rows, half = q_other.shape
    near, far = block(core, rows), block(1 - core, rows)
    x_near = jnp.concatenate((own[:tokens, near], other[:tokens, near]), axis=0)
    x_far = jnp.concatenate((own[:tokens, far], other[:tokens, far]), axis=0)
    share = jnp.dot(x_near, q_own[:, block(core, half)], preferred_element_type=F32)
    share += jnp.dot(x_far, q_other[...], preferred_element_type=F32)
    out[...] = share.astype(out.dtype)


def kv_kernel(where, *refs):
    vis, (kv_own, kv_other), shares = refs[: 2 * CHIPS], refs[2 * CHIPS : -CHIPS], refs[-CHIPS:]
    core = where[1]
    rows = kv_own.shape[0]
    head = kv_other.shape[1] // CHIPS
    near, far = block(core, rows), block(1 - core, rows)
    x_near = jnp.concatenate([x[:, near] for x in vis], axis=0)
    x_far = jnp.concatenate([x[:, far] for x in vis], axis=0)
    count = shares[0].shape[0]
    for j in range(CHIPS):
        out = jnp.dot(x_near, kv_own[:, block(2 * j + core, head)], preferred_element_type=F32)
        out += jnp.dot(x_far, kv_other[:, j * head : (j + 1) * head], preferred_element_type=F32)
        for s in range(CHIPS):
            shares[s][:, j * head : (j + 1) * head] = out[s * count : (s + 1) * count]


def kv_norm_kernel(where, k_gain, *refs):
    shares, outs = refs[:CHIPS], refs[CHIPS:]
    plane = where[2]
    head = outs[0].shape[1]
    dim = head // 2
    for t in range(CHIPS):
        cols = block(plane ^ t, head)
        total = (shares[0][:, cols] + shares[1][:, cols]) + (shares[2][:, cols] + shares[3][:, cols])
        keys = head_norm(total[:, :dim], k_gain[...])
        outs[t][:, :dim] = keys.astype(BF16)
        outs[t][:, dim:] = total[:, dim:].astype(BF16)


def attend_kernel(q_gain, *refs):
    shares, kv, (bias, context) = refs[:CHIPS], refs[CHIPS : 2 * CHIPS], refs[2 * CHIPS :]
    dim = q_gain.shape[1]
    keys = jnp.concatenate([x[:, :dim] for x in kv], axis=0)
    values = jnp.concatenate([x[:, dim:] for x in kv], axis=0)
    rows = context.shape[0]
    step = 128
    for r in range(0, rows, step):
        for g in range(context.shape[1] // dim):
            cols = slice(g * dim, (g + 1) * dim)
            x = [share[r : r + step, cols].astype(F32) for share in shares]
            query = head_norm((x[0] + x[1]) + (x[2] + x[3]), q_gain[...]).astype(BF16)
            scores = lax.dot_general(
                query, keys, (((1,), (1,)), ((), ())), preferred_element_type=F32
            )
            scores = scores * dim ** (-0.5) + bias[r : r + step, :]
            weights = jnp.exp(scores - jnp.max(scores, axis=-1, keepdims=True))
            total = jnp.sum(weights, axis=-1, keepdims=True)
            acc = jnp.dot(weights.astype(BF16), values, preferred_element_type=F32)
            context[r : r + step, cols] = (acc / total).astype(BF16)


def out_kernel(t, where, near, far, o_own, o_side, o_up, o_top, o_low, out, weight, sems):
    chip, core, plane = where[0], where[1], where[2]
    source = chip ^ plane ^ t
    half = near.shape[1]
    tokens = near.shape[0] // 2
    whole = (o_own, o_side, o_up)
    for s in range(CHIPS - 1):

        @pl.when(source == s)
        def _():
            copy = pltpu.make_async_copy(whole[s], weight, sems.at[0])
            copy.start()
            copy.wait()

    @pl.when(source == CHIPS - 1)
    def _():
        top = pltpu.make_async_copy(o_top, weight.at[pl.ds(0, half), :], sems.at[0])
        low = pltpu.make_async_copy(o_low, weight.at[pl.ds(half, half), :], sems.at[1])
        top.start()
        low.start()
        top.wait()
        low.wait()

    turned = jnp.concatenate((far[tokens:, :], far[:tokens, :]), axis=0)
    share = jnp.dot(near[...], weight[block(core, half), :], preferred_element_type=F32)
    share += jnp.dot(turned, weight[block(1 - core, half), :], preferred_element_type=F32)
    out[...] = share.astype(BF16)


def mix_kernel(gate, keep_text, give_text, *refs):
    shares, (keep, give) = refs[:CHIPS], refs[CHIPS:]
    tokens = keep.shape[0]
    for half, (text, out) in enumerate(((keep_text, keep), (give_text, give))):
        rows = slice(half * tokens, (half + 1) * tokens)
        x = [share[rows, :].astype(F32) for share in shares]
        update = (x[0] + x[1]) + (x[2] + x[3])
        out[...] = (text[...].astype(F32) + gate[0] * update).astype(BF16)


def paired(
    text,
    input_gain,
    q_weight,
    kv_weight,
    o_weight,
    q_gain,
    k_gain,
    attn_gate,
    vision,
    segment_ids,
    seg_images,
    image_slot,
):
    ctx_count = lax.axis_size("ctx")
    place, plane = lax.axis_index("ctx"), lax.axis_index("img")
    chip, core = place // 2, place % 2
    where = jnp.stack((chip, core, plane)).astype(jnp.int32)
    tokens, width = text.shape
    head_dim = q_gain.shape[0]
    rows_dev, cols_plane = q_weight.shape
    half = cols_plane // 2
    part = 2 * rows_dev
    slots_here, vt_dev = vision.shape[:2]
    vis_here = slots_here * vt_dev
    kv_cols = kv_weight.shape[1] // 2

    def shape(rows, cols, kind=BF16):
        return jax.ShapeDtypeStruct((rows, cols), kind)

    def swap(x):
        return lax.ppermute(x, "ctx", [(k, k ^ 1) for k in range(ctx_count)])

    def peer(x, s):
        return lax.ppermute(x, "ctx", [(k, k ^ (2 * s)) for k in range(ctx_count)])

    def across(x, t):
        return lax.ppermute(x, "img", [(k, k ^ t) for k in range(CHIPS)])

    steps = range(1, CHIPS)

    *pieces, q_give, kv_give, text_keep, text_give = call(
        spread_kernel,
        (where, text, input_gain[None], vision.reshape(vis_here, width), q_weight, kv_weight),
        [SMEM, VMEM, VMEM, VMEM, ANY, ANY],
        [shape(tokens + vis_here, part)] * CHIPS
        + [shape(rows_dev, half), shape(rows_dev, kv_cols)]
        + [shape(tokens, half)] * 2,
        out_specs=[VMEM] * CHIPS + [ANY, ANY, VMEM, VMEM],
        scratch=[pltpu.VMEM((tokens, 128), F32), pltpu.SemaphoreType.DMA((1 + CHIPS,))],
        flops=8 * tokens * width,
        size=8 * 2**20,
        name="spread",
    )
    own = [pieces[0]] + [peer(pieces[s], s) for s in steps]
    q_other, kv_other = swap(q_give), swap(kv_give)
    pairs = [(x, swap(x)) for x in own]

    o_weight, _ = lax.optimization_barrier((o_weight, own[3]))
    o_side, o_up = peer(o_weight, 1), peer(o_weight, 2)
    o_top, o_low = peer(o_up[:half], 1), peer(o_side[half:], 2)

    vis_spec = pl.BlockSpec((vis_here, part), lambda _: (tokens // vis_here, 0))
    shares = call(
        kv_kernel,
        (where, *[x for pair in pairs for x in pair], kv_weight, kv_other),
        [SMEM] + [vis_spec] * (2 * CHIPS) + [VMEM, VMEM],
        [shape(2 * vis_here, kv_cols, F32)] * CHIPS,
        flops=4 * vis_here * ctx_count * part * kv_cols,
        size=4 * 2**20,
        name="kv_shares",
        grid=(1,),
    )
    shares = [shares[0]] + [peer(shares[s], s) for s in steps]
    heads = call(
        kv_norm_kernel,
        (where, k_gain[None], *shares),
        [SMEM] + [VMEM] * (1 + CHIPS),
        [shape(2 * vis_here, 2 * head_dim)] * CHIPS,
        flops=2**20,
        size=2**19,
        name="kv_norm",
    )
    kv_own = jnp.concatenate([heads[0]] + [across(heads[t], t) for t in steps])
    kv_all = [kv_own] + [peer(kv_own, s) for s in steps]

    q_shares = [
        call(
            query_kernel,
            (where, *pairs[s], q_weight, q_other),
            [SMEM] + [VMEM] * 4,
            [shape(2 * tokens, half, F32 if s == 0 else BF16)],
            flops=4 * tokens * part * half,
            size=2 * 2**20,
            name="q_share",
        )[0]
        for s in range(CHIPS)
    ]
    q_shares = [q_shares[0]] + [peer(q_shares[s], s) for s in steps]

    ids = jnp.concatenate((segment_ids, swap(segment_ids)))
    images = jnp.arange(image_slot.shape[0])
    slot_of = jnp.sum(
        jnp.where(seg_images[:, :, None] == images, image_slot[None, None, :], 0), axis=2
    )
    numbers = jnp.arange(seg_images.shape[0])
    own_slots = jnp.sum(
        jnp.where((ids[:, None] == numbers)[:, :, None], slot_of[None], 0), axis=1
    )
    key_rows = jnp.arange(CHIPS * CHIPS * 2 * vis_here)
    key_plane = plane ^ (key_rows // (2 * vis_here) % CHIPS)
    key_slot = key_plane * slots_here + key_rows // vt_dev % slots_here
    sees = jnp.any(own_slots[:, :, None] == key_slot, axis=1)
    bias = jnp.where(sees, 0.0, NEG).astype(F32)

    context = call(
        attend_kernel,
        (q_gain[None], *q_shares, *kv_all, bias),
        [VMEM] * (2 + 2 * CHIPS),
        [shape(2 * tokens, half)],
        flops=8 * tokens * half * bias.shape[1],
        size=2 * 2**20,
        name="attend",
    )[0]
    far = swap(context)
    parts = [
        call(
            functools.partial(out_kernel, t),
            (where, context, far, o_weight, o_side, o_up, o_top, o_low),
            [SMEM, VMEM, VMEM] + [ANY] * 5,
            [shape(2 * tokens, half)],
            scratch=[pltpu.VMEM((cols_plane, half), BF16), pltpu.SemaphoreType.DMA((2,))],
            flops=4 * tokens * cols_plane * half,
            size=2 * 2**20,
            name="o_share",
        )[0]
        for t in (1, 2, 3, 0)
    ]
    landed = [parts[3]] + [across(parts[t - 1], t) for t in steps]
    other_text = swap(text_give)
    keep, give = call(
        mix_kernel,
        (jnp.tanh(attn_gate), text_keep, other_text, *landed),
        [SMEM] + [VMEM] * (2 + CHIPS),
        [shape(tokens, half)] * 2,
        flops=2**20,
        size=2**20,
        name="mix",
    )
    back = swap(give)
    return jnp.where(
        core == 0, jnp.concatenate((keep, back), axis=1), jnp.concatenate((back, keep), axis=1)
    )


def solution(mesh):
    fits = mesh.shape["img"] == 4 and mesh.shape["ctx"] == 8
    return jax.shard_map(
        paired if fits else general,
        mesh=mesh,
        in_specs=(
            P("ctx", None),
            P(),
            P("ctx", "img"),
            P("ctx", None),
            P("img", "ctx"),
            P(),
            P(),
            P(),
            P("img", "ctx", None),
            P("ctx"),
            P(),
            P(),
        ),
        out_specs=P("ctx", "img"),
        check_vma=False,
    )
```

```python
import jax
import jax.numpy as jnp
from jax import lax
from jax.experimental import pallas as pl
from jax.experimental.pallas import tpu as pltpu
from jax.sharding import PartitionSpec as P

KVH = 8


EPS = 1e-05
NEG = -1e30


def head_norm(values, gain):
    mean_sq = jnp.mean(values * values, axis=-1, keepdims=True)
    return values * lax.rsqrt(mean_sq + EPS) * gain


def attend(query, keys, values, mask):
    scale = query.shape[-1] ** (-0.5)
    scores = jnp.einsum("tkgd,nkd->tkgn", query, keys, preferred_element_type=jnp.float32) * scale
    live = mask[:, None, None, :]
    scores = jnp.where(live, scores, NEG)
    top = jnp.max(scores, axis=-1)
    weights = jnp.where(live, jnp.exp(scores - top[..., None]), 0.0)
    total = jnp.sum(weights, axis=-1)
    acc = jnp.einsum(
        "tkgn,nkd->tkgd", weights.astype(jnp.bfloat16), values, preferred_element_type=jnp.float32
    )
    return acc / total[..., None]


def general(
    text,
    input_gain,
    q_weight,
    kv_weight,
    o_weight,
    q_gain,
    k_gain,
    attn_gate,
    vision,
    segment_ids,
    seg_images,
    image_slot,
):
    tokens_here = text.shape[0]
    head_dim = q_gain.shape[0]
    ctx_count = lax.axis_size("ctx")
    img_count = lax.axis_size("img")
    heads_here = q_weight.shape[1] // head_dim
    kv_heads = max(1, KVH // img_count)
    group = heads_here // kv_heads
    slots_here, vt_dev = vision.shape[:2]
    rows_here = slots_here * vt_dev

    o_full = lax.all_gather(o_weight, "ctx", axis=1, tiled=True)
    vision_cols = lax.all_to_all(
        vision.reshape(rows_here, -1), "ctx", split_axis=1, concat_axis=0, tiled=True
    )
    hidden = head_norm(text.astype(jnp.float32), input_gain).astype(jnp.bfloat16)
    hidden_cols = lax.all_to_all(hidden, "ctx", split_axis=1, concat_axis=0, tiled=True)

    kv_share = jnp.dot(vision_cols, kv_weight, preferred_element_type=jnp.float32)
    kv_shares = lax.all_to_all(
        kv_share.reshape(ctx_count, rows_here, -1), "ctx", split_axis=0, concat_axis=0, tiled=True
    )
    projected = jnp.sum(kv_shares, axis=0).reshape(rows_here, KVH, 2, head_dim)
    keys = head_norm(projected[:, :, 0], k_gain).astype(jnp.bfloat16)
    values = projected[:, :, 1].astype(jnp.bfloat16)
    kv_rows = jnp.stack((keys, values), axis=2)
    owners = jnp.arange(img_count)[:, None] * KVH // img_count + jnp.arange(kv_heads)[None, :]
    kv_out = jnp.take(kv_rows, owners, axis=1).transpose(1, 0, 2, 3, 4)
    kv_in = lax.all_to_all(kv_out, "img", split_axis=0, concat_axis=0, tiled=True)
    kv_all = lax.all_gather(kv_in, "ctx", axis=0, tiled=False)

    q_share = jnp.dot(hidden_cols, q_weight, preferred_element_type=jnp.float32)
    q_shares = lax.all_to_all(
        q_share.astype(jnp.bfloat16).reshape(ctx_count, tokens_here, -1),
        "ctx",
        split_axis=0,
        concat_axis=0,
        tiled=True,
    )
    query = jnp.sum(q_shares.astype(jnp.float32), axis=0)
    query = head_norm(query.reshape(tokens_here, kv_heads, group, head_dim), q_gain).astype(
        jnp.bfloat16
    )

    slots = img_count * slots_here
    own_slots = jnp.take(image_slot, jnp.take(seg_images, segment_ids, axis=0), axis=0)
    slot_ids = jnp.arange(slots, dtype=jnp.int32)
    sees = jnp.any(own_slots[:, :, None] == slot_ids[None, None, :], axis=1)
    flat = kv_all.reshape(ctx_count * slots * vt_dev, kv_heads, 2, head_dim)
    mask = jnp.broadcast_to(
        sees[:, None, :, None], (tokens_here, ctx_count, slots, vt_dev)
    ).reshape(tokens_here, -1)
    context = attend(query, flat[:, :, 0], flat[:, :, 1], mask)
    context = context.astype(jnp.bfloat16).reshape(tokens_here, heads_here * head_dim)
    partial_terms = jnp.dot(context, o_full, preferred_element_type=jnp.float32)
    width = partial_terms.shape[1] // img_count
    shares = lax.all_to_all(
        partial_terms.astype(jnp.bfloat16).reshape(tokens_here, img_count, width),
        "img",
        split_axis=1,
        concat_axis=1,
        tiled=True,
    )
    update = jnp.sum(shares.astype(jnp.float32), axis=1)
    own_text = lax.dynamic_slice_in_dim(text, lax.axis_index("img") * width, width, 1)
    return (own_text.astype(jnp.float32) + jnp.tanh(attn_gate[0]) * update).astype(jnp.bfloat16)


BF16, F32 = jnp.bfloat16, jnp.float32
SMEM = pl.BlockSpec(memory_space=pltpu.SMEM)
VMEM = pl.BlockSpec(memory_space=pltpu.VMEM)
CHIPS = 4


def call(kernel, args, specs, outs, out_specs=None, scratch=(), flops=0, size=0, name=None, grid=()):
    return pl.pallas_call(
        kernel,
        out_shape=outs,
        in_specs=specs,
        out_specs=[VMEM] * len(outs) if out_specs is None else out_specs,
        scratch_shapes=scratch,
        grid=grid,
        compiler_params=pltpu.CompilerParams(vmem_limit_bytes=24 * 2**20),
        cost_estimate=pl.CostEstimate(flops=flops, bytes_accessed=size, transcendentals=0),
        name=name,
    )(*args)


def block(index, size):
    return pl.ds(pl.multiple_of(index * size, size), size)


def spread_kernel(where, text, gain, vis, *refs):
    pieces, vis_pieces = refs[:CHIPS], refs[CHIPS : 2 * CHIPS]
    text_keep, text_give, scale = refs[2 * CHIPS :]
    chip, core, plane = where[0], where[1], where[2]
    tokens, width = text.shape
    part = width // CHIPS
    half = text_keep.shape[1]
    step = 16
    for r in range(0, tokens, step):
        x = text[r : r + step, :].astype(F32)
        mean_sq = jnp.mean(x * x, axis=-1, keepdims=True)
        scale[r : r + step, :] = jnp.broadcast_to(lax.rsqrt(mean_sq + EPS), (step, 128))
    for s in range(CHIPS):
        cols = block(chip ^ s, part)
        vis_pieces[s][...] = vis[:, cols]
        row_gain = gain[:, cols]
        for r in range(0, tokens, step):
            x = text[r : r + step, cols].astype(F32)
            pieces[s][r : r + step, :] = (x * scale[r : r + step, 0:1] * row_gain).astype(BF16)
    text_keep[...] = text[:, block(2 * plane + core, half)]
    text_give[...] = text[:, block(2 * plane + 1 - core, half)]


def cut_kernel(where, q_own, kv_own, q_give, kv_give, sems):
    core = where[1]
    half = q_give.shape[1]
    head = kv_give.shape[1] // CHIPS
    copies = [pltpu.make_async_copy(q_own.at[:, block(1 - core, half)], q_give, sems.at[0])]
    for j in range(CHIPS):
        copies.append(
            pltpu.make_async_copy(
                kv_own.at[:, block(2 * j + 1 - core, head)],
                kv_give.at[:, pl.ds(j * head, head)],
                sems.at[1 + j],
            )
        )
    for copy in copies:
        copy.start()
    for copy in copies:
        copy.wait()


def query_kernel(where, own, other, q_own, q_other, kv_ref, out):
    core = where[1]
    tokens = own.shape[0]
    rows, half = q_other.shape
    near, far = block(core, rows), block(1 - core, rows)
    x_near = jnp.concatenate((own[:, near], other[:, near]), axis=0)
    x_far = jnp.concatenate((own[:, far], other[:, far]), axis=0)
    share = jnp.dot(x_near, q_own[:, block(core, half)], preferred_element_type=F32)
    share += jnp.dot(x_far, q_other[...], preferred_element_type=F32)
    out[: 2 * tokens, :] = share.astype(out.dtype)
    if kv_ref is not None:
        count, head = kv_ref.shape
        fold = half // head
        for k in range(fold):
            lines = count // fold
            out[2 * tokens :, k * head : (k + 1) * head] = kv_ref[k * lines : (k + 1) * lines, :]


def first_query_kernel(where, own, other, q_own, q_other, out):
    query_kernel(where, own, other, q_own, q_other, None, out)


def kv_kernel(where, vis, vis_other, kv_own, kv_other, *shares):
    core = where[1]
    rows = kv_own.shape[0]
    head = kv_other.shape[1] // CHIPS
    near, far = block(core, rows), block(1 - core, rows)
    x_near = jnp.concatenate((vis[:, near], vis_other[:, near]), axis=0)
    x_far = jnp.concatenate((vis[:, far], vis_other[:, far]), axis=0)
    total = vis.shape[0]
    count = total // CHIPS
    for j in range(CHIPS):
        cols = slice(j * head, (j + 1) * head)
        out = jnp.dot(x_near, kv_own[:, block(2 * j + core, head)], preferred_element_type=F32)
        out += jnp.dot(x_far, kv_other[:, cols], preferred_element_type=F32)
        for s in range(CHIPS):
            shares[s][:count, cols] = out[s * count : (s + 1) * count]
            shares[s][count:, cols] = out[total + s * count : total + (s + 1) * count]


def kv_norm_kernel(where, k_gain, *refs):
    shares, outs = refs[:CHIPS], refs[CHIPS:]
    plane = where[2]
    head = outs[0].shape[1]
    dim = head // 2
    for t in range(CHIPS):
        cols = block(plane ^ t, head)
        total = (shares[0][:, cols] + shares[1][:, cols]) + (shares[2][:, cols] + shares[3][:, cols])
        keys = head_norm(total[:, :dim], k_gain[...])
        outs[t][:, :dim] = keys.astype(BF16)
        outs[t][:, dim:] = total[:, dim:].astype(BF16)


def attend_kernel(q_gain, first, kv_first, *refs):
    landed, (bias, context) = refs[: CHIPS - 1], refs[CHIPS - 1 :]
    dim = q_gain.shape[1]
    rows, half = context.shape
    head = 2 * dim
    kv = [kv_first[...]]
    for x in landed:
        kv += [x[rows:, k * head : (k + 1) * head] for k in range(half // head)]
    keys = jnp.concatenate([x[:, :dim] for x in kv], axis=0)
    values = jnp.concatenate([x[:, dim:] for x in kv], axis=0)
    shares = (first,) + landed
    step = 128
    for r in range(0, rows, step):
        for g in range(half // dim):
            cols = slice(g * dim, (g + 1) * dim)
            x = [share[r : r + step, cols].astype(F32) for share in shares]
            query = head_norm((x[0] + x[1]) + (x[2] + x[3]), q_gain[...]).astype(BF16)
            scores = lax.dot_general(
                query, keys, (((1,), (1,)), ((), ())), preferred_element_type=F32
            )
            scores = scores * dim ** (-0.5) + bias[r : r + step, :]
            weights = jnp.exp(scores - jnp.max(scores, axis=-1, keepdims=True))
            total = jnp.sum(weights, axis=-1, keepdims=True)
            acc = jnp.dot(weights.astype(BF16), values, preferred_element_type=F32)
            context[r : r + step, cols] = (acc / total).astype(BF16)


def share_of(core, near, far, weight):
    half = near.shape[1]
    tokens = near.shape[0] // 2
    turned = jnp.concatenate((far[tokens:, :], far[:tokens, :]), axis=0)
    share = jnp.dot(near[...], weight[block(core, half), :], preferred_element_type=F32)
    share += jnp.dot(turned, weight[block(1 - core, half), :], preferred_element_type=F32)
    return share.astype(BF16)


def out_kernel(where, near, far, weight, own, other):
    tokens = own.shape[0]
    share = share_of(where[1], near, far, weight)
    own[...] = share[:tokens]
    other[...] = share[tokens:]


def pick_kernel(where, *refs):
    shares, outs = refs[:CHIPS], refs[CHIPS:]
    first = where[0] ^ where[2]
    for t in range(CHIPS):
        for s in range(CHIPS):

            @pl.when((first ^ t) == s)
            def _():
                outs[t][...] = shares[s][...]


def mixed_rows(gate, text, shares):
    x = [share[...].astype(F32) for share in shares]
    update = (x[0] + x[1]) + (x[2] + x[3])
    return (text[...].astype(F32) + gate[0] * update).astype(BF16)


def give_kernel(gate, text, *refs):
    refs[CHIPS][...] = mixed_rows(gate, text, refs[:CHIPS])


def last_kernel(where, gate, text, back, *refs):
    shares, out = refs[:CHIPS], refs[CHIPS]
    core = where[1]
    half = text.shape[1]
    out[:, block(core, half)] = mixed_rows(gate, text, shares)
    out[:, block(1 - core, half)] = back[...]


def paired(
    text,
    input_gain,
    q_weight,
    kv_weight,
    o_weight,
    q_gain,
    k_gain,
    attn_gate,
    vision,
    segment_ids,
    seg_images,
    image_slot,
):
    ctx_count = lax.axis_size("ctx")
    place, plane = lax.axis_index("ctx"), lax.axis_index("img")
    chip, core = place // 2, place % 2
    where = jnp.stack((chip, core, plane)).astype(jnp.int32)
    tokens, width = text.shape
    head_dim = q_gain.shape[0]
    rows_dev, cols_plane = q_weight.shape
    half = cols_plane // 2
    part = 2 * rows_dev
    slots_here, vt_dev = vision.shape[:2]
    vis_here = slots_here * vt_dev
    kv_cols = kv_weight.shape[1] // 2

    def shape(rows, cols, kind=BF16):
        return jax.ShapeDtypeStruct((rows, cols), kind)

    def swap(x):
        return lax.ppermute(x, "ctx", [(k, k ^ 1) for k in range(ctx_count)])

    def peer(x, s):
        return lax.ppermute(x, "ctx", [(k, k ^ (2 * s)) for k in range(ctx_count)])

    def across(x, t):
        return lax.ppermute(x, "img", [(k, k ^ t) for k in range(CHIPS)])

    steps = range(1, CHIPS)

    *pieces, text_keep, text_give = call(
        spread_kernel,
        (where, text, input_gain[None], vision.reshape(vis_here, width)),
        [SMEM] + [VMEM] * 3,
        [shape(tokens, part)] * CHIPS + [shape(vis_here, part)] * CHIPS + [shape(tokens, half)] * 2,
        scratch=[pltpu.VMEM((tokens, 128), F32)],
        flops=8 * tokens * width,
        size=4 * 2**20,
        name="spread",
    )
    pieces, vis_pieces = pieces[:CHIPS], pieces[CHIPS:]
    own = [pieces[0]] + [peer(pieces[s], s) for s in steps]

    q_give, kv_give = call(
        cut_kernel,
        (where, q_weight, kv_weight),
        [SMEM, VMEM, VMEM],
        [shape(rows_dev, half), shape(rows_dev, kv_cols)],
        scratch=[pltpu.SemaphoreType.DMA((1 + CHIPS,))],
        size=4 * 2**20,
        name="cut",
    )
    vis_own = jnp.concatenate([vis_pieces[0]] + [peer(vis_pieces[s], s) for s in steps])
    kv_other, vis_other = swap(kv_give), swap(vis_own)
    q_other = swap(q_give)

    shares = call(
        kv_kernel,
        (where, vis_own, vis_other, kv_weight, kv_other),
        [SMEM] + [VMEM] * 4,
        [shape(2 * vis_here, kv_cols, F32)] * CHIPS,
        flops=4 * vis_here * ctx_count * part * kv_cols,
        size=4 * 2**20,
        name="kv_shares",
    )
    shares = [shares[0]] + [peer(shares[s], s) for s in steps]
    heads = call(
        kv_norm_kernel,
        (where, k_gain[None], *shares),
        [SMEM] + [VMEM] * (1 + CHIPS),
        [shape(2 * vis_here, 2 * head_dim)] * CHIPS,
        flops=2**20,
        size=2**19,
        name="kv_norm",
    )
    kv_own = jnp.concatenate([heads[0]] + [across(heads[t], t) for t in steps])

    pairs = [(x, swap(x)) for x in own]
    kv_lines = kv_own.shape[0] * kv_own.shape[1] // half
    landed = [
        peer(
            call(
                query_kernel,
                (where, *pairs[s], q_weight, q_other, kv_own),
                [SMEM] + [VMEM] * 5,
                [shape(2 * tokens + kv_lines, half)],
                flops=4 * tokens * part * half,
                size=2 * 2**20,
                name="q_share",
            )[0],
            s,
        )
        for s in steps
    ]
    q_first = call(
        first_query_kernel,
        (where, *pairs[0], q_weight, q_other),
        [SMEM] + [VMEM] * 4,
        [shape(2 * tokens, half, F32)],
        flops=40 * tokens * part * half,
        size=2 * 2**20,
        name="q_first",
    )[0]
    ids = jnp.concatenate((segment_ids, swap(segment_ids)))
    images = jnp.arange(image_slot.shape[0])
    slot_of = jnp.sum(
        jnp.where(seg_images[:, :, None] == images, image_slot[None, None, :], 0), axis=2
    )
    numbers = jnp.arange(seg_images.shape[0])
    own_slots = jnp.sum(
        jnp.where((ids[:, None] == numbers)[:, :, None], slot_of[None], 0), axis=1
    )
    key_rows = jnp.arange(CHIPS * CHIPS * 2 * vis_here)
    key_plane = plane ^ (key_rows // (2 * vis_here) % CHIPS)
    key_slot = key_plane * slots_here + key_rows // vt_dev % slots_here
    sees = jnp.any(own_slots[:, :, None] == key_slot, axis=1)
    bias = jnp.where(sees, 0.0, NEG).astype(F32)

    context = call(
        attend_kernel,
        (q_gain[None], q_first, kv_own, *landed, bias),
        [VMEM] * (3 + CHIPS),
        [shape(2 * tokens, half)],
        flops=8 * tokens * half * bias.shape[1],
        size=2 * 2**20,
        name="attend",
    )[0]

    around = [context] + [peer(context, s) for s in steps]
    shares = [
        call(
            out_kernel,
            (where, x, swap(x), o_weight),
            [SMEM] + [VMEM] * 3,
            [shape(tokens, half)] * 2,
            flops=4 * tokens * cols_plane * half,
            size=2 * 2**20,
            name="o_share",
        )
        for x in around
    ]
    summands = []
    for rows in (1, 0):
        landed = [shares[0][rows]] + [peer(shares[s][rows], s) for s in steps]
        picked = call(
            pick_kernel,
            (where, *landed),
            [SMEM] + [VMEM] * CHIPS,
            [shape(tokens, half)] * CHIPS,
            flops=2**20,
            size=2**20,
            name="pick",
        )
        summands.append([picked[0]] + [across(picked[t], t) for t in steps])
    gate = jnp.tanh(attn_gate)
    give = call(
        give_kernel,
        (gate, swap(text_give), *summands[0]),
        [SMEM] + [VMEM] * (1 + CHIPS),
        [shape(tokens, half)],
        flops=2**20,
        size=2**20,
        name="mix_give",
    )[0]
    return call(
        last_kernel,
        (where, gate, text_keep, swap(give), *summands[1]),
        [SMEM, SMEM] + [VMEM] * (2 + CHIPS),
        [shape(tokens, 2 * half)],
        flops=2**20,
        size=2**20,
        name="mix_keep",
    )[0]


def solution(mesh):
    fits = mesh.shape["img"] == 4 and mesh.shape["ctx"] == 8
    return jax.shard_map(
        paired if fits else general,
        mesh=mesh,
        in_specs=(
            P("ctx", None),
            P(),
            P("ctx", "img"),
            P("ctx", None),
            P("img", "ctx"),
            P(),
            P(),
            P(),
            P("img", "ctx", None),
            P("ctx"),
            P(),
            P(),
        ),
        out_specs=P("ctx", "img"),
        check_vma=False,
    )
```

```python
import jax
import jax.numpy as jnp
from jax import lax
from jax.experimental import pallas as pl
from jax.experimental.pallas import tpu as pltpu
from jax.sharding import PartitionSpec as P

KVH = 8


EPS = 1e-05
NEG = -1e30


def head_norm(values, gain):
    mean_sq = jnp.mean(values * values, axis=-1, keepdims=True)
    return values * lax.rsqrt(mean_sq + EPS) * gain


def attend(query, keys, values, mask):
    scale = query.shape[-1] ** (-0.5)
    scores = jnp.einsum("tkgd,nkd->tkgn", query, keys, preferred_element_type=jnp.float32) * scale
    live = mask[:, None, None, :]
    scores = jnp.where(live, scores, NEG)
    top = jnp.max(scores, axis=-1)
    weights = jnp.where(live, jnp.exp(scores - top[..., None]), 0.0)
    total = jnp.sum(weights, axis=-1)
    acc = jnp.einsum(
        "tkgn,nkd->tkgd", weights.astype(jnp.bfloat16), values, preferred_element_type=jnp.float32
    )
    return acc / total[..., None]


def general(
    text,
    input_gain,
    q_weight,
    kv_weight,
    o_weight,
    q_gain,
    k_gain,
    attn_gate,
    vision,
    segment_ids,
    seg_images,
    image_slot,
):
    tokens_here = text.shape[0]
    head_dim = q_gain.shape[0]
    ctx_count = lax.axis_size("ctx")
    img_count = lax.axis_size("img")
    heads_here = q_weight.shape[1] // head_dim
    kv_heads = max(1, KVH // img_count)
    group = heads_here // kv_heads
    slots_here, vt_dev = vision.shape[:2]
    rows_here = slots_here * vt_dev

    o_full = lax.all_gather(o_weight, "ctx", axis=1, tiled=True)
    vision_cols = lax.all_to_all(
        vision.reshape(rows_here, -1), "ctx", split_axis=1, concat_axis=0, tiled=True
    )
    hidden = head_norm(text.astype(jnp.float32), input_gain).astype(jnp.bfloat16)
    hidden_cols = lax.all_to_all(hidden, "ctx", split_axis=1, concat_axis=0, tiled=True)

    kv_share = jnp.dot(vision_cols, kv_weight, preferred_element_type=jnp.float32)
    kv_shares = lax.all_to_all(
        kv_share.reshape(ctx_count, rows_here, -1), "ctx", split_axis=0, concat_axis=0, tiled=True
    )
    projected = jnp.sum(kv_shares, axis=0).reshape(rows_here, KVH, 2, head_dim)
    keys = head_norm(projected[:, :, 0], k_gain).astype(jnp.bfloat16)
    values = projected[:, :, 1].astype(jnp.bfloat16)
    kv_rows = jnp.stack((keys, values), axis=2)
    owners = jnp.arange(img_count)[:, None] * KVH // img_count + jnp.arange(kv_heads)[None, :]
    kv_out = jnp.take(kv_rows, owners, axis=1).transpose(1, 0, 2, 3, 4)
    kv_in = lax.all_to_all(kv_out, "img", split_axis=0, concat_axis=0, tiled=True)
    kv_all = lax.all_gather(kv_in, "ctx", axis=0, tiled=False)

    q_share = jnp.dot(hidden_cols, q_weight, preferred_element_type=jnp.float32)
    q_shares = lax.all_to_all(
        q_share.astype(jnp.bfloat16).reshape(ctx_count, tokens_here, -1),
        "ctx",
        split_axis=0,
        concat_axis=0,
        tiled=True,
    )
    query = jnp.sum(q_shares.astype(jnp.float32), axis=0)
    query = head_norm(query.reshape(tokens_here, kv_heads, group, head_dim), q_gain).astype(
        jnp.bfloat16
    )

    slots = img_count * slots_here
    own_slots = jnp.take(image_slot, jnp.take(seg_images, segment_ids, axis=0), axis=0)
    slot_ids = jnp.arange(slots, dtype=jnp.int32)
    sees = jnp.any(own_slots[:, :, None] == slot_ids[None, None, :], axis=1)
    flat = kv_all.reshape(ctx_count * slots * vt_dev, kv_heads, 2, head_dim)
    mask = jnp.broadcast_to(
        sees[:, None, :, None], (tokens_here, ctx_count, slots, vt_dev)
    ).reshape(tokens_here, -1)
    context = attend(query, flat[:, :, 0], flat[:, :, 1], mask)
    context = context.astype(jnp.bfloat16).reshape(tokens_here, heads_here * head_dim)
    partial_terms = jnp.dot(context, o_full, preferred_element_type=jnp.float32)
    width = partial_terms.shape[1] // img_count
    shares = lax.all_to_all(
        partial_terms.astype(jnp.bfloat16).reshape(tokens_here, img_count, width),
        "img",
        split_axis=1,
        concat_axis=1,
        tiled=True,
    )
    update = jnp.sum(shares.astype(jnp.float32), axis=1)
    own_text = lax.dynamic_slice_in_dim(text, lax.axis_index("img") * width, width, 1)
    return (own_text.astype(jnp.float32) + jnp.tanh(attn_gate[0]) * update).astype(jnp.bfloat16)


BF16, F32 = jnp.bfloat16, jnp.float32
SMEM = pl.BlockSpec(memory_space=pltpu.SMEM)
VMEM = pl.BlockSpec(memory_space=pltpu.VMEM)
CHIPS = 4


def call(kernel, args, specs, outs, out_specs=None, scratch=(), flops=0, size=0, name=None, grid=()):
    return pl.pallas_call(
        kernel,
        out_shape=outs,
        in_specs=specs,
        out_specs=[VMEM] * len(outs) if out_specs is None else out_specs,
        scratch_shapes=scratch,
        grid=grid,
        compiler_params=pltpu.CompilerParams(vmem_limit_bytes=24 * 2**20),
        cost_estimate=pl.CostEstimate(flops=flops, bytes_accessed=size, transcendentals=0),
        name=name,
    )(*args)


def block(index, size):
    return pl.ds(pl.multiple_of(index * size, size), size)


def vis_far_kernel(where, vis, out):
    out[...] = vis[:, block(1 - where[0] // 2, out.shape[1])]


def vis_side_kernel(where, vis, landed, keep, give):
    chip = where[0]
    part = keep.shape[1]
    rows = vis.shape[0]
    side = lax.rem(chip, 2)
    keep[:rows, :] = vis[:, block(chip, part)]
    give[:rows, :] = vis[:, block(chip ^ 1, part)]
    keep[rows:, :] = landed[:, block(side, part)]
    give[rows:, :] = landed[:, block(1 - side, part)]


def spread_kernel(where, text, gain, near, far, text_keep, text_give, scale):
    chip, core, plane = where[0], where[1], where[2]
    tokens, width = text.shape
    part = width // 2
    half = text_keep.shape[1]
    line = chip // 2
    step = 16
    for r in range(0, tokens, step):
        x = text[r : r + step, :].astype(F32)
        mean_sq = jnp.mean(x * x, axis=-1, keepdims=True)
        scale[r : r + step, :] = jnp.broadcast_to(lax.rsqrt(mean_sq + EPS), (step, 128))
    for out, index in ((far, 1 - line), (near, line)):
        cols = block(index, part)
        row_gain = gain[:, cols]
        for r in range(0, tokens, step):
            x = text[r : r + step, cols].astype(F32)
            out[r : r + step, :] = (x * scale[r : r + step, 0:1] * row_gain).astype(BF16)
    text_keep[...] = text[:, block(2 * plane + core, half)]
    text_give[...] = text[:, block(2 * plane + 1 - core, half)]


def cut_kernel(where, q_own, kv_own, q_keep, q_give, kv_give, sems):
    core = where[1]
    half = q_give.shape[1]
    head = kv_give.shape[1] // CHIPS
    copies = [
        pltpu.make_async_copy(q_own.at[:, block(1 - core, half)], q_give, sems.at[0]),
        pltpu.make_async_copy(q_own.at[:, block(core, half)], q_keep, sems.at[1]),
    ]
    for j in range(CHIPS):
        copies.append(
            pltpu.make_async_copy(
                kv_own.at[:, block(2 * j + 1 - core, head)],
                kv_give.at[:, pl.ds(j * head, head)],
                sems.at[2 + j],
            )
        )
    for copy in copies:
        copy.start()
    for copy in copies:
        copy.wait()


def kv_kernel(where, vis, vis_other, kv_own, kv_other, keep, give):
    core = where[1]
    rows = kv_own.shape[0]
    head = kv_other.shape[1] // CHIPS
    near, far = block(core, rows), block(1 - core, rows)
    x_near = jnp.concatenate((vis[:, near], vis_other[:, near]), axis=0)
    x_far = jnp.concatenate((vis[:, far], vis_other[:, far]), axis=0)
    count = vis.shape[0] // CHIPS
    for j in range(CHIPS):
        cols = slice(j * head, (j + 1) * head)
        out = jnp.dot(x_near, kv_own[:, block(2 * j + core, head)], preferred_element_type=F32)
        out += jnp.dot(x_far, kv_other[:, cols], preferred_element_type=F32)
        for k, ref in enumerate((keep, give, keep, give) * 2):
            row = (k // 2) * count
            ref[row : row + count, cols] = out[k * count : (k + 1) * count]


def kv_side_kernel(own, landed, give):
    count = own.shape[0] // CHIPS
    for k in range(2):
        rows = slice((2 * k + 1) * count, (2 * k + 2) * count)
        give[k * count : (k + 1) * count, :] = own[rows, :] + landed[rows, :]


def kv_norm_kernel(where, k_gain, own, landed, side, *outs):
    plane = where[2]
    head = outs[0].shape[1]
    dim = head // 2
    count = own.shape[0] // CHIPS
    for t in range(CHIPS):
        cols = block(plane ^ t, head)
        for k in range(2):
            rows = slice(2 * k * count, (2 * k + 1) * count)
            here = slice(k * count, (k + 1) * count)
            total = (own[rows, cols] + landed[rows, cols]) + side[here, cols]
            keys = head_norm(total[:, :dim], k_gain[...])
            outs[t][here, :dim] = keys.astype(BF16)
            outs[t][here, dim:] = total[:, dim:].astype(BF16)


def join_kernel(*refs):
    out = refs[-1]
    rows = refs[0].shape[0]
    for k, x in enumerate(refs[:-1]):
        out[k * rows : (k + 1) * rows, :] = x[...]


def query_share(index, own, other, first, second, flip):
    rows = first.shape[0]
    total = None
    for weight, k in ((first, index), (second, index ^ flip)):
        cols = block(k, rows)
        x = jnp.concatenate((own[:, cols], other[:, cols]), axis=0)
        share = jnp.dot(x, weight[...], preferred_element_type=F32)
        total = share if total is None else total + share
    return total


def early_kernel(where, own, other, q_keep, q_other, out):
    index = 2 * lax.rem(where[0], 2) + where[1]
    out[...] = query_share(index, own, other, q_keep, q_other, 1)


def late_kernel(where, own, other, q_side, q_corner, early, *refs):
    out = refs[-1]
    rows = early.shape[0]
    index = (2 * lax.rem(where[0], 2) + where[1]) ^ 2
    share = early[...] + query_share(index, own, other, q_side, q_corner, 1)
    out[:rows, :] = share.astype(out.dtype)
    for k, kv in enumerate(refs[:-1]):
        out[rows:, k * kv.shape[1] : (k + 1) * kv.shape[1]] = kv[...]


def attend_kernel(q_gain, first, kv_first, kv_side, landed, bias, context):
    dim = q_gain.shape[1]
    rows, half = context.shape
    head = 2 * dim
    kv = [kv_first[...], kv_side[...]]
    kv += [landed[rows:, k * head : (k + 1) * head] for k in range(half // head)]
    keys = jnp.concatenate([x[:, :dim] for x in kv], axis=0)
    values = jnp.concatenate([x[:, dim:] for x in kv], axis=0)
    step = 128
    for r in range(0, rows, step):
        for g in range(half // dim):
            cols = slice(g * dim, (g + 1) * dim)
            query = first[r : r + step, cols] + landed[r : r + step, cols].astype(F32)
            query = head_norm(query, q_gain[...]).astype(BF16)
            scores = lax.dot_general(
                query, keys, (((1,), (1,)), ((), ())), preferred_element_type=F32
            )
            scores = scores * dim ** (-0.5) + bias[r : r + step, :]
            weights = jnp.exp(scores - jnp.max(scores, axis=-1, keepdims=True))
            total = jnp.sum(weights, axis=-1, keepdims=True)
            acc = jnp.dot(weights.astype(BF16), values, preferred_element_type=F32)
            context[r : r + step, cols] = (acc / total).astype(BF16)


def out_kernel(where, near, far, o_own, o_side, own, other):
    core = where[1]
    tokens, width = own.shape
    half = near.shape[1]
    turned = jnp.concatenate((far[tokens:, :], far[:tokens, :]), axis=0)
    for k, weight in enumerate((o_own, o_side)):
        share = jnp.dot(near[...], weight[block(core, half), :], preferred_element_type=F32)
        share += jnp.dot(turned, weight[block(1 - core, half), :], preferred_element_type=F32)
        share = share.astype(BF16)
        cols = slice(k * width // 2, (k + 1) * width // 2)
        own[:, cols] = share[:tokens]
        other[:, cols] = share[tokens:]


def pick_kernel(where, own, landed, *outs):
    first = where[0] ^ where[2]
    half = outs[0].shape[1]
    for t in range(CHIPS):
        for s in range(CHIPS):

            @pl.when((first ^ t) == s)
            def _():
                outs[t][...] = (own, landed)[s // 2][:, (s % 2) * half : (s % 2 + 1) * half]


def mixed_rows(gate, text, shares):
    x = [share[...].astype(F32) for share in shares]
    update = (x[0] + x[1]) + (x[2] + x[3])
    return (text[...].astype(F32) + gate[0] * update).astype(BF16)


def give_kernel(gate, text, *refs):
    refs[CHIPS][...] = mixed_rows(gate, text, refs[:CHIPS])


def last_kernel(where, gate, text, back, *refs):
    shares, out = refs[:CHIPS], refs[CHIPS]
    core = where[1]
    half = text.shape[1]
    out[:, block(core, half)] = mixed_rows(gate, text, shares)
    out[:, block(1 - core, half)] = back[...]


def paired(
    text,
    input_gain,
    q_weight,
    kv_weight,
    o_weight,
    q_gain,
    k_gain,
    attn_gate,
    vision,
    segment_ids,
    seg_images,
    image_slot,
):
    ctx_count = lax.axis_size("ctx")
    place, plane = lax.axis_index("ctx"), lax.axis_index("img")
    chip, core = place // 2, place % 2
    where = jnp.stack((chip, core, plane)).astype(jnp.int32)
    tokens, width = text.shape
    head_dim = q_gain.shape[0]
    rows_dev, cols_plane = q_weight.shape
    half = cols_plane // 2
    part = 2 * rows_dev
    slots_here, vt_dev = vision.shape[:2]
    vis_here = slots_here * vt_dev
    kv_cols = kv_weight.shape[1] // 2

    def shape(rows, cols, kind=BF16):
        return jax.ShapeDtypeStruct((rows, cols), kind)

    def swap(x):
        return lax.ppermute(x, "ctx", [(k, k ^ 1) for k in range(ctx_count)])

    def along_x(x):
        return lax.ppermute(x, "ctx", [(k, k ^ 2) for k in range(ctx_count)])

    def along_y(x):
        return lax.ppermute(x, "ctx", [(k, k ^ 4) for k in range(ctx_count)])

    def across(x, t):
        return lax.ppermute(x, "img", [(k, k ^ t) for k in range(CHIPS)])

    steps = range(1, CHIPS)
    vis = vision.reshape(vis_here, width)

    vis_far = call(
        vis_far_kernel, (where, vis), [SMEM, VMEM], [shape(vis_here, width // 2)], name="vis_far"
    )[0]
    vis_y = along_y(vis_far)
    vis_keep, vis_give = call(
        vis_side_kernel,
        (where, vis, vis_y),
        [SMEM, VMEM, VMEM],
        [shape(2 * vis_here, part)] * 2,
        name="vis_side",
    )
    vis_own = jnp.concatenate((vis_keep, along_x(vis_give)))
    vis_other = swap(vis_own)

    near, far, text_keep, text_give = call(
        spread_kernel,
        (where, text, input_gain[None]),
        [SMEM] + [VMEM] * 2,
        [shape(tokens, width // 2)] * 2 + [shape(tokens, half)] * 2,
        scratch=[pltpu.VMEM((tokens, 128), F32)],
        flops=8 * tokens * width,
        size=4 * 2**20,
        name="spread",
    )
    far = along_y(far)
    q_keep, q_give, kv_give = call(
        cut_kernel,
        (where, q_weight, kv_weight),
        [SMEM, VMEM, VMEM],
        [shape(rows_dev, half)] * 2 + [shape(rows_dev, kv_cols)],
        scratch=[pltpu.SemaphoreType.DMA((2 + CHIPS,))],
        size=4 * 2**20,
        name="cut",
    )
    q_side = along_x(q_keep)
    q_other, kv_other = swap(q_give), swap(kv_give)
    q_corner = along_x(q_other)

    kv_keep, kv_far = call(
        kv_kernel,
        (where, vis_own, vis_other, kv_weight, kv_other),
        [SMEM] + [VMEM] * 4,
        [shape(4 * vis_here, kv_cols, F32)] * 2,
        flops=4 * vis_here * ctx_count * part * kv_cols,
        size=4 * 2**20,
        name="kv_shares",
    )
    kv_y = along_y(kv_far)
    kv_give = call(
        kv_side_kernel,
        (kv_keep, kv_y),
        [VMEM] * 2,
        [shape(2 * vis_here, kv_cols, F32)],
        name="kv_side",
    )[0]
    heads = call(
        kv_norm_kernel,
        (where, k_gain[None], kv_keep, kv_y, along_x(kv_give)),
        [SMEM] + [VMEM] * 4,
        [shape(2 * vis_here, 2 * head_dim)] * CHIPS,
        name="kv_norm",
    )
    kv_first = call(
        join_kernel,
        [heads[0]] + [across(heads[t], t) for t in steps],
        [VMEM] * CHIPS,
        [shape(8 * vis_here, 2 * head_dim)],
        name="kv_join",
    )[0]
    kv_side = along_x(kv_first)

    blocks = ((far, swap(far)), (near, swap(near)))
    early = [
        call(
            early_kernel,
            (where, *pair, q_keep, q_other),
            [SMEM] + [VMEM] * 4,
            [shape(2 * tokens, half, F32)],
            flops=4 * tokens * part * half,
            size=2 * 2**20,
            name="q_early",
        )[0]
        for pair in blocks
    ]
    kv_lines = kv_first.shape[0] * kv_first.shape[1] * 2 // half
    landed = along_y(
        call(
            late_kernel,
            (where, *blocks[0], q_side, q_corner, early[0], kv_first, kv_side),
            [SMEM] + [VMEM] * 7,
            [shape(2 * tokens + kv_lines, half)],
            flops=4 * tokens * part * half,
            size=2 * 2**20,
            name="q_far",
        )[0]
    )
    q_first = call(
        late_kernel,
        (where, *blocks[1], q_side, q_corner, early[1]),
        [SMEM] + [VMEM] * 5,
        [shape(2 * tokens, half, F32)],
        flops=4 * tokens * part * half,
        size=2 * 2**20,
        name="q_near",
    )[0]
    o_weight, _ = lax.optimization_barrier((o_weight, (q_side, q_corner)))
    o_side = along_x(o_weight)

    ids = jnp.concatenate((segment_ids, swap(segment_ids)))
    images = jnp.arange(image_slot.shape[0])
    slot_of = jnp.sum(
        jnp.where(seg_images[:, :, None] == images, image_slot[None, None, :], 0), axis=2
    )
    numbers = jnp.arange(seg_images.shape[0])
    own_slots = jnp.sum(
        jnp.where((ids[:, None] == numbers)[:, :, None], slot_of[None], 0), axis=1
    )
    key_rows = jnp.arange(CHIPS * CHIPS * 2 * vis_here)
    key_plane = plane ^ (key_rows // (2 * vis_here) % CHIPS)
    key_slot = key_plane * slots_here + key_rows // vt_dev % slots_here
    sees = jnp.any(own_slots[:, :, None] == key_slot, axis=1)
    bias = jnp.where(sees, 0.0, NEG).astype(F32)

    context = call(
        attend_kernel,
        (q_gain[None], q_first, kv_first, kv_side, landed, bias),
        [VMEM] * 6,
        [shape(2 * tokens, half)],
        flops=8 * tokens * half * bias.shape[1],
        size=2 * 2**20,
        name="attend",
    )[0]

    context_y = along_y(context)
    shares = [
        call(
            out_kernel,
            (where, x, swap(x), o_weight, o_side),
            [SMEM] + [VMEM] * 4,
            [shape(tokens, 2 * half)] * 2,
            flops=8 * tokens * cols_plane * half,
            size=2 * 2**20,
            name="o_share",
        )
        for x in (context_y, context)
    ]
    summands = []
    for rows in (1, 0):
        picked = call(
            pick_kernel,
            (where, shares[1][rows], along_y(shares[0][rows])),
            [SMEM] + [VMEM] * 2,
            [shape(tokens, half)] * CHIPS,
            flops=2**20,
            size=2**20,
            name="pick",
        )
        summands.append([picked[0]] + [across(picked[t], t) for t in steps])
    gate = jnp.tanh(attn_gate)
    give = call(
        give_kernel,
        (gate, swap(text_give), *summands[0]),
        [SMEM] + [VMEM] * (1 + CHIPS),
        [shape(tokens, half)],
        flops=2**20,
        size=2**20,
        name="mix_give",
    )[0]
    return call(
        last_kernel,
        (where, gate, text_keep, swap(give), *summands[1]),
        [SMEM, SMEM] + [VMEM] * (2 + CHIPS),
        [shape(tokens, 2 * half)],
        flops=2**20,
        size=2**20,
        name="mix_keep",
    )[0]


def solution(mesh):
    fits = mesh.shape["img"] == 4 and mesh.shape["ctx"] == 8
    return jax.shard_map(
        paired if fits else general,
        mesh=mesh,
        in_specs=(
            P("ctx", None),
            P(),
            P("ctx", "img"),
            P("ctx", None),
            P("img", "ctx"),
            P(),
            P(),
            P(),
            P("img", "ctx", None),
            P("ctx"),
            P(),
            P(),
        ),
        out_specs=P("ctx", "img"),
        check_vma=False,
    )
```

```python
import jax
import jax.numpy as jnp
from jax import lax
from jax.experimental import pallas as pl
from jax.experimental.pallas import tpu as pltpu
from jax.sharding import PartitionSpec as P

KVH = 8


EPS = 1e-05
NEG = -1e30


def head_norm(values, gain):
    mean_sq = jnp.mean(values * values, axis=-1, keepdims=True)
    return values * lax.rsqrt(mean_sq + EPS) * gain


def attend(query, keys, values, mask):
    scale = query.shape[-1] ** (-0.5)
    scores = jnp.einsum("tkgd,nkd->tkgn", query, keys, preferred_element_type=jnp.float32) * scale
    live = mask[:, None, None, :]
    scores = jnp.where(live, scores, NEG)
    top = jnp.max(scores, axis=-1)
    weights = jnp.where(live, jnp.exp(scores - top[..., None]), 0.0)
    total = jnp.sum(weights, axis=-1)
    acc = jnp.einsum(
        "tkgn,nkd->tkgd", weights.astype(jnp.bfloat16), values, preferred_element_type=jnp.float32
    )
    return acc / total[..., None]


def general(
    text,
    input_gain,
    q_weight,
    kv_weight,
    o_weight,
    q_gain,
    k_gain,
    attn_gate,
    vision,
    segment_ids,
    seg_images,
    image_slot,
):
    tokens_here = text.shape[0]
    head_dim = q_gain.shape[0]
    ctx_count = lax.axis_size("ctx")
    img_count = lax.axis_size("img")
    heads_here = q_weight.shape[1] // head_dim
    kv_heads = max(1, KVH // img_count)
    group = heads_here // kv_heads
    slots_here, vt_dev = vision.shape[:2]
    rows_here = slots_here * vt_dev

    o_full = lax.all_gather(o_weight, "ctx", axis=1, tiled=True)
    vision_cols = lax.all_to_all(
        vision.reshape(rows_here, -1), "ctx", split_axis=1, concat_axis=0, tiled=True
    )
    hidden = head_norm(text.astype(jnp.float32), input_gain).astype(jnp.bfloat16)
    hidden_cols = lax.all_to_all(hidden, "ctx", split_axis=1, concat_axis=0, tiled=True)

    kv_share = jnp.dot(vision_cols, kv_weight, preferred_element_type=jnp.float32)
    kv_shares = lax.all_to_all(
        kv_share.reshape(ctx_count, rows_here, -1), "ctx", split_axis=0, concat_axis=0, tiled=True
    )
    projected = jnp.sum(kv_shares, axis=0).reshape(rows_here, KVH, 2, head_dim)
    keys = head_norm(projected[:, :, 0], k_gain).astype(jnp.bfloat16)
    values = projected[:, :, 1].astype(jnp.bfloat16)
    kv_rows = jnp.stack((keys, values), axis=2)
    owners = jnp.arange(img_count)[:, None] * KVH // img_count + jnp.arange(kv_heads)[None, :]
    kv_out = jnp.take(kv_rows, owners, axis=1).transpose(1, 0, 2, 3, 4)
    kv_in = lax.all_to_all(kv_out, "img", split_axis=0, concat_axis=0, tiled=True)
    kv_all = lax.all_gather(kv_in, "ctx", axis=0, tiled=False)

    q_share = jnp.dot(hidden_cols, q_weight, preferred_element_type=jnp.float32)
    q_shares = lax.all_to_all(
        q_share.astype(jnp.bfloat16).reshape(ctx_count, tokens_here, -1),
        "ctx",
        split_axis=0,
        concat_axis=0,
        tiled=True,
    )
    query = jnp.sum(q_shares.astype(jnp.float32), axis=0)
    query = head_norm(query.reshape(tokens_here, kv_heads, group, head_dim), q_gain).astype(
        jnp.bfloat16
    )

    slots = img_count * slots_here
    own_slots = jnp.take(image_slot, jnp.take(seg_images, segment_ids, axis=0), axis=0)
    slot_ids = jnp.arange(slots, dtype=jnp.int32)
    sees = jnp.any(own_slots[:, :, None] == slot_ids[None, None, :], axis=1)
    flat = kv_all.reshape(ctx_count * slots * vt_dev, kv_heads, 2, head_dim)
    mask = jnp.broadcast_to(
        sees[:, None, :, None], (tokens_here, ctx_count, slots, vt_dev)
    ).reshape(tokens_here, -1)
    context = attend(query, flat[:, :, 0], flat[:, :, 1], mask)
    context = context.astype(jnp.bfloat16).reshape(tokens_here, heads_here * head_dim)
    partial_terms = jnp.dot(context, o_full, preferred_element_type=jnp.float32)
    width = partial_terms.shape[1] // img_count
    shares = lax.all_to_all(
        partial_terms.astype(jnp.bfloat16).reshape(tokens_here, img_count, width),
        "img",
        split_axis=1,
        concat_axis=1,
        tiled=True,
    )
    update = jnp.sum(shares.astype(jnp.float32), axis=1)
    own_text = lax.dynamic_slice_in_dim(text, lax.axis_index("img") * width, width, 1)
    return (own_text.astype(jnp.float32) + jnp.tanh(attn_gate[0]) * update).astype(jnp.bfloat16)


BF16, F32 = jnp.bfloat16, jnp.float32
SMEM = pl.BlockSpec(memory_space=pltpu.SMEM)
VMEM = pl.BlockSpec(memory_space=pltpu.VMEM)
CHIPS = 4


def call(kernel, args, specs, outs, out_specs=None, scratch=(), flops=0, size=0, name=None, grid=()):
    return pl.pallas_call(
        kernel,
        out_shape=outs,
        in_specs=specs,
        out_specs=[VMEM] * len(outs) if out_specs is None else out_specs,
        scratch_shapes=scratch,
        grid=grid,
        compiler_params=pltpu.CompilerParams(vmem_limit_bytes=24 * 2**20),
        cost_estimate=pl.CostEstimate(flops=flops, bytes_accessed=size, transcendentals=0),
        name=name,
    )(*args)


def block(index, size):
    return pl.ds(pl.multiple_of(index * size, size), size)


def vis_far_kernel(where, vis, out):
    out[...] = vis[:, block(1 - where[0] // 2, out.shape[1])]


def vis_side_kernel(where, vis, landed, keep, give):
    chip = where[0]
    part = keep.shape[1]
    rows = vis.shape[0]
    side = lax.rem(chip, 2)
    keep[:rows, :] = vis[:, block(chip, part)]
    give[:rows, :] = vis[:, block(chip ^ 1, part)]
    keep[rows:, :] = landed[:, block(side, part)]
    give[rows:, :] = landed[:, block(1 - side, part)]


def spread_kernel(where, text, gain, near, far, text_keep, text_give, scale):
    chip, core, plane = where[0], where[1], where[2]
    tokens, width = text.shape
    part = width // 2
    half = text_keep.shape[1]
    line = chip // 2
    step = 16
    for r in range(0, tokens, step):
        x = text[r : r + step, :].astype(F32)
        mean_sq = jnp.mean(x * x, axis=-1, keepdims=True)
        scale[r : r + step, :] = jnp.broadcast_to(lax.rsqrt(mean_sq + EPS), (step, 128))
    for out, index in ((far, 1 - line), (near, line)):
        cols = block(index, part)
        row_gain = gain[:, cols]
        for r in range(0, tokens, step):
            x = text[r : r + step, cols].astype(F32)
            out[r : r + step, :] = (x * scale[r : r + step, 0:1] * row_gain).astype(BF16)
    text_keep[...] = text[:, block(2 * plane + core, half)]
    text_give[...] = text[:, block(2 * plane + 1 - core, half)]


def cut_kernel(where, q_own, kv_own, q_keep, q_give, kv_give, sems):
    core = where[1]
    half = q_give.shape[1]
    head = kv_give.shape[1] // CHIPS
    copies = [
        pltpu.make_async_copy(q_own.at[:, block(1 - core, half)], q_give, sems.at[0]),
        pltpu.make_async_copy(q_own.at[:, block(core, half)], q_keep, sems.at[1]),
    ]
    for j in range(CHIPS):
        copies.append(
            pltpu.make_async_copy(
                kv_own.at[:, block(2 * j + 1 - core, head)],
                kv_give.at[:, pl.ds(j * head, head)],
                sems.at[2 + j],
            )
        )
    for copy in copies:
        copy.start()
    for copy in copies:
        copy.wait()


def kv_kernel(where, vis, vis_other, kv_own, kv_other, keep, give):
    core = where[1]
    rows = kv_own.shape[0]
    head = kv_other.shape[1] // CHIPS
    near, far = block(core, rows), block(1 - core, rows)
    x_near = jnp.concatenate((vis[:, near], vis_other[:, near]), axis=0)
    x_far = jnp.concatenate((vis[:, far], vis_other[:, far]), axis=0)
    count = vis.shape[0] // CHIPS
    for j in range(CHIPS):
        cols = slice(j * head, (j + 1) * head)
        out = jnp.dot(x_near, kv_own[:, block(2 * j + core, head)], preferred_element_type=F32)
        out += jnp.dot(x_far, kv_other[:, cols], preferred_element_type=F32)
        for k, ref in enumerate((keep, give, keep, give) * 2):
            row = (k // 2) * count
            ref[row : row + count, cols] = out[k * count : (k + 1) * count]


def kv_side_kernel(own, landed, give):
    count = own.shape[0] // CHIPS
    for k in range(2):
        rows = slice((2 * k + 1) * count, (2 * k + 2) * count)
        give[k * count : (k + 1) * count, :] = own[rows, :] + landed[rows, :]


def kv_norm_kernel(where, k_gain, own, landed, side, *outs):
    plane = where[2]
    head = outs[0].shape[1]
    dim = head // 2
    count = own.shape[0] // CHIPS
    for t in range(CHIPS):
        cols = block(plane ^ t, head)
        for k in range(2):
            rows = slice(2 * k * count, (2 * k + 1) * count)
            here = slice(k * count, (k + 1) * count)
            total = (own[rows, cols] + landed[rows, cols]) + side[here, cols]
            keys = head_norm(total[:, :dim], k_gain[...])
            outs[t][here, :dim] = keys.astype(BF16)
            outs[t][here, dim:] = total[:, dim:].astype(BF16)


def join_kernel(*refs):
    out = refs[-1]
    rows = refs[0].shape[0]
    for k, x in enumerate(refs[:-1]):
        out[k * rows : (k + 1) * rows, :] = x[...]


def query_share(index, own, other, first, second, flip):
    rows = first.shape[0]
    total = None
    for weight, k in ((first, index), (second, index ^ flip)):
        cols = block(k, rows)
        x = jnp.concatenate((own[:, cols], other[:, cols]), axis=0)
        share = jnp.dot(x, weight[...], preferred_element_type=F32)
        total = share if total is None else total + share
    return total


def early_kernel(where, own, other, q_keep, q_other, out):
    index = 2 * lax.rem(where[0], 2) + where[1]
    out[...] = query_share(index, own, other, q_keep, q_other, 1)


def late_kernel(where, own, other, q_side, q_corner, early, *refs):
    out = refs[-1]
    rows = early.shape[0]
    index = (2 * lax.rem(where[0], 2) + where[1]) ^ 2
    share = early[...] + query_share(index, own, other, q_side, q_corner, 1)
    out[:rows, :] = share.astype(out.dtype)
    for k, kv in enumerate(refs[:-1]):
        out[rows:, k * kv.shape[1] : (k + 1) * kv.shape[1]] = kv[...]


def attend_kernel(q_gain, first, kv_first, kv_side, landed, bias, context):
    dim = q_gain.shape[1]
    rows, half = context.shape
    head = 2 * dim
    kv = [kv_first[...], kv_side[...]]
    kv += [landed[rows:, k * head : (k + 1) * head] for k in range(half // head)]
    keys = jnp.concatenate([x[:, :dim] for x in kv], axis=0)
    values = jnp.concatenate([x[:, dim:] for x in kv], axis=0)
    step = 128
    for r in range(0, rows, step):
        for g in range(half // dim):
            cols = slice(g * dim, (g + 1) * dim)
            query = first[r : r + step, cols] + landed[r : r + step, cols].astype(F32)
            query = head_norm(query, q_gain[...]).astype(BF16)
            scores = lax.dot_general(
                query, keys, (((1,), (1,)), ((), ())), preferred_element_type=F32
            )
            scores = scores * dim ** (-0.5) + bias[r : r + step, :]
            weights = jnp.exp(scores - jnp.max(scores, axis=-1, keepdims=True))
            total = jnp.sum(weights, axis=-1, keepdims=True)
            acc = jnp.dot(weights.astype(BF16), values, preferred_element_type=F32)
            context[r : r + step, cols] = (acc / total).astype(BF16)


def out_kernel(where, near, far, o_own, o_side, own, other):
    core = where[1]
    tokens, width = own.shape
    half = near.shape[1]
    turned = jnp.concatenate((far[tokens:, :], far[:tokens, :]), axis=0)
    for k, weight in enumerate((o_own, o_side)):
        share = jnp.dot(near[...], weight[block(core, half), :], preferred_element_type=F32)
        share += jnp.dot(turned, weight[block(1 - core, half), :], preferred_element_type=F32)
        share = share.astype(BF16)
        cols = slice(k * width // 2, (k + 1) * width // 2)
        own[:, cols] = share[:tokens]
        other[:, cols] = share[tokens:]


def pick_kernel(where, own, landed, *outs):
    first = where[0] ^ where[2]
    half = outs[0].shape[1]
    for t in range(CHIPS):
        for s in range(CHIPS):

            @pl.when((first ^ t) == s)
            def _():
                outs[t][...] = (own, landed)[s // 2][:, (s % 2) * half : (s % 2 + 1) * half]


def mixed_rows(gate, text, shares):
    x = [share[...].astype(F32) for share in shares]
    update = (x[0] + x[1]) + (x[2] + x[3])
    return (text[...].astype(F32) + gate[0] * update).astype(BF16)


def give_kernel(gate, text, *refs):
    refs[CHIPS][...] = mixed_rows(gate, text, refs[:CHIPS])


def last_kernel(where, gate, text, back, *refs):
    shares, out = refs[:CHIPS], refs[CHIPS]
    core = where[1]
    half = text.shape[1]
    out[:, block(core, half)] = mixed_rows(gate, text, shares)
    out[:, block(1 - core, half)] = back[...]


def paired(
    text,
    input_gain,
    q_weight,
    kv_weight,
    o_weight,
    q_gain,
    k_gain,
    attn_gate,
    vision,
    segment_ids,
    seg_images,
    image_slot,
):
    ctx_count = lax.axis_size("ctx")
    place, plane = lax.axis_index("ctx"), lax.axis_index("img")
    chip, core = place // 2, place % 2
    where = jnp.stack((chip, core, plane)).astype(jnp.int32)
    tokens, width = text.shape
    head_dim = q_gain.shape[0]
    rows_dev, cols_plane = q_weight.shape
    half = cols_plane // 2
    part = 2 * rows_dev
    slots_here, vt_dev = vision.shape[:2]
    vis_here = slots_here * vt_dev
    kv_cols = kv_weight.shape[1] // 2

    def shape(rows, cols, kind=BF16):
        return jax.ShapeDtypeStruct((rows, cols), kind)

    def swap(x):
        return lax.ppermute(x, "ctx", [(k, k ^ 1) for k in range(ctx_count)])

    def along_x(x):
        return lax.ppermute(x, "ctx", [(k, k ^ 2) for k in range(ctx_count)])

    def along_y(x):
        return lax.ppermute(x, "ctx", [(k, k ^ 4) for k in range(ctx_count)])

    def across(x, t):
        return lax.ppermute(x, "img", [(k, k ^ t) for k in range(CHIPS)])

    steps = range(1, CHIPS)
    vis = vision.reshape(vis_here, width)

    vis_far = call(
        vis_far_kernel, (where, vis), [SMEM, VMEM], [shape(vis_here, width // 2)], name="vis_far"
    )[0]
    vis_y = along_y(vis_far)
    vis_keep, vis_give = call(
        vis_side_kernel,
        (where, vis, vis_y),
        [SMEM, VMEM, VMEM],
        [shape(2 * vis_here, part)] * 2,
        name="vis_side",
    )
    vis_own = jnp.concatenate((vis_keep, along_x(vis_give)))
    vis_other = swap(vis_own)

    near, far, text_keep, text_give = call(
        spread_kernel,
        (where, text, input_gain[None]),
        [SMEM] + [VMEM] * 2,
        [shape(tokens, width // 2)] * 2 + [shape(tokens, half)] * 2,
        scratch=[pltpu.VMEM((tokens, 128), F32)],
        flops=8 * tokens * width,
        size=4 * 2**20,
        name="spread",
    )
    where_cut, _ = lax.optimization_barrier((where, vis_y))
    q_keep, q_give, kv_give = call(
        cut_kernel,
        (where_cut, q_weight, kv_weight),
        [SMEM, VMEM, VMEM],
        [shape(rows_dev, half)] * 2 + [shape(rows_dev, kv_cols)],
        scratch=[pltpu.SemaphoreType.DMA((2 + CHIPS,))],
        size=4 * 2**20,
        name="cut",
    )
    q_side = along_x(q_keep)
    q_other, kv_other = swap(q_give), swap(kv_give)

    kv_keep, kv_far = call(
        kv_kernel,
        (where, vis_own, vis_other, kv_weight, kv_other),
        [SMEM] + [VMEM] * 4,
        [shape(4 * vis_here, kv_cols, F32)] * 2,
        flops=4 * vis_here * ctx_count * part * kv_cols,
        size=4 * 2**20,
        name="kv_shares",
    )
    kv_y = along_y(kv_far)
    kv_y, q_side, far = lax.optimization_barrier((kv_y, q_side, far))
    far = along_y(far)
    kv_give = call(
        kv_side_kernel,
        (kv_keep, kv_y),
        [VMEM] * 2,
        [shape(2 * vis_here, kv_cols, F32)],
        name="kv_side",
    )[0]
    q_behind, _ = lax.optimization_barrier((q_other, kv_give))
    q_corner = along_x(q_behind)
    heads = call(
        kv_norm_kernel,
        (where, k_gain[None], kv_keep, kv_y, along_x(kv_give)),
        [SMEM] + [VMEM] * 4,
        [shape(2 * vis_here, 2 * head_dim)] * CHIPS,
        name="kv_norm",
    )
    kv_first = call(
        join_kernel,
        [heads[0]] + [across(heads[t], t) for t in steps],
        [VMEM] * CHIPS,
        [shape(8 * vis_here, 2 * head_dim)],
        name="kv_join",
    )[0]
    kv_side = along_x(kv_first)

    blocks = ((far, swap(far)), (near, swap(near)))
    early = [
        call(
            early_kernel,
            (where, *pair, q_keep, q_other),
            [SMEM] + [VMEM] * 4,
            [shape(2 * tokens, half, F32)],
            flops=4 * tokens * part * half,
            size=2 * 2**20,
            name="q_early",
        )[0]
        for pair in blocks
    ]
    kv_lines = kv_first.shape[0] * kv_first.shape[1] * 2 // half
    landed = along_y(
        call(
            late_kernel,
            (where, *blocks[0], q_side, q_corner, early[0], kv_first, kv_side),
            [SMEM] + [VMEM] * 7,
            [shape(2 * tokens + kv_lines, half)],
            flops=4 * tokens * part * half,
            size=2 * 2**20,
            name="q_far",
        )[0]
    )
    q_first = call(
        late_kernel,
        (where, *blocks[1], q_side, q_corner, early[1]),
        [SMEM] + [VMEM] * 5,
        [shape(2 * tokens, half, F32)],
        flops=4 * tokens * part * half,
        size=2 * 2**20,
        name="q_near",
    )[0]
    o_weight, _ = lax.optimization_barrier((o_weight, kv_side))
    o_side = along_x(o_weight)

    ids = jnp.concatenate((segment_ids, swap(segment_ids)))
    images = jnp.arange(image_slot.shape[0])
    slot_of = jnp.sum(
        jnp.where(seg_images[:, :, None] == images, image_slot[None, None, :], 0), axis=2
    )
    numbers = jnp.arange(seg_images.shape[0])
    own_slots = jnp.sum(
        jnp.where((ids[:, None] == numbers)[:, :, None], slot_of[None], 0), axis=1
    )
    key_rows = jnp.arange(CHIPS * CHIPS * 2 * vis_here)
    key_plane = plane ^ (key_rows // (2 * vis_here) % CHIPS)
    key_slot = key_plane * slots_here + key_rows // vt_dev % slots_here
    sees = jnp.any(own_slots[:, :, None] == key_slot, axis=1)
    bias = jnp.where(sees, 0.0, NEG).astype(F32)

    context = call(
        attend_kernel,
        (q_gain[None], q_first, kv_first, kv_side, landed, bias),
        [VMEM] * 6,
        [shape(2 * tokens, half)],
        flops=8 * tokens * half * bias.shape[1],
        size=2 * 2**20,
        name="attend",
    )[0]

    context_y = along_y(context)
    shares = [
        call(
            out_kernel,
            (where, x, swap(x), o_weight, o_side),
            [SMEM] + [VMEM] * 4,
            [shape(tokens, 2 * half)] * 2,
            flops=8 * tokens * cols_plane * half,
            size=2 * 2**20,
            name="o_share",
        )
        for x in (context_y, context)
    ]
    summands = []
    for rows in (1, 0):
        picked = call(
            pick_kernel,
            (where, shares[1][rows], along_y(shares[0][rows])),
            [SMEM] + [VMEM] * 2,
            [shape(tokens, half)] * CHIPS,
            flops=2**20,
            size=2**20,
            name="pick",
        )
        summands.append([picked[0]] + [across(picked[t], t) for t in steps])
    gate = jnp.tanh(attn_gate)
    give = call(
        give_kernel,
        (gate, swap(text_give), *summands[0]),
        [SMEM] + [VMEM] * (1 + CHIPS),
        [shape(tokens, half)],
        flops=2**20,
        size=2**20,
        name="mix_give",
    )[0]
    return call(
        last_kernel,
        (where, gate, text_keep, swap(give), *summands[1]),
        [SMEM, SMEM] + [VMEM] * (2 + CHIPS),
        [shape(tokens, 2 * half)],
        flops=2**20,
        size=2**20,
        name="mix_keep",
    )[0]


def solution(mesh):
    fits = mesh.shape["img"] == 4 and mesh.shape["ctx"] == 8
    return jax.shard_map(
        paired if fits else general,
        mesh=mesh,
        in_specs=(
            P("ctx", None),
            P(),
            P("ctx", "img"),
            P("ctx", None),
            P("img", "ctx"),
            P(),
            P(),
            P(),
            P("img", "ctx", None),
            P("ctx"),
            P(),
            P(),
        ),
        out_specs=P("ctx", "img"),
        check_vma=False,
    )
```

```python
import jax
import jax.numpy as jnp
from jax import lax
from jax.experimental import pallas as pl
from jax.experimental.pallas import tpu as pltpu
from jax.sharding import PartitionSpec as P

KVH = 8


EPS = 1e-05
NEG = -1e30


def head_norm(values, gain):
    mean_sq = jnp.mean(values * values, axis=-1, keepdims=True)
    return values * lax.rsqrt(mean_sq + EPS) * gain


def attend(query, keys, values, mask):
    scale = query.shape[-1] ** (-0.5)
    scores = jnp.einsum("tkgd,nkd->tkgn", query, keys, preferred_element_type=jnp.float32) * scale
    live = mask[:, None, None, :]
    scores = jnp.where(live, scores, NEG)
    top = jnp.max(scores, axis=-1)
    weights = jnp.where(live, jnp.exp(scores - top[..., None]), 0.0)
    total = jnp.sum(weights, axis=-1)
    acc = jnp.einsum(
        "tkgn,nkd->tkgd", weights.astype(jnp.bfloat16), values, preferred_element_type=jnp.float32
    )
    return acc / total[..., None]


def general(
    text,
    input_gain,
    q_weight,
    kv_weight,
    o_weight,
    q_gain,
    k_gain,
    attn_gate,
    vision,
    segment_ids,
    seg_images,
    image_slot,
):
    tokens_here = text.shape[0]
    head_dim = q_gain.shape[0]
    ctx_count = lax.axis_size("ctx")
    img_count = lax.axis_size("img")
    heads_here = q_weight.shape[1] // head_dim
    kv_heads = max(1, KVH // img_count)
    group = heads_here // kv_heads
    slots_here, vt_dev = vision.shape[:2]
    rows_here = slots_here * vt_dev

    o_full = lax.all_gather(o_weight, "ctx", axis=1, tiled=True)
    vision_cols = lax.all_to_all(
        vision.reshape(rows_here, -1), "ctx", split_axis=1, concat_axis=0, tiled=True
    )
    hidden = head_norm(text.astype(jnp.float32), input_gain).astype(jnp.bfloat16)
    hidden_cols = lax.all_to_all(hidden, "ctx", split_axis=1, concat_axis=0, tiled=True)

    kv_share = jnp.dot(vision_cols, kv_weight, preferred_element_type=jnp.float32)
    kv_shares = lax.all_to_all(
        kv_share.reshape(ctx_count, rows_here, -1), "ctx", split_axis=0, concat_axis=0, tiled=True
    )
    projected = jnp.sum(kv_shares, axis=0).reshape(rows_here, KVH, 2, head_dim)
    keys = head_norm(projected[:, :, 0], k_gain).astype(jnp.bfloat16)
    values = projected[:, :, 1].astype(jnp.bfloat16)
    kv_rows = jnp.stack((keys, values), axis=2)
    owners = jnp.arange(img_count)[:, None] * KVH // img_count + jnp.arange(kv_heads)[None, :]
    kv_out = jnp.take(kv_rows, owners, axis=1).transpose(1, 0, 2, 3, 4)
    kv_in = lax.all_to_all(kv_out, "img", split_axis=0, concat_axis=0, tiled=True)
    kv_all = lax.all_gather(kv_in, "ctx", axis=0, tiled=False)

    q_share = jnp.dot(hidden_cols, q_weight, preferred_element_type=jnp.float32)
    q_shares = lax.all_to_all(
        q_share.astype(jnp.bfloat16).reshape(ctx_count, tokens_here, -1),
        "ctx",
        split_axis=0,
        concat_axis=0,
        tiled=True,
    )
    query = jnp.sum(q_shares.astype(jnp.float32), axis=0)
    query = head_norm(query.reshape(tokens_here, kv_heads, group, head_dim), q_gain).astype(
        jnp.bfloat16
    )

    slots = img_count * slots_here
    own_slots = jnp.take(image_slot, jnp.take(seg_images, segment_ids, axis=0), axis=0)
    slot_ids = jnp.arange(slots, dtype=jnp.int32)
    sees = jnp.any(own_slots[:, :, None] == slot_ids[None, None, :], axis=1)
    flat = kv_all.reshape(ctx_count * slots * vt_dev, kv_heads, 2, head_dim)
    mask = jnp.broadcast_to(
        sees[:, None, :, None], (tokens_here, ctx_count, slots, vt_dev)
    ).reshape(tokens_here, -1)
    context = attend(query, flat[:, :, 0], flat[:, :, 1], mask)
    context = context.astype(jnp.bfloat16).reshape(tokens_here, heads_here * head_dim)
    partial_terms = jnp.dot(context, o_full, preferred_element_type=jnp.float32)
    width = partial_terms.shape[1] // img_count
    shares = lax.all_to_all(
        partial_terms.astype(jnp.bfloat16).reshape(tokens_here, img_count, width),
        "img",
        split_axis=1,
        concat_axis=1,
        tiled=True,
    )
    update = jnp.sum(shares.astype(jnp.float32), axis=1)
    own_text = lax.dynamic_slice_in_dim(text, lax.axis_index("img") * width, width, 1)
    return (own_text.astype(jnp.float32) + jnp.tanh(attn_gate[0]) * update).astype(jnp.bfloat16)


BF16, F32 = jnp.bfloat16, jnp.float32
SMEM = pl.BlockSpec(memory_space=pltpu.SMEM)
VMEM = pl.BlockSpec(memory_space=pltpu.VMEM)
CHIPS = 4


def call(kernel, args, specs, outs, out_specs=None, scratch=(), flops=0, size=0, name=None, grid=()):
    return pl.pallas_call(
        kernel,
        out_shape=outs,
        in_specs=specs,
        out_specs=[VMEM] * len(outs) if out_specs is None else out_specs,
        scratch_shapes=scratch,
        grid=grid,
        compiler_params=pltpu.CompilerParams(vmem_limit_bytes=24 * 2**20),
        cost_estimate=pl.CostEstimate(flops=flops, bytes_accessed=size, transcendentals=0),
        name=name,
    )(*args)


def block(index, size):
    return pl.ds(pl.multiple_of(index * size, size), size)


def vis_far_kernel(where, vis, out):
    out[...] = vis[:, block(1 - where[0] // 2, out.shape[1])]


def vis_side_kernel(where, vis, landed, keep, give):
    chip = where[0]
    part = keep.shape[1]
    rows = vis.shape[0]
    side = lax.rem(chip, 2)
    keep[:rows, :] = vis[:, block(chip, part)]
    give[:rows, :] = vis[:, block(chip ^ 1, part)]
    keep[rows:, :] = landed[:, block(side, part)]
    give[rows:, :] = landed[:, block(1 - side, part)]


def spread_kernel(where, text, gain, near, far, text_keep, text_give, scale):
    chip, core, plane = where[0], where[1], where[2]
    tokens, width = text.shape
    part = width // 2
    half = text_keep.shape[1]
    line = chip // 2
    step = 16
    for r in range(0, tokens, step):
        x = text[r : r + step, :].astype(F32)
        mean_sq = jnp.mean(x * x, axis=-1, keepdims=True)
        scale[r : r + step, :] = jnp.broadcast_to(lax.rsqrt(mean_sq + EPS), (step, 128))
    for out, index in ((far, 1 - line), (near, line)):
        cols = block(index, part)
        row_gain = gain[:, cols]
        for r in range(0, tokens, step):
            x = text[r : r + step, cols].astype(F32)
            out[r : r + step, :] = (x * scale[r : r + step, 0:1] * row_gain).astype(BF16)
    text_keep[...] = text[:, block(2 * plane + core, half)]
    text_give[...] = text[:, block(2 * plane + 1 - core, half)]


def cut_q_kernel(where, q_own, keep, give):
    core = where[1]
    half = keep.shape[1]
    keep[...] = q_own[:, block(core, half)]
    give[...] = q_own[:, block(1 - core, half)]


def kv_kernel(where, vis, vis_other, kv_own, kv_other, keep, give):
    core = where[1]
    rows = kv_own.shape[0]
    head = kv_other.shape[1] // (2 * CHIPS)
    near, far = block(core, rows), block(1 - core, rows)
    x_near = jnp.concatenate((vis[:, near], vis_other[:, near]), axis=0)
    x_far = jnp.concatenate((vis[:, far], vis_other[:, far]), axis=0)
    count = vis.shape[0] // CHIPS
    for j in range(CHIPS):
        cols = slice(j * head, (j + 1) * head)
        heads = block(2 * j + core, head)
        out = jnp.dot(x_near, kv_own[:, heads], preferred_element_type=F32)
        out += jnp.dot(x_far, kv_other[:, heads], preferred_element_type=F32)
        for k, ref in enumerate((keep, give, keep, give) * 2):
            row = (k // 2) * count
            ref[row : row + count, cols] = out[k * count : (k + 1) * count]


def kv_side_kernel(own, landed, give):
    count = own.shape[0] // CHIPS
    for k in range(2):
        rows = slice((2 * k + 1) * count, (2 * k + 2) * count)
        give[k * count : (k + 1) * count, :] = own[rows, :] + landed[rows, :]


def kv_norm_kernel(where, k_gain, own, landed, side, here, there, give):
    plane = where[2]
    count = own.shape[0] // CHIPS
    lines, head = here.shape
    dim = head // 2
    for t, (out, row) in enumerate(((here, 0), (give, 0), (there, 0), (give, lines))):
        cols = block(plane ^ t, head)
        for k in range(2):
            rows = slice(2 * k * count, (2 * k + 1) * count)
            line = slice(k * count, (k + 1) * count)
            total = (own[rows, cols] + landed[rows, cols]) + side[line, cols]
            keys = head_norm(total[:, :dim], k_gain[...])
            to = slice(row + k * count, row + (k + 1) * count)
            out[to, :dim] = keys.astype(BF16)
            out[to, dim:] = total[:, dim:].astype(BF16)


def kv_turn_kernel(there, landed, out):
    lines = there.shape[0]
    out[:lines, :] = there[...]
    out[lines:, :] = landed[lines:, :]


def kv_join_kernel(here, landed, last, out):
    lines = here.shape[0]
    out[:lines, :] = here[...]
    out[lines : 2 * lines, :] = landed[:lines, :]
    out[2 * lines :, :] = last[...]


def query_share(index, own, other, first, second, flip):
    rows = first.shape[0]
    total = None
    for weight, k in ((first, index), (second, index ^ flip)):
        cols = block(k, rows)
        x = jnp.concatenate((own[:, cols], other[:, cols]), axis=0)
        share = jnp.dot(x, weight[...], preferred_element_type=F32)
        total = share if total is None else total + share
    return total


def early_kernel(where, own, other, q_keep, q_other, out):
    index = 2 * lax.rem(where[0], 2) + where[1]
    out[...] = query_share(index, own, other, q_keep, q_other, 1)


def late_kernel(where, own, other, q_side, q_corner, early, *refs):
    out = refs[-1]
    rows = early.shape[0]
    index = (2 * lax.rem(where[0], 2) + where[1]) ^ 2
    share = early[...] + query_share(index, own, other, q_side, q_corner, 1)
    out[:rows, :] = share.astype(out.dtype)
    for k, kv in enumerate(refs[:-1]):
        out[rows:, k * kv.shape[1] : (k + 1) * kv.shape[1]] = kv[...]


def attend_kernel(q_gain, first, kv_first, kv_side, landed, bias, context):
    dim = q_gain.shape[1]
    rows, half = context.shape
    head = 2 * dim
    kv = [kv_first[...], kv_side[...]]
    kv += [landed[rows:, k * head : (k + 1) * head] for k in range(half // head)]
    keys = jnp.concatenate([x[:, :dim] for x in kv], axis=0)
    values = jnp.concatenate([x[:, dim:] for x in kv], axis=0)
    step = 128
    for r in range(0, rows, step):
        for g in range(half // dim):
            cols = slice(g * dim, (g + 1) * dim)
            query = first[r : r + step, cols] + landed[r : r + step, cols].astype(F32)
            query = head_norm(query, q_gain[...]).astype(BF16)
            scores = lax.dot_general(
                query, keys, (((1,), (1,)), ((), ())), preferred_element_type=F32
            )
            scores = scores * dim ** (-0.5) + bias[r : r + step, :]
            weights = jnp.exp(scores - jnp.max(scores, axis=-1, keepdims=True))
            total = jnp.sum(weights, axis=-1, keepdims=True)
            acc = jnp.dot(weights.astype(BF16), values, preferred_element_type=F32)
            context[r : r + step, cols] = (acc / total).astype(BF16)


def out_kernel(where, near, far, o_own, o_early, o_late, own, other):
    core = where[1]
    tokens, width = own.shape
    half = near.shape[1]
    turned = jnp.concatenate((far[tokens:, :], far[:tokens, :]), axis=0)
    share = jnp.dot(near[...], o_own[block(core, half), :], preferred_element_type=F32)
    share += jnp.dot(turned, o_own[block(1 - core, half), :], preferred_element_type=F32)
    own[:, : width // 2] = share[:tokens].astype(BF16)
    other[:, : width // 2] = share[tokens:].astype(BF16)
    top = jnp.where(core == 0, near[...], turned)
    low = jnp.where(core == 0, turned, near[...])
    first = o_early.shape[0]
    share = jnp.dot(top[:, :first], o_early[...], preferred_element_type=F32)
    share += jnp.dot(top[:, first:], o_late[: half - first, :], preferred_element_type=F32)
    share += jnp.dot(low, o_late[half - first :, :], preferred_element_type=F32)
    own[:, width // 2 :] = share[:tokens].astype(BF16)
    other[:, width // 2 :] = share[tokens:].astype(BF16)


def pick_kernel(where, own, landed, *outs):
    first = where[0] ^ where[2]
    half = outs[0].shape[1]
    for t in range(CHIPS):
        for s in range(CHIPS):

            @pl.when((first ^ t) == s)
            def _():
                outs[t][...] = (own, landed)[s // 2][:, (s % 2) * half : (s % 2 + 1) * half]


def mixed_rows(gate, text, shares):
    x = [share[...].astype(F32) for share in shares]
    update = (x[0] + x[1]) + (x[2] + x[3])
    return (text[...].astype(F32) + gate[0] * update).astype(BF16)


def give_kernel(gate, text, *refs):
    refs[CHIPS][...] = mixed_rows(gate, text, refs[:CHIPS])


def last_kernel(where, gate, text, back, *refs):
    shares, out = refs[:CHIPS], refs[CHIPS]
    core = where[1]
    half = text.shape[1]
    out[:, block(core, half)] = mixed_rows(gate, text, shares)
    out[:, block(1 - core, half)] = back[...]


def paired(
    text,
    input_gain,
    q_weight,
    kv_weight,
    o_weight,
    q_gain,
    k_gain,
    attn_gate,
    vision,
    segment_ids,
    seg_images,
    image_slot,
):
    ctx_count = lax.axis_size("ctx")
    place, plane = lax.axis_index("ctx"), lax.axis_index("img")
    chip, core = place // 2, place % 2
    where = jnp.stack((chip, core, plane)).astype(jnp.int32)
    tokens, width = text.shape
    head_dim = q_gain.shape[0]
    rows_dev, cols_plane = q_weight.shape
    half = cols_plane // 2
    part = 2 * rows_dev
    slots_here, vt_dev = vision.shape[:2]
    vis_here = slots_here * vt_dev
    kv_cols = kv_weight.shape[1] // 2

    def shape(rows, cols, kind=BF16):
        return jax.ShapeDtypeStruct((rows, cols), kind)

    def swap(x):
        return lax.ppermute(x, "ctx", [(k, k ^ 1) for k in range(ctx_count)])

    def along_x(x):
        return lax.ppermute(x, "ctx", [(k, k ^ 2) for k in range(ctx_count)])

    def along_y(x):
        return lax.ppermute(x, "ctx", [(k, k ^ 4) for k in range(ctx_count)])

    def across(x, t):
        return lax.ppermute(x, "img", [(k, k ^ t) for k in range(CHIPS)])

    steps = range(1, CHIPS)
    vis = vision.reshape(vis_here, width)
    kv_other = swap(kv_weight)

    vis_far = call(
        vis_far_kernel, (where, vis), [SMEM, VMEM], [shape(vis_here, width // 2)], name="vis_far"
    )[0]
    vis_y = along_y(vis_far)
    o_early = along_x(o_weight[: half // 2])
    vis_y, o_early = lax.optimization_barrier((vis_y, o_early))
    vis_keep, vis_give = call(
        vis_side_kernel,
        (where, vis, vis_y),
        [SMEM, VMEM, VMEM],
        [shape(2 * vis_here, part)] * 2,
        name="vis_side",
    )
    vis_own = jnp.concatenate((vis_keep, along_x(vis_give)))
    vis_other = swap(vis_own)

    near, far, text_keep, text_give = call(
        spread_kernel,
        (where, text, input_gain[None]),
        [SMEM] + [VMEM] * 2,
        [shape(tokens, width // 2)] * 2 + [shape(tokens, half)] * 2,
        scratch=[pltpu.VMEM((tokens, 128), F32)],
        flops=8 * tokens * width,
        size=4 * 2**20,
        name="spread",
    )
    where_cut, _ = lax.optimization_barrier((where, vis_own))
    q_keep, q_give = call(
        cut_q_kernel, (where_cut, q_weight), [SMEM, VMEM], [shape(rows_dev, half)] * 2, name="cut_q"
    )
    q_side, q_other = along_x(q_keep), swap(q_give)

    kv_keep, kv_far = call(
        kv_kernel,
        (where, vis_own, vis_other, kv_weight, kv_other),
        [SMEM] + [VMEM] * 4,
        [shape(4 * vis_here, kv_cols, F32)] * 2,
        flops=4 * vis_here * ctx_count * part * kv_cols,
        size=4 * 2**20,
        name="kv_shares",
    )
    kv_y = along_y(kv_far)
    kv_y, q_side, far = lax.optimization_barrier((kv_y, q_side, far))
    far = along_y(far)
    kv_give = call(
        kv_side_kernel,
        (kv_keep, kv_y),
        [VMEM] * 2,
        [shape(2 * vis_here, kv_cols, F32)],
        name="kv_side",
    )[0]
    q_behind, _ = lax.optimization_barrier((q_other, kv_give))
    q_corner = along_x(q_behind)
    here, there, give = call(
        kv_norm_kernel,
        (where, k_gain[None], kv_keep, kv_y, along_x(kv_give)),
        [SMEM] + [VMEM] * 4,
        [shape(2 * vis_here, 2 * head_dim)] * 2 + [shape(4 * vis_here, 2 * head_dim)],
        name="kv_norm",
    )
    kv_z = across(give, 1)
    turn = call(
        kv_turn_kernel,
        (there, kv_z),
        [VMEM] * 2,
        [shape(4 * vis_here, 2 * head_dim)],
        name="kv_turn",
    )[0]
    kv_first = call(
        kv_join_kernel,
        (here, kv_z, across(turn, 2)),
        [VMEM] * 3,
        [shape(8 * vis_here, 2 * head_dim)],
        name="kv_join",
    )[0]
    far, _ = lax.optimization_barrier((far, kv_first))
    kv_first, q_corner = lax.optimization_barrier((kv_first, q_corner))
    kv_side = along_x(kv_first)

    blocks = ((far, swap(far)), (near, swap(near)))
    early = [
        call(
            early_kernel,
            (where, *pair, q_keep, q_other),
            [SMEM] + [VMEM] * 4,
            [shape(2 * tokens, half, F32)],
            flops=4 * tokens * part * half,
            size=2 * 2**20,
            name="q_early",
        )[0]
        for pair in blocks
    ]
    kv_lines = kv_first.shape[0] * kv_first.shape[1] * 2 // half
    landed = along_y(
        call(
            late_kernel,
            (where, *blocks[0], q_side, q_corner, early[0], kv_first, kv_side),
            [SMEM] + [VMEM] * 7,
            [shape(2 * tokens + kv_lines, half)],
            flops=4 * tokens * part * half,
            size=2 * 2**20,
            name="q_far",
        )[0]
    )
    q_first = call(
        late_kernel,
        (where, *blocks[1], q_side, q_corner, early[1]),
        [SMEM] + [VMEM] * 5,
        [shape(2 * tokens, half, F32)],
        flops=4 * tokens * part * half,
        size=2 * 2**20,
        name="q_near",
    )[0]
    o_late, _ = lax.optimization_barrier((o_weight[half // 2 :], kv_side))
    o_late = along_x(o_late)

    ids = jnp.concatenate((segment_ids, swap(segment_ids)))
    images = jnp.arange(image_slot.shape[0])
    slot_of = jnp.sum(
        jnp.where(seg_images[:, :, None] == images, image_slot[None, None, :], 0), axis=2
    )
    numbers = jnp.arange(seg_images.shape[0])
    own_slots = jnp.sum(
        jnp.where((ids[:, None] == numbers)[:, :, None], slot_of[None], 0), axis=1
    )
    key_rows = jnp.arange(CHIPS * CHIPS * 2 * vis_here)
    key_plane = plane ^ (key_rows // (2 * vis_here) % CHIPS)
    key_slot = key_plane * slots_here + key_rows // vt_dev % slots_here
    sees = jnp.any(own_slots[:, :, None] == key_slot, axis=1)
    bias = jnp.where(sees, 0.0, NEG).astype(F32)

    context = call(
        attend_kernel,
        (q_gain[None], q_first, kv_first, kv_side, landed, bias),
        [VMEM] * 6,
        [shape(2 * tokens, half)],
        flops=8 * tokens * half * bias.shape[1],
        size=2 * 2**20,
        name="attend",
    )[0]

    context_y = along_y(context)
    shares = [
        call(
            out_kernel,
            (where, x, swap(x), o_weight, o_early, o_late),
            [SMEM] + [VMEM] * 5,
            [shape(tokens, 2 * half)] * 2,
            flops=8 * tokens * cols_plane * half,
            size=2 * 2**20,
            name="o_share",
        )
        for x in (context_y, context)
    ]
    summands = []
    for rows in (1, 0):
        picked = call(
            pick_kernel,
            (where, shares[1][rows], along_y(shares[0][rows])),
            [SMEM] + [VMEM] * 2,
            [shape(tokens, half)] * CHIPS,
            flops=2**20,
            size=2**20,
            name="pick",
        )
        summands.append([picked[0]] + [across(picked[t], t) for t in steps])
    gate = jnp.tanh(attn_gate)
    give = call(
        give_kernel,
        (gate, swap(text_give), *summands[0]),
        [SMEM] + [VMEM] * (1 + CHIPS),
        [shape(tokens, half)],
        flops=2**20,
        size=2**20,
        name="mix_give",
    )[0]
    return call(
        last_kernel,
        (where, gate, text_keep, swap(give), *summands[1]),
        [SMEM, SMEM] + [VMEM] * (2 + CHIPS),
        [shape(tokens, 2 * half)],
        flops=2**20,
        size=2**20,
        name="mix_keep",
    )[0]


def solution(mesh):
    fits = mesh.shape["img"] == 4 and mesh.shape["ctx"] == 8
    return jax.shard_map(
        paired if fits else general,
        mesh=mesh,
        in_specs=(
            P("ctx", None),
            P(),
            P("ctx", "img"),
            P("ctx", None),
            P("img", "ctx"),
            P(),
            P(),
            P(),
            P("img", "ctx", None),
            P("ctx"),
            P(),
            P(),
        ),
        out_specs=P("ctx", "img"),
        check_vma=False,
    )
```

```python
import jax
import jax.numpy as jnp
from jax import lax
from jax.experimental import pallas as pl
from jax.experimental.pallas import tpu as pltpu
from jax.sharding import PartitionSpec as P

KVH = 8


EPS = 1e-05
NEG = -1e30


def head_norm(values, gain):
    mean_sq = jnp.mean(values * values, axis=-1, keepdims=True)
    return values * lax.rsqrt(mean_sq + EPS) * gain


def attend(query, keys, values, mask):
    scale = query.shape[-1] ** (-0.5)
    scores = jnp.einsum("tkgd,nkd->tkgn", query, keys, preferred_element_type=jnp.float32) * scale
    live = mask[:, None, None, :]
    scores = jnp.where(live, scores, NEG)
    top = jnp.max(scores, axis=-1)
    weights = jnp.where(live, jnp.exp(scores - top[..., None]), 0.0)
    total = jnp.sum(weights, axis=-1)
    acc = jnp.einsum(
        "tkgn,nkd->tkgd", weights.astype(jnp.bfloat16), values, preferred_element_type=jnp.float32
    )
    return acc / total[..., None]


def general(
    text,
    input_gain,
    q_weight,
    kv_weight,
    o_weight,
    q_gain,
    k_gain,
    attn_gate,
    vision,
    segment_ids,
    seg_images,
    image_slot,
):
    tokens_here = text.shape[0]
    head_dim = q_gain.shape[0]
    ctx_count = lax.axis_size("ctx")
    img_count = lax.axis_size("img")
    heads_here = q_weight.shape[1] // head_dim
    kv_heads = max(1, KVH // img_count)
    group = heads_here // kv_heads
    slots_here, vt_dev = vision.shape[:2]
    rows_here = slots_here * vt_dev

    o_full = lax.all_gather(o_weight, "ctx", axis=1, tiled=True)
    vision_cols = lax.all_to_all(
        vision.reshape(rows_here, -1), "ctx", split_axis=1, concat_axis=0, tiled=True
    )
    hidden = head_norm(text.astype(jnp.float32), input_gain).astype(jnp.bfloat16)
    hidden_cols = lax.all_to_all(hidden, "ctx", split_axis=1, concat_axis=0, tiled=True)

    kv_share = jnp.dot(vision_cols, kv_weight, preferred_element_type=jnp.float32)
    kv_shares = lax.all_to_all(
        kv_share.reshape(ctx_count, rows_here, -1), "ctx", split_axis=0, concat_axis=0, tiled=True
    )
    projected = jnp.sum(kv_shares, axis=0).reshape(rows_here, KVH, 2, head_dim)
    keys = head_norm(projected[:, :, 0], k_gain).astype(jnp.bfloat16)
    values = projected[:, :, 1].astype(jnp.bfloat16)
    kv_rows = jnp.stack((keys, values), axis=2)
    owners = jnp.arange(img_count)[:, None] * KVH // img_count + jnp.arange(kv_heads)[None, :]
    kv_out = jnp.take(kv_rows, owners, axis=1).transpose(1, 0, 2, 3, 4)
    kv_in = lax.all_to_all(kv_out, "img", split_axis=0, concat_axis=0, tiled=True)
    kv_all = lax.all_gather(kv_in, "ctx", axis=0, tiled=False)

    q_share = jnp.dot(hidden_cols, q_weight, preferred_element_type=jnp.float32)
    q_shares = lax.all_to_all(
        q_share.astype(jnp.bfloat16).reshape(ctx_count, tokens_here, -1),
        "ctx",
        split_axis=0,
        concat_axis=0,
        tiled=True,
    )
    query = jnp.sum(q_shares.astype(jnp.float32), axis=0)
    query = head_norm(query.reshape(tokens_here, kv_heads, group, head_dim), q_gain).astype(
        jnp.bfloat16
    )

    slots = img_count * slots_here
    own_slots = jnp.take(image_slot, jnp.take(seg_images, segment_ids, axis=0), axis=0)
    slot_ids = jnp.arange(slots, dtype=jnp.int32)
    sees = jnp.any(own_slots[:, :, None] == slot_ids[None, None, :], axis=1)
    flat = kv_all.reshape(ctx_count * slots * vt_dev, kv_heads, 2, head_dim)
    mask = jnp.broadcast_to(
        sees[:, None, :, None], (tokens_here, ctx_count, slots, vt_dev)
    ).reshape(tokens_here, -1)
    context = attend(query, flat[:, :, 0], flat[:, :, 1], mask)
    context = context.astype(jnp.bfloat16).reshape(tokens_here, heads_here * head_dim)
    partial_terms = jnp.dot(context, o_full, preferred_element_type=jnp.float32)
    width = partial_terms.shape[1] // img_count
    shares = lax.all_to_all(
        partial_terms.astype(jnp.bfloat16).reshape(tokens_here, img_count, width),
        "img",
        split_axis=1,
        concat_axis=1,
        tiled=True,
    )
    update = jnp.sum(shares.astype(jnp.float32), axis=1)
    own_text = lax.dynamic_slice_in_dim(text, lax.axis_index("img") * width, width, 1)
    return (own_text.astype(jnp.float32) + jnp.tanh(attn_gate[0]) * update).astype(jnp.bfloat16)


BF16, F32 = jnp.bfloat16, jnp.float32
SMEM = pl.BlockSpec(memory_space=pltpu.SMEM)
VMEM = pl.BlockSpec(memory_space=pltpu.VMEM)
CHIPS = 4


def call(kernel, args, specs, outs, out_specs=None, scratch=(), flops=0, size=0, name=None, grid=()):
    return pl.pallas_call(
        kernel,
        out_shape=outs,
        in_specs=specs,
        out_specs=[VMEM] * len(outs) if out_specs is None else out_specs,
        scratch_shapes=scratch,
        grid=grid,
        compiler_params=pltpu.CompilerParams(vmem_limit_bytes=24 * 2**20),
        cost_estimate=pl.CostEstimate(flops=flops, bytes_accessed=size, transcendentals=0),
        name=name,
    )(*args)


def block(index, size):
    return pl.ds(pl.multiple_of(index * size, size), size)


def vis_far_kernel(where, vis, out):
    out[...] = vis[:, block(1 - where[0] // 2, out.shape[1])]


def vis_side_kernel(where, vis, landed, keep, give):
    chip = where[0]
    part = keep.shape[1]
    rows = vis.shape[0]
    side = lax.rem(chip, 2)
    keep[:rows, :] = vis[:, block(chip, part)]
    give[:rows, :] = vis[:, block(chip ^ 1, part)]
    keep[rows:, :] = landed[:, block(side, part)]
    give[rows:, :] = landed[:, block(1 - side, part)]


def spread_kernel(where, text, gain, near, far, text_keep, text_give, scale):
    chip, core, plane = where[0], where[1], where[2]
    tokens, width = text.shape
    part = width // 2
    half = text_keep.shape[1]
    line = chip // 2
    step = 16
    for r in range(0, tokens, step):
        x = text[r : r + step, :].astype(F32)
        mean_sq = jnp.mean(x * x, axis=-1, keepdims=True)
        scale[r : r + step, :] = jnp.broadcast_to(lax.rsqrt(mean_sq + EPS), (step, 128))
    for out, index in ((far, 1 - line), (near, line)):
        cols = block(index, part)
        row_gain = gain[:, cols]
        for r in range(0, tokens, step):
            x = text[r : r + step, cols].astype(F32)
            out[r : r + step, :] = (x * scale[r : r + step, 0:1] * row_gain).astype(BF16)
    text_keep[...] = text[:, block(2 * plane + core, half)]
    text_give[...] = text[:, block(2 * plane + 1 - core, half)]


def cut_q_kernel(where, q_own, keep, give):
    core = where[1]
    half = keep.shape[1]
    keep[...] = q_own[:, block(core, half)]
    give[...] = q_own[:, block(1 - core, half)]


def kv_kernel(where, vis, vis_other, kv_own, kv_other, keep, give):
    core = where[1]
    rows = kv_own.shape[0]
    head = kv_other.shape[1] // (2 * CHIPS)
    near, far = block(core, rows), block(1 - core, rows)
    x_near = jnp.concatenate((vis[:, near], vis_other[:, near]), axis=0)
    x_far = jnp.concatenate((vis[:, far], vis_other[:, far]), axis=0)
    count = vis.shape[0] // CHIPS
    for j in range(CHIPS):
        cols = slice(j * head, (j + 1) * head)
        heads = block(2 * j + core, head)
        out = jnp.dot(x_near, kv_own[:, heads], preferred_element_type=F32)
        out += jnp.dot(x_far, kv_other[:, heads], preferred_element_type=F32)
        for k, ref in enumerate((keep, give, keep, give) * 2):
            row = (k // 2) * count
            ref[row : row + count, cols] = out[k * count : (k + 1) * count]


def kv_side_kernel(own, landed, give):
    count = own.shape[0] // CHIPS
    for k in range(2):
        rows = slice((2 * k + 1) * count, (2 * k + 2) * count)
        give[k * count : (k + 1) * count, :] = own[rows, :] + landed[rows, :]


def kv_norm_kernel(where, k_gain, own, landed, side, here, there, give):
    plane = where[2]
    count = own.shape[0] // CHIPS
    lines, head = here.shape
    dim = head // 2
    for t, (out, row) in enumerate(((here, 0), (give, 0), (there, 0), (give, lines))):
        cols = block(plane ^ t, head)
        for k in range(2):
            rows = slice(2 * k * count, (2 * k + 1) * count)
            line = slice(k * count, (k + 1) * count)
            total = (own[rows, cols] + landed[rows, cols]) + side[line, cols]
            keys = head_norm(total[:, :dim], k_gain[...])
            to = slice(row + k * count, row + (k + 1) * count)
            out[to, :dim] = keys.astype(BF16)
            out[to, dim:] = total[:, dim:].astype(BF16)


def kv_turn_kernel(there, landed, out):
    lines = there.shape[0]
    out[:lines, :] = there[...]
    out[lines:, :] = landed[lines:, :]


def kv_join_kernel(here, landed, last, out):
    lines = here.shape[0]
    out[:lines, :] = here[...]
    out[lines : 2 * lines, :] = landed[:lines, :]
    out[2 * lines :, :] = last[...]


def query_share(index, own, other, first, second, flip):
    rows = first.shape[0]
    total = None
    for weight, k in ((first, index), (second, index ^ flip)):
        cols = block(k, rows)
        x = jnp.concatenate((own[:, cols], other[:, cols]), axis=0)
        share = jnp.dot(x, weight[...], preferred_element_type=F32)
        total = share if total is None else total + share
    return total


def early_kernel(where, own, other, q_keep, q_other, out):
    index = 2 * lax.rem(where[0], 2) + where[1]
    out[...] = query_share(index, own, other, q_keep, q_other, 1)


def late_kernel(where, own, other, q_side, q_corner, early, *refs):
    out = refs[-1]
    rows = early.shape[0]
    index = (2 * lax.rem(where[0], 2) + where[1]) ^ 2
    share = early[...] + query_share(index, own, other, q_side, q_corner, 1)
    out[:rows, :] = share.astype(out.dtype)
    for k, kv in enumerate(refs[:-1]):
        out[rows:, k * kv.shape[1] : (k + 1) * kv.shape[1]] = kv[...]


def attend_kernel(q_gain, first, kv_first, kv_side, landed, bias, context):
    dim = q_gain.shape[1]
    rows, half = context.shape
    head = 2 * dim
    kv = [kv_first[...], kv_side[...]]
    kv += [landed[rows:, k * head : (k + 1) * head] for k in range(half // head)]
    keys = jnp.concatenate([x[:, :dim] for x in kv], axis=0)
    values = jnp.concatenate([x[:, dim:] for x in kv], axis=0)
    step = 128
    for r in range(0, rows, step):
        for g in range(half // dim):
            cols = slice(g * dim, (g + 1) * dim)
            query = first[r : r + step, cols] + landed[r : r + step, cols].astype(F32)
            query = head_norm(query, q_gain[...]).astype(BF16)
            scores = lax.dot_general(
                query, keys, (((1,), (1,)), ((), ())), preferred_element_type=F32
            )
            scores = scores * dim ** (-0.5) + bias[r : r + step, :]
            weights = jnp.exp(scores - jnp.max(scores, axis=-1, keepdims=True))
            total = jnp.sum(weights, axis=-1, keepdims=True)
            acc = jnp.dot(weights.astype(BF16), values, preferred_element_type=F32)
            context[r : r + step, cols] = (acc / total).astype(BF16)


def out_kernel(where, near, far, o_own, o_early, o_late, own, other):
    core = where[1]
    tokens, width = own.shape
    half = near.shape[1]
    turned = jnp.concatenate((far[tokens:, :], far[:tokens, :]), axis=0)
    share = jnp.dot(near[...], o_own[block(core, half), :], preferred_element_type=F32)
    share += jnp.dot(turned, o_own[block(1 - core, half), :], preferred_element_type=F32)
    own[:, : width // 2] = share[:tokens].astype(BF16)
    other[:, : width // 2] = share[tokens:].astype(BF16)
    top = jnp.where(core == 0, near[...], turned)
    low = jnp.where(core == 0, turned, near[...])
    first = o_early.shape[0]
    share = jnp.dot(top[:, :first], o_early[...], preferred_element_type=F32)
    share += jnp.dot(top[:, first:], o_late[: half - first, :], preferred_element_type=F32)
    share += jnp.dot(low, o_late[half - first :, :], preferred_element_type=F32)
    own[:, width // 2 :] = share[:tokens].astype(BF16)
    other[:, width // 2 :] = share[tokens:].astype(BF16)


def pick_kernel(where, own, landed, *outs):
    first = where[0] ^ where[2]
    half = outs[0].shape[1]
    for t in range(CHIPS):
        for s in range(CHIPS):

            @pl.when((first ^ t) == s)
            def _():
                outs[t][...] = (own, landed)[s // 2][:, (s % 2) * half : (s % 2 + 1) * half]


def mixed_rows(gate, text, shares):
    x = [share[...].astype(F32) for share in shares]
    update = (x[0] + x[1]) + (x[2] + x[3])
    return (text[...].astype(F32) + gate[0] * update).astype(BF16)


def give_kernel(gate, text, *refs):
    refs[CHIPS][...] = mixed_rows(gate, text, refs[:CHIPS])


def last_kernel(where, gate, text, back, *refs):
    shares, out = refs[:CHIPS], refs[CHIPS]
    core = where[1]
    half = text.shape[1]
    out[:, block(core, half)] = mixed_rows(gate, text, shares)
    out[:, block(1 - core, half)] = back[...]


def paired(
    text,
    input_gain,
    q_weight,
    kv_weight,
    o_weight,
    q_gain,
    k_gain,
    attn_gate,
    vision,
    segment_ids,
    seg_images,
    image_slot,
):
    ctx_count = lax.axis_size("ctx")
    place, plane = lax.axis_index("ctx"), lax.axis_index("img")
    chip, core = place // 2, place % 2
    where = jnp.stack((chip, core, plane)).astype(jnp.int32)
    tokens, width = text.shape
    head_dim = q_gain.shape[0]
    rows_dev, cols_plane = q_weight.shape
    half = cols_plane // 2
    part = 2 * rows_dev
    slots_here, vt_dev = vision.shape[:2]
    vis_here = slots_here * vt_dev
    kv_cols = kv_weight.shape[1] // 2

    def shape(rows, cols, kind=BF16):
        return jax.ShapeDtypeStruct((rows, cols), kind)

    def swap(x):
        return lax.ppermute(x, "ctx", [(k, k ^ 1) for k in range(ctx_count)])

    def along_x(x):
        return lax.ppermute(x, "ctx", [(k, k ^ 2) for k in range(ctx_count)])

    def along_y(x):
        return lax.ppermute(x, "ctx", [(k, k ^ 4) for k in range(ctx_count)])

    def across(x, t):
        return lax.ppermute(x, "img", [(k, k ^ t) for k in range(CHIPS)])

    steps = range(1, CHIPS)
    vis = vision.reshape(vis_here, width)
    kv_other = swap(kv_weight)

    q_keep, q_give = call(
        cut_q_kernel, (where, q_weight), [SMEM, VMEM], [shape(rows_dev, half)] * 2, name="cut_q"
    )
    q_side, q_other = along_x(q_keep), swap(q_give)

    vis_far = call(
        vis_far_kernel, (where, vis), [SMEM, VMEM], [shape(vis_here, width // 2)], name="vis_far"
    )[0]
    vis_y = along_y(vis_far)
    vis_keep, vis_give = call(
        vis_side_kernel,
        (where, vis, vis_y),
        [SMEM, VMEM, VMEM],
        [shape(2 * vis_here, part)] * 2,
        name="vis_side",
    )
    vis_own = jnp.concatenate((vis_keep, along_x(vis_give)))
    vis_own, q_side = lax.optimization_barrier((vis_own, q_side))
    vis_other = swap(vis_own)

    near, far, text_keep, text_give = call(
        spread_kernel,
        (where, text, input_gain[None]),
        [SMEM] + [VMEM] * 2,
        [shape(tokens, width // 2)] * 2 + [shape(tokens, half)] * 2,
        scratch=[pltpu.VMEM((tokens, 128), F32)],
        flops=8 * tokens * width,
        size=4 * 2**20,
        name="spread",
    )
    kv_keep, kv_far = call(
        kv_kernel,
        (where, vis_own, vis_other, kv_weight, kv_other),
        [SMEM] + [VMEM] * 4,
        [shape(4 * vis_here, kv_cols, F32)] * 2,
        flops=4 * vis_here * ctx_count * part * kv_cols,
        size=4 * 2**20,
        name="kv_shares",
    )
    far, _ = lax.optimization_barrier((far, vis_y))
    kv_far, far = lax.optimization_barrier((kv_far, along_y(far)))
    kv_y = along_y(kv_far)
    q_behind, _ = lax.optimization_barrier((q_other, vis_own))
    q_corner = along_x(q_behind)
    kv_y, q_corner = lax.optimization_barrier((kv_y, q_corner))
    kv_give = call(
        kv_side_kernel,
        (kv_keep, kv_y),
        [VMEM] * 2,
        [shape(2 * vis_here, kv_cols, F32)],
        name="kv_side",
    )[0]
    kv_x = along_x(kv_give)
    here, there, give = call(
        kv_norm_kernel,
        (where, k_gain[None], kv_keep, kv_y, kv_x),
        [SMEM] + [VMEM] * 4,
        [shape(2 * vis_here, 2 * head_dim)] * 2 + [shape(4 * vis_here, 2 * head_dim)],
        name="kv_norm",
    )
    kv_z = across(give, 1)
    turn = call(
        kv_turn_kernel,
        (there, kv_z),
        [VMEM] * 2,
        [shape(4 * vis_here, 2 * head_dim)],
        name="kv_turn",
    )[0]
    o_early, _ = lax.optimization_barrier((o_weight[: half // 2], kv_x))
    kv_far_z, o_early = lax.optimization_barrier((across(turn, 2), along_x(o_early)))
    kv_first = call(
        kv_join_kernel,
        (here, kv_z, kv_far_z),
        [VMEM] * 3,
        [shape(8 * vis_here, 2 * head_dim)],
        name="kv_join",
    )[0]
    kv_side = along_x(kv_first)

    blocks = ((far, swap(far)), (near, swap(near)))
    early = [
        call(
            early_kernel,
            (where, *pair, q_keep, q_other),
            [SMEM] + [VMEM] * 4,
            [shape(2 * tokens, half, F32)],
            flops=4 * tokens * part * half,
            size=2 * 2**20,
            name="q_early",
        )[0]
        for pair in blocks
    ]
    kv_lines = kv_first.shape[0] * kv_first.shape[1] * 2 // half
    landed = along_y(
        call(
            late_kernel,
            (where, *blocks[0], q_side, q_corner, early[0], kv_first, kv_side),
            [SMEM] + [VMEM] * 7,
            [shape(2 * tokens + kv_lines, half)],
            flops=4 * tokens * part * half,
            size=2 * 2**20,
            name="q_far",
        )[0]
    )
    q_first = call(
        late_kernel,
        (where, *blocks[1], q_side, q_corner, early[1]),
        [SMEM] + [VMEM] * 5,
        [shape(2 * tokens, half, F32)],
        flops=4 * tokens * part * half,
        size=2 * 2**20,
        name="q_near",
    )[0]
    o_late, _ = lax.optimization_barrier((o_weight[half // 2 :], kv_side))
    o_late = along_x(o_late)

    ids = jnp.concatenate((segment_ids, swap(segment_ids)))
    images = jnp.arange(image_slot.shape[0])
    slot_of = jnp.sum(
        jnp.where(seg_images[:, :, None] == images, image_slot[None, None, :], 0), axis=2
    )
    numbers = jnp.arange(seg_images.shape[0])
    own_slots = jnp.sum(
        jnp.where((ids[:, None] == numbers)[:, :, None], slot_of[None], 0), axis=1
    )
    key_rows = jnp.arange(CHIPS * CHIPS * 2 * vis_here)
    key_plane = plane ^ (key_rows // (2 * vis_here) % CHIPS)
    key_slot = key_plane * slots_here + key_rows // vt_dev % slots_here
    sees = jnp.any(own_slots[:, :, None] == key_slot, axis=1)
    bias = jnp.where(sees, 0.0, NEG).astype(F32)

    context = call(
        attend_kernel,
        (q_gain[None], q_first, kv_first, kv_side, landed, bias),
        [VMEM] * 6,
        [shape(2 * tokens, half)],
        flops=8 * tokens * half * bias.shape[1],
        size=2 * 2**20,
        name="attend",
    )[0]

    context_y = along_y(context)
    shares = [
        call(
            out_kernel,
            (where, x, swap(x), o_weight, o_early, o_late),
            [SMEM] + [VMEM] * 5,
            [shape(tokens, 2 * half)] * 2,
            flops=8 * tokens * cols_plane * half,
            size=2 * 2**20,
            name="o_share",
        )
        for x in (context_y, context)
    ]
    summands = []
    for rows in (1, 0):
        picked = call(
            pick_kernel,
            (where, shares[1][rows], along_y(shares[0][rows])),
            [SMEM] + [VMEM] * 2,
            [shape(tokens, half)] * CHIPS,
            flops=2**20,
            size=2**20,
            name="pick",
        )
        summands.append([picked[0]] + [across(picked[t], t) for t in steps])
    gate = jnp.tanh(attn_gate)
    give = call(
        give_kernel,
        (gate, swap(text_give), *summands[0]),
        [SMEM] + [VMEM] * (1 + CHIPS),
        [shape(tokens, half)],
        flops=2**20,
        size=2**20,
        name="mix_give",
    )[0]
    return call(
        last_kernel,
        (where, gate, text_keep, swap(give), *summands[1]),
        [SMEM, SMEM] + [VMEM] * (2 + CHIPS),
        [shape(tokens, 2 * half)],
        flops=2**20,
        size=2**20,
        name="mix_keep",
    )[0]


def solution(mesh):
    fits = mesh.shape["img"] == 4 and mesh.shape["ctx"] == 8
    return jax.shard_map(
        paired if fits else general,
        mesh=mesh,
        in_specs=(
            P("ctx", None),
            P(),
            P("ctx", "img"),
            P("ctx", None),
            P("img", "ctx"),
            P(),
            P(),
            P(),
            P("img", "ctx", None),
            P("ctx"),
            P(),
            P(),
        ),
        out_specs=P("ctx", "img"),
        check_vma=False,
    )
```

```python
import jax
import jax.numpy as jnp
from jax import lax
from jax.experimental import pallas as pl
from jax.experimental.pallas import tpu as pltpu
from jax.sharding import PartitionSpec as P

KVH = 8


EPS = 1e-05
NEG = -1e30


def head_norm(values, gain):
    mean_sq = jnp.mean(values * values, axis=-1, keepdims=True)
    return values * lax.rsqrt(mean_sq + EPS) * gain


def attend(query, keys, values, mask):
    scale = query.shape[-1] ** (-0.5)
    scores = jnp.einsum("tkgd,nkd->tkgn", query, keys, preferred_element_type=jnp.float32) * scale
    live = mask[:, None, None, :]
    scores = jnp.where(live, scores, NEG)
    top = jnp.max(scores, axis=-1)
    weights = jnp.where(live, jnp.exp(scores - top[..., None]), 0.0)
    total = jnp.sum(weights, axis=-1)
    acc = jnp.einsum(
        "tkgn,nkd->tkgd", weights.astype(jnp.bfloat16), values, preferred_element_type=jnp.float32
    )
    return acc / total[..., None]


def general(
    text,
    input_gain,
    q_weight,
    kv_weight,
    o_weight,
    q_gain,
    k_gain,
    attn_gate,
    vision,
    segment_ids,
    seg_images,
    image_slot,
):
    tokens_here = text.shape[0]
    head_dim = q_gain.shape[0]
    ctx_count = lax.axis_size("ctx")
    img_count = lax.axis_size("img")
    heads_here = q_weight.shape[1] // head_dim
    kv_heads = max(1, KVH // img_count)
    group = heads_here // kv_heads
    slots_here, vt_dev = vision.shape[:2]
    rows_here = slots_here * vt_dev

    o_full = lax.all_gather(o_weight, "ctx", axis=1, tiled=True)
    vision_cols = lax.all_to_all(
        vision.reshape(rows_here, -1), "ctx", split_axis=1, concat_axis=0, tiled=True
    )
    hidden = head_norm(text.astype(jnp.float32), input_gain).astype(jnp.bfloat16)
    hidden_cols = lax.all_to_all(hidden, "ctx", split_axis=1, concat_axis=0, tiled=True)

    kv_share = jnp.dot(vision_cols, kv_weight, preferred_element_type=jnp.float32)
    kv_shares = lax.all_to_all(
        kv_share.reshape(ctx_count, rows_here, -1), "ctx", split_axis=0, concat_axis=0, tiled=True
    )
    projected = jnp.sum(kv_shares, axis=0).reshape(rows_here, KVH, 2, head_dim)
    keys = head_norm(projected[:, :, 0], k_gain).astype(jnp.bfloat16)
    values = projected[:, :, 1].astype(jnp.bfloat16)
    kv_rows = jnp.stack((keys, values), axis=2)
    owners = jnp.arange(img_count)[:, None] * KVH // img_count + jnp.arange(kv_heads)[None, :]
    kv_out = jnp.take(kv_rows, owners, axis=1).transpose(1, 0, 2, 3, 4)
    kv_in = lax.all_to_all(kv_out, "img", split_axis=0, concat_axis=0, tiled=True)
    kv_all = lax.all_gather(kv_in, "ctx", axis=0, tiled=False)

    q_share = jnp.dot(hidden_cols, q_weight, preferred_element_type=jnp.float32)
    q_shares = lax.all_to_all(
        q_share.astype(jnp.bfloat16).reshape(ctx_count, tokens_here, -1),
        "ctx",
        split_axis=0,
        concat_axis=0,
        tiled=True,
    )
    query = jnp.sum(q_shares.astype(jnp.float32), axis=0)
    query = head_norm(query.reshape(tokens_here, kv_heads, group, head_dim), q_gain).astype(
        jnp.bfloat16
    )

    slots = img_count * slots_here
    own_slots = jnp.take(image_slot, jnp.take(seg_images, segment_ids, axis=0), axis=0)
    slot_ids = jnp.arange(slots, dtype=jnp.int32)
    sees = jnp.any(own_slots[:, :, None] == slot_ids[None, None, :], axis=1)
    flat = kv_all.reshape(ctx_count * slots * vt_dev, kv_heads, 2, head_dim)
    mask = jnp.broadcast_to(
        sees[:, None, :, None], (tokens_here, ctx_count, slots, vt_dev)
    ).reshape(tokens_here, -1)
    context = attend(query, flat[:, :, 0], flat[:, :, 1], mask)
    context = context.astype(jnp.bfloat16).reshape(tokens_here, heads_here * head_dim)
    partial_terms = jnp.dot(context, o_full, preferred_element_type=jnp.float32)
    width = partial_terms.shape[1] // img_count
    shares = lax.all_to_all(
        partial_terms.astype(jnp.bfloat16).reshape(tokens_here, img_count, width),
        "img",
        split_axis=1,
        concat_axis=1,
        tiled=True,
    )
    update = jnp.sum(shares.astype(jnp.float32), axis=1)
    own_text = lax.dynamic_slice_in_dim(text, lax.axis_index("img") * width, width, 1)
    return (own_text.astype(jnp.float32) + jnp.tanh(attn_gate[0]) * update).astype(jnp.bfloat16)


BF16, F32 = jnp.bfloat16, jnp.float32
SMEM = pl.BlockSpec(memory_space=pltpu.SMEM)
VMEM = pl.BlockSpec(memory_space=pltpu.VMEM)
CHIPS = 4


def call(kernel, args, specs, outs, out_specs=None, scratch=(), flops=0, size=0, name=None, grid=()):
    return pl.pallas_call(
        kernel,
        out_shape=outs,
        in_specs=specs,
        out_specs=[VMEM] * len(outs) if out_specs is None else out_specs,
        scratch_shapes=scratch,
        grid=grid,
        compiler_params=pltpu.CompilerParams(vmem_limit_bytes=24 * 2**20),
        cost_estimate=pl.CostEstimate(flops=flops, bytes_accessed=size, transcendentals=0),
        name=name,
    )(*args)


def block(index, size):
    return pl.ds(pl.multiple_of(index * size, size), size)


def vis_kernel(where, vis, *pieces):
    for s in range(CHIPS):
        pieces[s][...] = vis[:, block(where[0] ^ s, pieces[s].shape[1])]


def spread_kernel(where, text, gain, near, far, text_keep, text_give, scale):
    chip, core, plane = where[0], where[1], where[2]
    tokens, width = text.shape
    part = width // 2
    half = text_keep.shape[1]
    line = chip // 2
    step = 16
    for r in range(0, tokens, step):
        x = text[r : r + step, :].astype(F32)
        mean_sq = jnp.mean(x * x, axis=-1, keepdims=True)
        scale[r : r + step, :] = jnp.broadcast_to(lax.rsqrt(mean_sq + EPS), (step, 128))
    for out, index in ((far, 1 - line), (near, line)):
        cols = block(index, part)
        row_gain = gain[:, cols]
        for r in range(0, tokens, step):
            x = text[r : r + step, cols].astype(F32)
            out[r : r + step, :] = (x * scale[r : r + step, 0:1] * row_gain).astype(BF16)
    text_keep[...] = text[:, block(2 * plane + core, half)]
    text_give[...] = text[:, block(2 * plane + 1 - core, half)]


def cut_q_kernel(where, q_own, keep, give):
    core = where[1]
    half = keep.shape[1]
    keep[...] = q_own[:, block(core, half)]
    give[...] = q_own[:, block(1 - core, half)]


def kv_kernel(where, vis, vis_other, kv_own, kv_other, *refs):
    shares, (other, near_total, sems) = refs[:CHIPS], refs[CHIPS:]
    core = where[1]
    rows = kv_own.shape[0]
    head = kv_own.shape[1] // (2 * CHIPS)
    copies = []
    for j in range(CHIPS):
        copies.append(
            pltpu.make_async_copy(
                kv_other.at[:, block(2 * j + core, head)],
                other.at[:, pl.ds(j * head, head)],
                sems.at[j],
            )
        )
        copies[-1].start()
    near, far = block(core, rows), block(1 - core, rows)
    x_near = jnp.concatenate((vis[:, near], vis_other[:, near]), axis=0)
    x_far = jnp.concatenate((vis[:, far], vis_other[:, far]), axis=0)
    total = vis.shape[0]
    count = total // CHIPS
    for j in range(CHIPS):
        near_total[:, j * head : (j + 1) * head] = jnp.dot(
            x_near, kv_own[:, block(2 * j + core, head)], preferred_element_type=F32
        )
    for j in range(CHIPS):
        copies[j].wait()
        cols = slice(j * head, (j + 1) * head)
        out = near_total[:, cols] + jnp.dot(x_far, other[:, cols], preferred_element_type=F32)
        for s in range(CHIPS):
            shares[s][:count, cols] = out[s * count : (s + 1) * count]
            shares[s][count:, cols] = out[total + s * count : total + (s + 1) * count]


def kv_norm_kernel(where, k_gain, *refs):
    shares, (here, there, give) = refs[:CHIPS], refs[CHIPS:]
    plane = where[2]
    lines, head = here.shape
    dim = head // 2
    for t, (out, row) in enumerate(((here, 0), (give, 0), (there, 0), (give, lines))):
        cols = block(plane ^ t, head)
        total = (shares[0][:, cols] + shares[1][:, cols]) + (shares[2][:, cols] + shares[3][:, cols])
        keys = head_norm(total[:, :dim], k_gain[...])
        out[row : row + lines, :dim] = keys.astype(BF16)
        out[row : row + lines, dim:] = total[:, dim:].astype(BF16)


def kv_turn_kernel(there, landed, out):
    lines = there.shape[0]
    out[:lines, :] = there[...]
    out[lines:, :] = landed[lines:, :]


def kv_join_kernel(here, landed, last, out):
    lines = here.shape[0]
    out[:lines, :] = here[...]
    out[lines : 2 * lines, :] = landed[:lines, :]
    out[2 * lines :, :] = last[...]


def query_share(index, own, other, first, second, flip):
    rows = first.shape[0]
    total = None
    for weight, k in ((first, index), (second, index ^ flip)):
        cols = block(k, rows)
        x = jnp.concatenate((own[:, cols], other[:, cols]), axis=0)
        share = jnp.dot(x, weight[...], preferred_element_type=F32)
        total = share if total is None else total + share
    return total


def early_kernel(where, own, other, q_keep, q_other, out):
    index = 2 * lax.rem(where[0], 2) + where[1]
    out[...] = query_share(index, own, other, q_keep, q_other, 1)


def late_kernel(where, own, other, q_side, q_corner, early, out):
    index = (2 * lax.rem(where[0], 2) + where[1]) ^ 2
    share = early[...] + query_share(index, own, other, q_side, q_corner, 1)
    out[...] = share.astype(out.dtype)


def attend_kernel(q_gain, first, landed, *refs):
    kv, (bias, context) = refs[:CHIPS], refs[CHIPS:]
    dim = q_gain.shape[1]
    rows, half = context.shape
    keys = jnp.concatenate([x[:, :dim] for x in kv], axis=0)
    values = jnp.concatenate([x[:, dim:] for x in kv], axis=0)
    step = 128
    for r in range(0, rows, step):
        for g in range(half // dim):
            cols = slice(g * dim, (g + 1) * dim)
            query = first[r : r + step, cols] + landed[r : r + step, cols].astype(F32)
            query = head_norm(query, q_gain[...]).astype(BF16)
            scores = lax.dot_general(
                query, keys, (((1,), (1,)), ((), ())), preferred_element_type=F32
            )
            scores = scores * dim ** (-0.5) + bias[r : r + step, :]
            weights = jnp.exp(scores - jnp.max(scores, axis=-1, keepdims=True))
            total = jnp.sum(weights, axis=-1, keepdims=True)
            acc = jnp.dot(weights.astype(BF16), values, preferred_element_type=F32)
            context[r : r + step, cols] = (acc / total).astype(BF16)


def out_kernel(where, near, far, o_own, o_early, o_late, own, other):
    core = where[1]
    tokens, width = own.shape
    half = near.shape[1]
    turned = jnp.concatenate((far[tokens:, :], far[:tokens, :]), axis=0)
    share = jnp.dot(near[...], o_own[block(core, half), :], preferred_element_type=F32)
    share += jnp.dot(turned, o_own[block(1 - core, half), :], preferred_element_type=F32)
    own[:, : width // 2] = share[:tokens].astype(BF16)
    other[:, : width // 2] = share[tokens:].astype(BF16)
    top = jnp.where(core == 0, near[...], turned)
    low = jnp.where(core == 0, turned, near[...])
    share = jnp.dot(top, o_early[...], preferred_element_type=F32)
    share += jnp.dot(low, o_late[...], preferred_element_type=F32)
    own[:, width // 2 :] = share[:tokens].astype(BF16)
    other[:, width // 2 :] = share[tokens:].astype(BF16)


def pick_kernel(where, own, landed, *outs):
    first = where[0] ^ where[2]
    half = outs[0].shape[1]
    for t in range(CHIPS):
        for s in range(CHIPS):

            @pl.when((first ^ t) == s)
            def _():
                outs[t][...] = (own, landed)[s % 2][:, (s // 2) * half : (s // 2 + 1) * half]


def mixed_rows(gate, text, shares):
    x = [share[...].astype(F32) for share in shares]
    update = (x[0] + x[1]) + (x[2] + x[3])
    return (text[...].astype(F32) + gate[0] * update).astype(BF16)


def give_kernel(gate, text, *refs):
    refs[CHIPS][...] = mixed_rows(gate, text, refs[:CHIPS])


def last_kernel(where, gate, text, back, *refs):
    shares, out = refs[:CHIPS], refs[CHIPS]
    core = where[1]
    half = text.shape[1]
    out[:, block(core, half)] = mixed_rows(gate, text, shares)
    out[:, block(1 - core, half)] = back[...]


def paired(
    text,
    input_gain,
    q_weight,
    kv_weight,
    o_weight,
    q_gain,
    k_gain,
    attn_gate,
    vision,
    segment_ids,
    seg_images,
    image_slot,
):
    ctx_count = lax.axis_size("ctx")
    place, plane = lax.axis_index("ctx"), lax.axis_index("img")
    chip, core = place // 2, place % 2
    where = jnp.stack((chip, core, plane)).astype(jnp.int32)
    tokens, width = text.shape
    head_dim = q_gain.shape[0]
    rows_dev, cols_plane = q_weight.shape
    half = cols_plane // 2
    part = 2 * rows_dev
    slots_here, vt_dev = vision.shape[:2]
    vis_here = slots_here * vt_dev
    kv_cols = kv_weight.shape[1] // 2

    def shape(rows, cols, kind=BF16):
        return jax.ShapeDtypeStruct((rows, cols), kind)

    def swap(x):
        return lax.ppermute(x, "ctx", [(k, k ^ 1) for k in range(ctx_count)])

    def peer(x, s):
        return lax.ppermute(x, "ctx", [(k, k ^ (2 * s)) for k in range(ctx_count)])

    def along_x(x):
        return peer(x, 1)

    def along_y(x):
        return peer(x, 2)

    def across(x, t):
        return lax.ppermute(x, "img", [(k, k ^ t) for k in range(CHIPS)])

    steps = range(1, CHIPS)
    vis = vision.reshape(vis_here, width)
    kv_other = swap(kv_weight)

    vis_pieces = call(
        vis_kernel, (where, vis), [SMEM, VMEM], [shape(vis_here, part)] * CHIPS, name="vis"
    )
    vis_own = jnp.concatenate([vis_pieces[0]] + [peer(vis_pieces[s], s) for s in steps])
    vis_other = swap(vis_own)

    where_cut, _ = lax.optimization_barrier((where, vis_pieces[0]))
    q_keep, q_give = call(
        cut_q_kernel, (where_cut, q_weight), [SMEM, VMEM], [shape(rows_dev, half)] * 2, name="cut_q"
    )
    q_side, q_other = along_x(q_keep), swap(q_give)

    near, far, text_keep, text_give = call(
        spread_kernel,
        (where, text, input_gain[None]),
        [SMEM] + [VMEM] * 2,
        [shape(tokens, width // 2)] * 2 + [shape(tokens, half)] * 2,
        scratch=[pltpu.VMEM((tokens, 128), F32)],
        flops=8 * tokens * width,
        size=4 * 2**20,
        name="spread",
    )
    far, _ = lax.optimization_barrier((far, vis_own))
    far = along_y(far)

    shares = call(
        kv_kernel,
        (where, vis_own, vis_other, kv_weight, kv_other),
        [SMEM] + [VMEM] * 3 + [pl.BlockSpec(memory_space=pl.ANY)],
        [shape(2 * vis_here, kv_cols, F32)] * CHIPS,
        scratch=[
            pltpu.VMEM((rows_dev, kv_cols), BF16),
            pltpu.VMEM((8 * vis_here, kv_cols), F32),
            pltpu.SemaphoreType.DMA((CHIPS,)),
        ],
        flops=4 * vis_here * ctx_count * part * kv_cols,
        size=4 * 2**20,
        name="kv_shares",
    )
    shares = [shares[0]] + [peer(shares[s], s) for s in steps]
    shares[3], q_side, far = lax.optimization_barrier((shares[3], q_side, far))
    here, there, give = call(
        kv_norm_kernel,
        (where, k_gain[None], *shares),
        [SMEM] + [VMEM] * (1 + CHIPS),
        [shape(2 * vis_here, 2 * head_dim)] * 2 + [shape(4 * vis_here, 2 * head_dim)],
        name="kv_norm",
    )
    kv_z = across(give, 1)
    turn = call(
        kv_turn_kernel,
        (there, kv_z),
        [VMEM] * 2,
        [shape(4 * vis_here, 2 * head_dim)],
        name="kv_turn",
    )[0]
    kv_first = call(
        kv_join_kernel,
        (here, kv_z, across(turn, 2)),
        [VMEM] * 3,
        [shape(8 * vis_here, 2 * head_dim)],
        name="kv_join",
    )[0]
    q_behind, _ = lax.optimization_barrier((q_other, shares[0]))
    q_corner = along_x(q_behind)
    kv_first, q_corner = lax.optimization_barrier((kv_first, q_corner))
    kv_all = [kv_first] + [peer(kv_first, s) for s in steps]

    blocks = ((far, swap(far)), (near, swap(near)))
    early = [
        call(
            early_kernel,
            (where, *pair, q_keep, q_other),
            [SMEM] + [VMEM] * 4,
            [shape(2 * tokens, half, F32)],
            flops=4 * tokens * part * half,
            size=2 * 2**20,
            name="q_early",
        )[0]
        for pair in blocks
    ]
    o_early, _ = lax.optimization_barrier((o_weight[:half], here))
    q_corner, o_early = lax.optimization_barrier((q_corner, along_y(o_early)))
    q_far, q_first = [
        call(
            late_kernel,
            (where, *blocks[k], q_side, q_corner, early[k]),
            [SMEM] + [VMEM] * 5,
            [shape(2 * tokens, half, kind)],
            flops=4 * tokens * part * half,
            size=2 * 2**20,
            name="q_late",
        )[0]
        for k, kind in ((0, BF16), (1, F32))
    ]
    landed = along_y(q_far)
    o_late, _ = lax.optimization_barrier((o_weight[half:], q_far))
    o_late = along_y(o_late)

    ids = jnp.concatenate((segment_ids, swap(segment_ids)))
    images = jnp.arange(image_slot.shape[0])
    slot_of = jnp.sum(
        jnp.where(seg_images[:, :, None] == images, image_slot[None, None, :], 0), axis=2
    )
    numbers = jnp.arange(seg_images.shape[0])
    own_slots = jnp.sum(
        jnp.where((ids[:, None] == numbers)[:, :, None], slot_of[None], 0), axis=1
    )
    key_rows = jnp.arange(CHIPS * CHIPS * 2 * vis_here)
    key_plane = plane ^ (key_rows // (2 * vis_here) % CHIPS)
    key_slot = key_plane * slots_here + key_rows // vt_dev % slots_here
    sees = jnp.any(own_slots[:, :, None] == key_slot, axis=1)
    bias = jnp.where(sees, 0.0, NEG).astype(F32)

    context = call(
        attend_kernel,
        (q_gain[None], q_first, landed, *kv_all, bias),
        [VMEM] * (4 + CHIPS),
        [shape(2 * tokens, half)],
        flops=8 * tokens * half * bias.shape[1],
        size=2 * 2**20,
        name="attend",
    )[0]

    context_x = along_x(context)
    shares = [
        call(
            out_kernel,
            (where, x, swap(x), o_weight, o_early, o_late),
            [SMEM] + [VMEM] * 5,
            [shape(tokens, 2 * half)] * 2,
            flops=8 * tokens * cols_plane * half,
            size=2 * 2**20,
            name="o_share",
        )
        for x in (context_x, context)
    ]
    summands = []
    for rows in (1, 0):
        picked = call(
            pick_kernel,
            (where, shares[1][rows], along_x(shares[0][rows])),
            [SMEM] + [VMEM] * 2,
            [shape(tokens, half)] * CHIPS,
            flops=2**20,
            size=2**20,
            name="pick",
        )
        summands.append([picked[0]] + [across(picked[t], t) for t in steps])
    gate = jnp.tanh(attn_gate)
    give = call(
        give_kernel,
        (gate, swap(text_give), *summands[0]),
        [SMEM] + [VMEM] * (1 + CHIPS),
        [shape(tokens, half)],
        flops=2**20,
        size=2**20,
        name="mix_give",
    )[0]
    return call(
        last_kernel,
        (where, gate, text_keep, swap(give), *summands[1]),
        [SMEM, SMEM] + [VMEM] * (2 + CHIPS),
        [shape(tokens, 2 * half)],
        flops=2**20,
        size=2**20,
        name="mix_keep",
    )[0]


def solution(mesh):
    fits = mesh.shape["img"] == 4 and mesh.shape["ctx"] == 8
    return jax.shard_map(
        paired if fits else general,
        mesh=mesh,
        in_specs=(
            P("ctx", None),
            P(),
            P("ctx", "img"),
            P("ctx", None),
            P("img", "ctx"),
            P(),
            P(),
            P(),
            P("img", "ctx", None),
            P("ctx"),
            P(),
            P(),
        ),
        out_specs=P("ctx", "img"),
        check_vma=False,
    )
```

```python
import jax
import jax.numpy as jnp
from jax import lax
from jax.experimental import pallas as pl
from jax.experimental.pallas import tpu as pltpu
from jax.sharding import PartitionSpec as P

KVH = 8


EPS = 1e-05
NEG = -1e30


def head_norm(values, gain):
    mean_sq = jnp.mean(values * values, axis=-1, keepdims=True)
    return values * lax.rsqrt(mean_sq + EPS) * gain


def attend(query, keys, values, mask):
    scale = query.shape[-1] ** (-0.5)
    scores = jnp.einsum("tkgd,nkd->tkgn", query, keys, preferred_element_type=jnp.float32) * scale
    live = mask[:, None, None, :]
    scores = jnp.where(live, scores, NEG)
    top = jnp.max(scores, axis=-1)
    weights = jnp.where(live, jnp.exp(scores - top[..., None]), 0.0)
    total = jnp.sum(weights, axis=-1)
    acc = jnp.einsum(
        "tkgn,nkd->tkgd", weights.astype(jnp.bfloat16), values, preferred_element_type=jnp.float32
    )
    return acc / total[..., None]


def general(
    text,
    input_gain,
    q_weight,
    kv_weight,
    o_weight,
    q_gain,
    k_gain,
    attn_gate,
    vision,
    segment_ids,
    seg_images,
    image_slot,
):
    tokens_here = text.shape[0]
    head_dim = q_gain.shape[0]
    ctx_count = lax.axis_size("ctx")
    img_count = lax.axis_size("img")
    heads_here = q_weight.shape[1] // head_dim
    kv_heads = max(1, KVH // img_count)
    group = heads_here // kv_heads
    slots_here, vt_dev = vision.shape[:2]
    rows_here = slots_here * vt_dev

    o_full = lax.all_gather(o_weight, "ctx", axis=1, tiled=True)
    vision_cols = lax.all_to_all(
        vision.reshape(rows_here, -1), "ctx", split_axis=1, concat_axis=0, tiled=True
    )
    hidden = head_norm(text.astype(jnp.float32), input_gain).astype(jnp.bfloat16)
    hidden_cols = lax.all_to_all(hidden, "ctx", split_axis=1, concat_axis=0, tiled=True)

    kv_share = jnp.dot(vision_cols, kv_weight, preferred_element_type=jnp.float32)
    kv_shares = lax.all_to_all(
        kv_share.reshape(ctx_count, rows_here, -1), "ctx", split_axis=0, concat_axis=0, tiled=True
    )
    projected = jnp.sum(kv_shares, axis=0).reshape(rows_here, KVH, 2, head_dim)
    keys = head_norm(projected[:, :, 0], k_gain).astype(jnp.bfloat16)
    values = projected[:, :, 1].astype(jnp.bfloat16)
    kv_rows = jnp.stack((keys, values), axis=2)
    owners = jnp.arange(img_count)[:, None] * KVH // img_count + jnp.arange(kv_heads)[None, :]
    kv_out = jnp.take(kv_rows, owners, axis=1).transpose(1, 0, 2, 3, 4)
    kv_in = lax.all_to_all(kv_out, "img", split_axis=0, concat_axis=0, tiled=True)
    kv_all = lax.all_gather(kv_in, "ctx", axis=0, tiled=False)

    q_share = jnp.dot(hidden_cols, q_weight, preferred_element_type=jnp.float32)
    q_shares = lax.all_to_all(
        q_share.astype(jnp.bfloat16).reshape(ctx_count, tokens_here, -1),
        "ctx",
        split_axis=0,
        concat_axis=0,
        tiled=True,
    )
    query = jnp.sum(q_shares.astype(jnp.float32), axis=0)
    query = head_norm(query.reshape(tokens_here, kv_heads, group, head_dim), q_gain).astype(
        jnp.bfloat16
    )

    slots = img_count * slots_here
    own_slots = jnp.take(image_slot, jnp.take(seg_images, segment_ids, axis=0), axis=0)
    slot_ids = jnp.arange(slots, dtype=jnp.int32)
    sees = jnp.any(own_slots[:, :, None] == slot_ids[None, None, :], axis=1)
    flat = kv_all.reshape(ctx_count * slots * vt_dev, kv_heads, 2, head_dim)
    mask = jnp.broadcast_to(
        sees[:, None, :, None], (tokens_here, ctx_count, slots, vt_dev)
    ).reshape(tokens_here, -1)
    context = attend(query, flat[:, :, 0], flat[:, :, 1], mask)
    context = context.astype(jnp.bfloat16).reshape(tokens_here, heads_here * head_dim)
    partial_terms = jnp.dot(context, o_full, preferred_element_type=jnp.float32)
    width = partial_terms.shape[1] // img_count
    shares = lax.all_to_all(
        partial_terms.astype(jnp.bfloat16).reshape(tokens_here, img_count, width),
        "img",
        split_axis=1,
        concat_axis=1,
        tiled=True,
    )
    update = jnp.sum(shares.astype(jnp.float32), axis=1)
    own_text = lax.dynamic_slice_in_dim(text, lax.axis_index("img") * width, width, 1)
    return (own_text.astype(jnp.float32) + jnp.tanh(attn_gate[0]) * update).astype(jnp.bfloat16)


BF16, F32 = jnp.bfloat16, jnp.float32
SMEM = pl.BlockSpec(memory_space=pltpu.SMEM)
VMEM = pl.BlockSpec(memory_space=pltpu.VMEM)
CHIPS = 4


def call(kernel, args, specs, outs, out_specs=None, scratch=(), flops=0, size=0, name=None, grid=(), limit=24):
    return pl.pallas_call(
        kernel,
        out_shape=outs,
        in_specs=specs,
        out_specs=[VMEM] * len(outs) if out_specs is None else out_specs,
        scratch_shapes=scratch,
        grid=grid,
        compiler_params=pltpu.CompilerParams(vmem_limit_bytes=limit * 2**20),
        cost_estimate=pl.CostEstimate(flops=flops, bytes_accessed=size, transcendentals=0),
        name=name,
    )(*args)


def block(index, size):
    return pl.ds(pl.multiple_of(index * size, size), size)


def start_kernel(where, text_hbm, gain, vis_hbm, q_hbm, *refs):
    pieces, refs = refs[:CHIPS], refs[CHIPS:]
    near, far, text_keep, text_give, q_keep, q_give, text, vis, scale, sems = refs
    chip, core, plane = where[0], where[1], where[2]
    tokens, width = text.shape
    part = width // 2
    half = text_keep.shape[1]
    step = 16
    first = pltpu.make_async_copy(vis_hbm, vis, sems.at[0])
    first.start()
    copies = []
    for k, r in enumerate(range(0, tokens, 2 * step)):
        rows = pl.ds(r, 2 * step)
        copies.append(pltpu.make_async_copy(text_hbm.at[rows, :], text.at[rows, :], sems.at[3 + k]))
        copies[-1].start()
    cuts = [
        pltpu.make_async_copy(q_hbm.at[:, block(core, half)], q_keep, sems.at[1]),
        pltpu.make_async_copy(q_hbm.at[:, block(1 - core, half)], q_give, sems.at[2]),
    ]
    for copy in cuts:
        copy.start()
    first.wait()
    for s in range(CHIPS):
        pieces[s][...] = vis[:, block(chip ^ s, pieces[s].shape[1])]
    for r in range(0, tokens, step):
        if r % (2 * step) == 0:
            copies[r // (2 * step)].wait()
        x = text[r : r + step, :].astype(F32)
        mean_sq = jnp.mean(x * x, axis=-1, keepdims=True)
        scale[r : r + step, :] = jnp.broadcast_to(lax.rsqrt(mean_sq + EPS), (step, 128))
    line = chip // 2
    for out, index in ((far, 1 - line), (near, line)):
        cols = block(index, part)
        row_gain = gain[:, cols]
        for r in range(0, tokens, step):
            x = text[r : r + step, cols].astype(F32)
            out[r : r + step, :] = (x * scale[r : r + step, 0:1] * row_gain).astype(BF16)
    text_keep[...] = text[:, block(2 * plane + core, half)]
    text_give[...] = text[:, block(2 * plane + 1 - core, half)]
    for copy in cuts:
        copy.wait()


def kv_kernel(where, vis, vis_other, kv_own, kv_other, *refs):
    shares, (other, near_total, sems) = refs[:CHIPS], refs[CHIPS:]
    core = where[1]
    rows = kv_own.shape[0]
    head = kv_own.shape[1] // (2 * CHIPS)
    copies = []
    for j in range(CHIPS):
        copies.append(
            pltpu.make_async_copy(
                kv_other.at[:, block(2 * j + core, head)],
                other.at[:, pl.ds(j * head, head)],
                sems.at[j],
            )
        )
        copies[-1].start()
    near, far = block(core, rows), block(1 - core, rows)
    x_near = jnp.concatenate((vis[:, near], vis_other[:, near]), axis=0)
    x_far = jnp.concatenate((vis[:, far], vis_other[:, far]), axis=0)
    total = vis.shape[0]
    count = total // CHIPS
    for j in range(CHIPS):
        near_total[:, j * head : (j + 1) * head] = jnp.dot(
            x_near, kv_own[:, block(2 * j + core, head)], preferred_element_type=F32
        )
    for j in range(CHIPS):
        copies[j].wait()
        cols = slice(j * head, (j + 1) * head)
        out = near_total[:, cols] + jnp.dot(x_far, other[:, cols], preferred_element_type=F32)
        for s in range(CHIPS):
            shares[s][:count, cols] = out[s * count : (s + 1) * count]
            shares[s][count:, cols] = out[total + s * count : total + (s + 1) * count]


def kv_norm_kernel(where, k_gain, *refs):
    shares, (here, there, give) = refs[:CHIPS], refs[CHIPS:]
    plane = where[2]
    lines, head = here.shape
    dim = head // 2
    for t, (out, row) in enumerate(((here, 0), (give, 0), (there, 0), (give, lines))):
        cols = block(plane ^ t, head)
        total = (shares[0][:, cols] + shares[1][:, cols]) + (shares[2][:, cols] + shares[3][:, cols])
        keys = head_norm(total[:, :dim], k_gain[...])
        out[row : row + lines, :dim] = keys.astype(BF16)
        out[row : row + lines, dim:] = total[:, dim:].astype(BF16)


def kv_turn_kernel(there, landed, out):
    lines = there.shape[0]
    out[:lines, :] = there[...]
    out[lines:, :] = landed[lines:, :]


def kv_join_kernel(here, landed, last, out):
    lines = here.shape[0]
    out[:lines, :] = here[...]
    out[lines : 2 * lines, :] = landed[:lines, :]
    out[2 * lines :, :] = last[...]


def query_share(index, own, other, first, second, flip):
    rows = first.shape[0]
    total = None
    for weight, k in ((first, index), (second, index ^ flip)):
        cols = block(k, rows)
        x = jnp.concatenate((own[:, cols], other[:, cols]), axis=0)
        share = jnp.dot(x, weight[...], preferred_element_type=F32)
        total = share if total is None else total + share
    return total


def early_kernel(where, own, other, q_keep, q_other, out):
    index = 2 * lax.rem(where[0], 2) + where[1]
    out[...] = query_share(index, own, other, q_keep, q_other, 1)


def late_kernel(where, own, other, q_side, q_corner, early, out):
    index = (2 * lax.rem(where[0], 2) + where[1]) ^ 2
    share = early[...] + query_share(index, own, other, q_side, q_corner, 1)
    out[...] = share.astype(out.dtype)


def attend_kernel(q_gain, first, landed, *refs):
    kv, (bias, context) = refs[:CHIPS], refs[CHIPS:]
    dim = q_gain.shape[1]
    rows, half = context.shape
    keys = jnp.concatenate([x[:, :dim] for x in kv], axis=0)
    values = jnp.concatenate([x[:, dim:] for x in kv], axis=0)
    step = 128
    for r in range(0, rows, step):
        for g in range(half // dim):
            cols = slice(g * dim, (g + 1) * dim)
            query = first[r : r + step, cols] + landed[r : r + step, cols].astype(F32)
            query = head_norm(query, q_gain[...]).astype(BF16)
            scores = lax.dot_general(
                query, keys, (((1,), (1,)), ((), ())), preferred_element_type=F32
            )
            scores = scores * dim ** (-0.5) + bias[r : r + step, :]
            weights = jnp.exp(scores - jnp.max(scores, axis=-1, keepdims=True))
            total = jnp.sum(weights, axis=-1, keepdims=True)
            acc = jnp.dot(weights.astype(BF16), values, preferred_element_type=F32)
            context[r : r + step, cols] = (acc / total).astype(BF16)


def out_kernel(where, near, far, o_own, o_early, o_late, own, other):
    core = where[1]
    tokens, width = own.shape
    half = near.shape[1]
    turned = jnp.concatenate((far[tokens:, :], far[:tokens, :]), axis=0)
    share = jnp.dot(near[...], o_own[block(core, half), :], preferred_element_type=F32)
    share += jnp.dot(turned, o_own[block(1 - core, half), :], preferred_element_type=F32)
    own[:, : width // 2] = share[:tokens].astype(BF16)
    other[:, : width // 2] = share[tokens:].astype(BF16)
    top = jnp.where(core == 0, near[...], turned)
    low = jnp.where(core == 0, turned, near[...])
    share = jnp.dot(top, o_early[...], preferred_element_type=F32)
    share += jnp.dot(low, o_late[...], preferred_element_type=F32)
    own[:, width // 2 :] = share[:tokens].astype(BF16)
    other[:, width // 2 :] = share[tokens:].astype(BF16)


def pick_kernel(where, own, landed, *outs):
    first = where[0] ^ where[2]
    half = outs[0].shape[1]
    for t in range(CHIPS):
        for s in range(CHIPS):

            @pl.when((first ^ t) == s)
            def _():
                outs[t][...] = (own, landed)[s % 2][:, (s // 2) * half : (s // 2 + 1) * half]


def mixed_rows(gate, text, shares):
    x = [share[...].astype(F32) for share in shares]
    update = (x[0] + x[1]) + (x[2] + x[3])
    return (text[...].astype(F32) + gate[0] * update).astype(BF16)


def give_kernel(gate, text, *refs):
    refs[CHIPS][...] = mixed_rows(gate, text, refs[:CHIPS])


def last_kernel(where, gate, text, back, *refs):
    shares, out = refs[:CHIPS], refs[CHIPS]
    core = where[1]
    half = text.shape[1]
    out[:, block(core, half)] = mixed_rows(gate, text, shares)
    out[:, block(1 - core, half)] = back[...]


def paired(
    text,
    input_gain,
    q_weight,
    kv_weight,
    o_weight,
    q_gain,
    k_gain,
    attn_gate,
    vision,
    segment_ids,
    seg_images,
    image_slot,
):
    ctx_count = lax.axis_size("ctx")
    place, plane = lax.axis_index("ctx"), lax.axis_index("img")
    chip, core = place // 2, place % 2
    where = jnp.stack((chip, core, plane)).astype(jnp.int32)
    tokens, width = text.shape
    head_dim = q_gain.shape[0]
    rows_dev, cols_plane = q_weight.shape
    half = cols_plane // 2
    part = 2 * rows_dev
    slots_here, vt_dev = vision.shape[:2]
    vis_here = slots_here * vt_dev
    kv_cols = kv_weight.shape[1] // 2

    def shape(rows, cols, kind=BF16):
        return jax.ShapeDtypeStruct((rows, cols), kind)

    def swap(x):
        return lax.ppermute(x, "ctx", [(k, k ^ 1) for k in range(ctx_count)])

    def peer(x, s):
        return lax.ppermute(x, "ctx", [(k, k ^ (2 * s)) for k in range(ctx_count)])

    def along_x(x):
        return peer(x, 1)

    def along_y(x):
        return peer(x, 2)

    def across(x, t):
        return lax.ppermute(x, "img", [(k, k ^ t) for k in range(CHIPS)])

    steps = range(1, CHIPS)
    vis = vision.reshape(vis_here, width)
    kv_other = swap(kv_weight)

    anywhere = pl.BlockSpec(memory_space=pl.ANY)
    *vis_pieces, near, far, text_keep, text_give, q_keep, q_give = call(
        start_kernel,
        (where, text, input_gain[None], vis, q_weight),
        [SMEM, anywhere, VMEM, anywhere, anywhere],
        [shape(vis_here, part)] * CHIPS
        + [shape(tokens, width // 2)] * 2
        + [shape(tokens, half)] * 2
        + [shape(rows_dev, half)] * 2,
        scratch=[
            pltpu.VMEM((tokens, width), BF16),
            pltpu.VMEM((vis_here, width), BF16),
            pltpu.VMEM((tokens, 128), F32),
            pltpu.SemaphoreType.DMA((3 + tokens // 32,)),
        ],
        flops=8 * tokens * width,
        size=4 * 2**20,
        name="start",
        limit=60,
    )
    vis_own = jnp.concatenate([vis_pieces[0]] + [peer(vis_pieces[s], s) for s in steps])
    vis_other = swap(vis_own)
    q_side, q_other = along_x(q_keep), swap(q_give)
    far = along_y(far)

    shares = call(
        kv_kernel,
        (where, vis_own, vis_other, kv_weight, kv_other),
        [SMEM] + [VMEM] * 3 + [pl.BlockSpec(memory_space=pl.ANY)],
        [shape(2 * vis_here, kv_cols, F32)] * CHIPS,
        scratch=[
            pltpu.VMEM((rows_dev, kv_cols), BF16),
            pltpu.VMEM((8 * vis_here, kv_cols), F32),
            pltpu.SemaphoreType.DMA((CHIPS,)),
        ],
        flops=4 * vis_here * ctx_count * part * kv_cols,
        size=4 * 2**20,
        name="kv_shares",
    )
    shares = [shares[0]] + [peer(shares[s], s) for s in steps]
    shares[3], q_side, far = lax.optimization_barrier((shares[3], q_side, far))
    here, there, give = call(
        kv_norm_kernel,
        (where, k_gain[None], *shares),
        [SMEM] + [VMEM] * (1 + CHIPS),
        [shape(2 * vis_here, 2 * head_dim)] * 2 + [shape(4 * vis_here, 2 * head_dim)],
        name="kv_norm",
    )
    kv_z = across(give, 1)
    turn = call(
        kv_turn_kernel,
        (there, kv_z),
        [VMEM] * 2,
        [shape(4 * vis_here, 2 * head_dim)],
        name="kv_turn",
    )[0]
    kv_first = call(
        kv_join_kernel,
        (here, kv_z, across(turn, 2)),
        [VMEM] * 3,
        [shape(8 * vis_here, 2 * head_dim)],
        name="kv_join",
    )[0]
    q_behind, _ = lax.optimization_barrier((q_other, shares[0]))
    q_corner = along_x(q_behind)

    blocks = ((far, swap(far)), (near, swap(near)))
    early = [
        call(
            early_kernel,
            (where, *pair, q_keep, q_other),
            [SMEM] + [VMEM] * 4,
            [shape(2 * tokens, half, F32)],
            flops=4 * tokens * part * half,
            size=2 * 2**20,
            name="q_early",
        )[0]
        for pair in blocks
    ]
    o_early, _ = lax.optimization_barrier((o_weight[:half], here))
    q_corner, o_early = lax.optimization_barrier((q_corner, along_y(o_early)))
    q_far, q_first = [
        call(
            late_kernel,
            (where, *blocks[k], q_side, q_corner, early[k]),
            [SMEM] + [VMEM] * 5,
            [shape(2 * tokens, half, kind)],
            flops=4 * tokens * part * half,
            size=2 * 2**20,
            name="q_late",
        )[0]
        for k, kind in ((0, BF16), (1, F32))
    ]
    landed = along_y(q_far)
    kv_first, _ = lax.optimization_barrier((kv_first, q_first))
    kv_all = [kv_first] + [peer(kv_first, s) for s in steps]
    o_late, _ = lax.optimization_barrier((o_weight[half:], q_far))
    o_late = along_y(o_late)

    ids = jnp.concatenate((segment_ids, swap(segment_ids)))
    images = jnp.arange(image_slot.shape[0])
    slot_of = jnp.sum(
        jnp.where(seg_images[:, :, None] == images, image_slot[None, None, :], 0), axis=2
    )
    numbers = jnp.arange(seg_images.shape[0])
    own_slots = jnp.sum(
        jnp.where((ids[:, None] == numbers)[:, :, None], slot_of[None], 0), axis=1
    )
    key_rows = jnp.arange(CHIPS * CHIPS * 2 * vis_here)
    key_plane = plane ^ (key_rows // (2 * vis_here) % CHIPS)
    key_slot = key_plane * slots_here + key_rows // vt_dev % slots_here
    sees = jnp.any(own_slots[:, :, None] == key_slot, axis=1)
    bias = jnp.where(sees, 0.0, NEG).astype(F32)

    context = call(
        attend_kernel,
        (q_gain[None], q_first, landed, *kv_all, bias),
        [VMEM] * (4 + CHIPS),
        [shape(2 * tokens, half)],
        flops=8 * tokens * half * bias.shape[1],
        size=2 * 2**20,
        name="attend",
    )[0]

    context_x = along_x(context)
    shares = [
        call(
            out_kernel,
            (where, x, swap(x), o_weight, o_early, o_late),
            [SMEM] + [VMEM] * 5,
            [shape(tokens, 2 * half)] * 2,
            flops=8 * tokens * cols_plane * half,
            size=2 * 2**20,
            name="o_share",
        )
        for x in (context_x, context)
    ]
    summands = []
    for rows in (1, 0):
        picked = call(
            pick_kernel,
            (where, shares[1][rows], along_x(shares[0][rows])),
            [SMEM] + [VMEM] * 2,
            [shape(tokens, half)] * CHIPS,
            flops=2**20,
            size=2**20,
            name="pick",
        )
        summands.append([picked[0]] + [across(picked[t], t) for t in steps])
    gate = jnp.tanh(attn_gate)
    give = call(
        give_kernel,
        (gate, swap(text_give), *summands[0]),
        [SMEM] + [VMEM] * (1 + CHIPS),
        [shape(tokens, half)],
        flops=2**20,
        size=2**20,
        name="mix_give",
    )[0]
    return call(
        last_kernel,
        (where, gate, text_keep, swap(give), *summands[1]),
        [SMEM, SMEM] + [VMEM] * (2 + CHIPS),
        [shape(tokens, 2 * half)],
        flops=2**20,
        size=2**20,
        name="mix_keep",
    )[0]


def solution(mesh):
    fits = mesh.shape["img"] == 4 and mesh.shape["ctx"] == 8
    return jax.shard_map(
        paired if fits else general,
        mesh=mesh,
        in_specs=(
            P("ctx", None),
            P(),
            P("ctx", "img"),
            P("ctx", None),
            P("img", "ctx"),
            P(),
            P(),
            P(),
            P("img", "ctx", None),
            P("ctx"),
            P(),
            P(),
        ),
        out_specs=P("ctx", "img"),
        check_vma=False,
    )
```

```python
import jax
import jax.numpy as jnp
from jax import lax
from jax.experimental import pallas as pl
from jax.experimental.pallas import tpu as pltpu
from jax.sharding import PartitionSpec as P

KVH = 8


EPS = 1e-05
NEG = -1e30


def head_norm(values, gain):
    mean_sq = jnp.mean(values * values, axis=-1, keepdims=True)
    return values * lax.rsqrt(mean_sq + EPS) * gain


def attend(query, keys, values, mask):
    scale = query.shape[-1] ** (-0.5)
    scores = jnp.einsum("tkgd,nkd->tkgn", query, keys, preferred_element_type=jnp.float32) * scale
    live = mask[:, None, None, :]
    scores = jnp.where(live, scores, NEG)
    top = jnp.max(scores, axis=-1)
    weights = jnp.where(live, jnp.exp(scores - top[..., None]), 0.0)
    total = jnp.sum(weights, axis=-1)
    acc = jnp.einsum(
        "tkgn,nkd->tkgd", weights.astype(jnp.bfloat16), values, preferred_element_type=jnp.float32
    )
    return acc / total[..., None]


def general(
    text,
    input_gain,
    q_weight,
    kv_weight,
    o_weight,
    q_gain,
    k_gain,
    attn_gate,
    vision,
    segment_ids,
    seg_images,
    image_slot,
):
    tokens_here = text.shape[0]
    head_dim = q_gain.shape[0]
    ctx_count = lax.axis_size("ctx")
    img_count = lax.axis_size("img")
    heads_here = q_weight.shape[1] // head_dim
    kv_heads = max(1, KVH // img_count)
    group = heads_here // kv_heads
    slots_here, vt_dev = vision.shape[:2]
    rows_here = slots_here * vt_dev

    o_full = lax.all_gather(o_weight, "ctx", axis=1, tiled=True)
    vision_cols = lax.all_to_all(
        vision.reshape(rows_here, -1), "ctx", split_axis=1, concat_axis=0, tiled=True
    )
    hidden = head_norm(text.astype(jnp.float32), input_gain).astype(jnp.bfloat16)
    hidden_cols = lax.all_to_all(hidden, "ctx", split_axis=1, concat_axis=0, tiled=True)

    kv_share = jnp.dot(vision_cols, kv_weight, preferred_element_type=jnp.float32)
    kv_shares = lax.all_to_all(
        kv_share.reshape(ctx_count, rows_here, -1), "ctx", split_axis=0, concat_axis=0, tiled=True
    )
    projected = jnp.sum(kv_shares, axis=0).reshape(rows_here, KVH, 2, head_dim)
    keys = head_norm(projected[:, :, 0], k_gain).astype(jnp.bfloat16)
    values = projected[:, :, 1].astype(jnp.bfloat16)
    kv_rows = jnp.stack((keys, values), axis=2)
    owners = jnp.arange(img_count)[:, None] * KVH // img_count + jnp.arange(kv_heads)[None, :]
    kv_out = jnp.take(kv_rows, owners, axis=1).transpose(1, 0, 2, 3, 4)
    kv_in = lax.all_to_all(kv_out, "img", split_axis=0, concat_axis=0, tiled=True)
    kv_all = lax.all_gather(kv_in, "ctx", axis=0, tiled=False)

    q_share = jnp.dot(hidden_cols, q_weight, preferred_element_type=jnp.float32)
    q_shares = lax.all_to_all(
        q_share.astype(jnp.bfloat16).reshape(ctx_count, tokens_here, -1),
        "ctx",
        split_axis=0,
        concat_axis=0,
        tiled=True,
    )
    query = jnp.sum(q_shares.astype(jnp.float32), axis=0)
    query = head_norm(query.reshape(tokens_here, kv_heads, group, head_dim), q_gain).astype(
        jnp.bfloat16
    )

    slots = img_count * slots_here
    own_slots = jnp.take(image_slot, jnp.take(seg_images, segment_ids, axis=0), axis=0)
    slot_ids = jnp.arange(slots, dtype=jnp.int32)
    sees = jnp.any(own_slots[:, :, None] == slot_ids[None, None, :], axis=1)
    flat = kv_all.reshape(ctx_count * slots * vt_dev, kv_heads, 2, head_dim)
    mask = jnp.broadcast_to(
        sees[:, None, :, None], (tokens_here, ctx_count, slots, vt_dev)
    ).reshape(tokens_here, -1)
    context = attend(query, flat[:, :, 0], flat[:, :, 1], mask)
    context = context.astype(jnp.bfloat16).reshape(tokens_here, heads_here * head_dim)
    partial_terms = jnp.dot(context, o_full, preferred_element_type=jnp.float32)
    width = partial_terms.shape[1] // img_count
    shares = lax.all_to_all(
        partial_terms.astype(jnp.bfloat16).reshape(tokens_here, img_count, width),
        "img",
        split_axis=1,
        concat_axis=1,
        tiled=True,
    )
    update = jnp.sum(shares.astype(jnp.float32), axis=1)
    own_text = lax.dynamic_slice_in_dim(text, lax.axis_index("img") * width, width, 1)
    return (own_text.astype(jnp.float32) + jnp.tanh(attn_gate[0]) * update).astype(jnp.bfloat16)


BF16, F32 = jnp.bfloat16, jnp.float32
SMEM = pl.BlockSpec(memory_space=pltpu.SMEM)
VMEM = pl.BlockSpec(memory_space=pltpu.VMEM)
CHIPS = 4


def call(kernel, args, specs, outs, out_specs=None, scratch=(), flops=0, size=0, name=None, grid=(), limit=24):
    return pl.pallas_call(
        kernel,
        out_shape=outs,
        in_specs=specs,
        out_specs=[VMEM] * len(outs) if out_specs is None else out_specs,
        scratch_shapes=scratch,
        grid=grid,
        compiler_params=pltpu.CompilerParams(vmem_limit_bytes=limit * 2**20),
        cost_estimate=pl.CostEstimate(flops=flops, bytes_accessed=size, transcendentals=0),
        name=name,
    )(*args)


def block(index, size):
    return pl.ds(pl.multiple_of(index * size, size), size)


def row_scales(text, scale, step, ready=()):
    for k, r in enumerate(range(0, text.shape[0], step)):
        if ready:
            ready[k].wait()
        x = text[r : r + step, :].astype(F32)
        mean_sq = jnp.mean(x * x, axis=-1, keepdims=True)
        scale[r : r + step, :] = jnp.broadcast_to(lax.rsqrt(mean_sq + EPS), (step, 128))


def scaled(text, scale, gain, out, index, step):
    cols = block(index, out.shape[1])
    row_gain = gain[:, cols]
    for r in range(0, text.shape[0], step):
        x = text[r : r + step, cols].astype(F32)
        out[r : r + step, :] = (x * scale[r : r + step, 0:1] * row_gain).astype(BF16)


def start_kernel(where, text_hbm, gain, vis_hbm, q_hbm, *refs):
    pieces, refs = refs[:CHIPS], refs[CHIPS:]
    far, q_keep, q_give, text, vis, scale, sems = refs
    chip, core = where[0], where[1]
    tokens = text.shape[0]
    half = q_keep.shape[1]
    step = 16
    first = pltpu.make_async_copy(vis_hbm, vis, sems.at[0])
    first.start()
    copies = []
    for k, r in enumerate(range(0, tokens, step)):
        rows = pl.ds(r, step)
        copies.append(pltpu.make_async_copy(text_hbm.at[rows, :], text.at[rows, :], sems.at[3 + k]))
        copies[-1].start()
    cuts = [
        pltpu.make_async_copy(q_hbm.at[:, block(core, half)], q_keep, sems.at[1]),
        pltpu.make_async_copy(q_hbm.at[:, block(1 - core, half)], q_give, sems.at[2]),
    ]
    for copy in cuts:
        copy.start()
    first.wait()
    for s in range(CHIPS):
        pieces[s][...] = vis[:, block(chip ^ s, pieces[s].shape[1])]
    row_scales(text, scale, step, copies)
    scaled(text, scale, gain, far, 1 - chip // 2, step)
    for copy in cuts:
        copy.wait()


def near_kernel(where, text, gain, near, text_keep, text_give, scale):
    chip, core, plane = where[0], where[1], where[2]
    half = text_keep.shape[1]
    row_scales(text, scale, 16)
    scaled(text, scale, gain, near, chip // 2, 16)
    text_keep[...] = text[:, block(2 * plane + core, half)]
    text_give[...] = text[:, block(2 * plane + 1 - core, half)]


def kv_kernel(where, *refs):
    vis, vis_other, refs = refs[:CHIPS], refs[CHIPS : 2 * CHIPS], refs[2 * CHIPS :]
    (kv_own, kv_other), refs = refs[:2], refs[2:]
    shares, (other, near_total, sems) = refs[:CHIPS], refs[CHIPS:]
    core = where[1]
    rows = kv_own.shape[0]
    head = kv_own.shape[1] // (2 * CHIPS)
    copies = []
    for j in range(CHIPS):
        copies.append(
            pltpu.make_async_copy(
                kv_other.at[:, block(2 * j + core, head)],
                other.at[:, pl.ds(j * head, head)],
                sems.at[j],
            )
        )
        copies[-1].start()
    near, far = block(core, rows), block(1 - core, rows)
    x_near = jnp.concatenate([x[:, near] for x in vis + vis_other], axis=0)
    x_far = jnp.concatenate([x[:, far] for x in vis + vis_other], axis=0)
    count = vis[0].shape[0]
    total = CHIPS * count
    for j in range(CHIPS):
        near_total[:, j * head : (j + 1) * head] = jnp.dot(
            x_near, kv_own[:, block(2 * j + core, head)], preferred_element_type=F32
        )
    for j in range(CHIPS):
        copies[j].wait()
        cols = slice(j * head, (j + 1) * head)
        out = near_total[:, cols] + jnp.dot(x_far, other[:, cols], preferred_element_type=F32)
        for s in range(CHIPS):
            shares[s][:count, cols] = out[s * count : (s + 1) * count]
            shares[s][count:, cols] = out[total + s * count : total + (s + 1) * count]


def kv_norm_kernel(where, k_gain, *refs):
    shares, (here, there, give) = refs[:CHIPS], refs[CHIPS:]
    plane = where[2]
    lines, head = here.shape
    dim = head // 2
    for t, (out, row) in enumerate(((here, 0), (give, 0), (there, 0), (give, lines))):
        cols = block(plane ^ t, head)
        total = (shares[0][:, cols] + shares[1][:, cols]) + (shares[2][:, cols] + shares[3][:, cols])
        keys = head_norm(total[:, :dim], k_gain[...])
        out[row : row + lines, :dim] = keys.astype(BF16)
        out[row : row + lines, dim:] = total[:, dim:].astype(BF16)


def kv_turn_kernel(there, landed, out):
    lines = there.shape[0]
    out[:lines, :] = there[...]
    out[lines:, :] = landed[lines:, :]


def kv_join_kernel(here, landed, last, out):
    lines = here.shape[0]
    out[:lines, :] = here[...]
    out[lines : 2 * lines, :] = landed[:lines, :]
    out[2 * lines :, :] = last[...]


def query_share(index, own, other, first, second, flip):
    rows = first.shape[0]
    total = None
    for weight, k in ((first, index), (second, index ^ flip)):
        cols = block(k, rows)
        x = jnp.concatenate((own[:, cols], other[:, cols]), axis=0)
        share = jnp.dot(x, weight[...], preferred_element_type=F32)
        total = share if total is None else total + share
    return total


def early_kernel(where, own, other, q_keep, q_other, out):
    index = 2 * lax.rem(where[0], 2) + where[1]
    out[...] = query_share(index, own, other, q_keep, q_other, 1)


def late_kernel(where, own, other, q_side, q_corner, early, out):
    index = (2 * lax.rem(where[0], 2) + where[1]) ^ 2
    share = early[...] + query_share(index, own, other, q_side, q_corner, 1)
    out[...] = share.astype(out.dtype)


def attend_kernel(q_gain, first, landed, *refs):
    kv, (bias, context) = refs[:CHIPS], refs[CHIPS:]
    dim = q_gain.shape[1]
    rows, half = context.shape
    keys = jnp.concatenate([x[:, :dim] for x in kv], axis=0)
    values = jnp.concatenate([x[:, dim:] for x in kv], axis=0)
    step = 128
    for r in range(0, rows, step):
        for g in range(half // dim):
            cols = slice(g * dim, (g + 1) * dim)
            query = first[r : r + step, cols] + landed[r : r + step, cols].astype(F32)
            query = head_norm(query, q_gain[...]).astype(BF16)
            scores = lax.dot_general(
                query, keys, (((1,), (1,)), ((), ())), preferred_element_type=F32
            )
            scores = scores * dim ** (-0.5) + bias[r : r + step, :]
            weights = jnp.exp(scores - jnp.max(scores, axis=-1, keepdims=True))
            total = jnp.sum(weights, axis=-1, keepdims=True)
            acc = jnp.dot(weights.astype(BF16), values, preferred_element_type=F32)
            context[r : r + step, cols] = (acc / total).astype(BF16)


def out_kernel(where, near, far, o_own, o_early, o_late, own, other):
    core = where[1]
    tokens, width = own.shape
    half = near.shape[1]
    turned = jnp.concatenate((far[tokens:, :], far[:tokens, :]), axis=0)
    share = jnp.dot(near[...], o_own[block(core, half), :], preferred_element_type=F32)
    share += jnp.dot(turned, o_own[block(1 - core, half), :], preferred_element_type=F32)
    own[:, : width // 2] = share[:tokens].astype(BF16)
    other[:, : width // 2] = share[tokens:].astype(BF16)
    top = jnp.where(core == 0, near[...], turned)
    low = jnp.where(core == 0, turned, near[...])
    share = jnp.dot(top, o_early[...], preferred_element_type=F32)
    share += jnp.dot(low, o_late[...], preferred_element_type=F32)
    own[:, width // 2 :] = share[:tokens].astype(BF16)
    other[:, width // 2 :] = share[tokens:].astype(BF16)


def pick_kernel(where, own, landed, *outs):
    first = where[0] ^ where[2]
    half = outs[0].shape[1]
    for t in range(CHIPS):
        for s in range(CHIPS):

            @pl.when((first ^ t) == s)
            def _():
                outs[t][...] = (own, landed)[s % 2][:, (s // 2) * half : (s // 2 + 1) * half]


def mixed_rows(gate, text, shares):
    x = [share[...].astype(F32) for share in shares]
    update = (x[0] + x[1]) + (x[2] + x[3])
    return (text[...].astype(F32) + gate[0] * update).astype(BF16)


def give_kernel(gate, text, *refs):
    refs[CHIPS][...] = mixed_rows(gate, text, refs[:CHIPS])


def last_kernel(where, gate, text, back, *refs):
    shares, out = refs[:CHIPS], refs[CHIPS]
    core = where[1]
    half = text.shape[1]
    out[:, block(core, half)] = mixed_rows(gate, text, shares)
    out[:, block(1 - core, half)] = back[...]


def paired(
    text,
    input_gain,
    q_weight,
    kv_weight,
    o_weight,
    q_gain,
    k_gain,
    attn_gate,
    vision,
    segment_ids,
    seg_images,
    image_slot,
):
    ctx_count = lax.axis_size("ctx")
    place, plane = lax.axis_index("ctx"), lax.axis_index("img")
    chip, core = place // 2, place % 2
    where = jnp.stack((chip, core, plane)).astype(jnp.int32)
    tokens, width = text.shape
    head_dim = q_gain.shape[0]
    rows_dev, cols_plane = q_weight.shape
    half = cols_plane // 2
    part = 2 * rows_dev
    slots_here, vt_dev = vision.shape[:2]
    vis_here = slots_here * vt_dev
    kv_cols = kv_weight.shape[1] // 2

    def shape(rows, cols, kind=BF16):
        return jax.ShapeDtypeStruct((rows, cols), kind)

    def swap(x):
        return lax.ppermute(x, "ctx", [(k, k ^ 1) for k in range(ctx_count)])

    def peer(x, s):
        return lax.ppermute(x, "ctx", [(k, k ^ (2 * s)) for k in range(ctx_count)])

    def along_x(x):
        return peer(x, 1)

    def along_y(x):
        return peer(x, 2)

    def across(x, t):
        return lax.ppermute(x, "img", [(k, k ^ t) for k in range(CHIPS)])

    steps = range(1, CHIPS)
    vis = vision.reshape(vis_here, width)
    kv_other = swap(kv_weight)

    anywhere = pl.BlockSpec(memory_space=pl.ANY)
    *vis_pieces, far, q_keep, q_give = call(
        start_kernel,
        (where, text, input_gain[None], vis, q_weight),
        [SMEM, anywhere, VMEM, anywhere, anywhere],
        [shape(vis_here, part)] * CHIPS
        + [shape(tokens, width // 2)]
        + [shape(rows_dev, half)] * 2,
        out_specs=[VMEM] * (1 + CHIPS) + [anywhere] * 2,
        scratch=[
            pltpu.VMEM((tokens, width), BF16),
            pltpu.VMEM((vis_here, width), BF16),
            pltpu.VMEM((tokens, 128), F32),
            pltpu.SemaphoreType.DMA((3 + tokens // 16,)),
        ],
        flops=8 * tokens * width,
        size=4 * 2**20,
        name="start",
        limit=60,
    )
    vis_own = [vis_pieces[0]] + [peer(vis_pieces[s], s) for s in steps]
    vis_other = [swap(x) for x in vis_own]
    q_side, q_other = along_x(q_keep), swap(q_give)
    far = along_y(far)

    shares = call(
        kv_kernel,
        (where, *vis_own, *vis_other, kv_weight, kv_other),
        [SMEM] + [VMEM] * (1 + 2 * CHIPS) + [pl.BlockSpec(memory_space=pl.ANY)],
        [shape(2 * vis_here, kv_cols, F32)] * CHIPS,
        scratch=[
            pltpu.VMEM((rows_dev, kv_cols), BF16),
            pltpu.VMEM((8 * vis_here, kv_cols), F32),
            pltpu.SemaphoreType.DMA((CHIPS,)),
        ],
        flops=4 * vis_here * ctx_count * part * kv_cols,
        size=4 * 2**20,
        name="kv_shares",
    )
    where_near, _ = lax.optimization_barrier((where, shares[0]))
    near, text_keep, text_give = call(
        near_kernel,
        (where_near, text, input_gain[None]),
        [SMEM, VMEM, VMEM],
        [shape(tokens, width // 2)] + [shape(tokens, half)] * 2,
        scratch=[pltpu.VMEM((tokens, 128), F32)],
        flops=8 * tokens * width,
        size=4 * 2**20,
        name="near",
    )
    shares = [shares[0]] + [peer(shares[s], s) for s in steps]
    shares[3], q_side, far, near = lax.optimization_barrier((shares[3], q_side, far, near))
    here, there, give = call(
        kv_norm_kernel,
        (where, k_gain[None], *shares),
        [SMEM] + [VMEM] * (1 + CHIPS),
        [shape(2 * vis_here, 2 * head_dim)] * 2 + [shape(4 * vis_here, 2 * head_dim)],
        name="kv_norm",
    )
    blocks = ((far, swap(far)), (near, swap(near)))
    early = [
        call(
            early_kernel,
            (where, *pair, q_keep, q_other),
            [SMEM] + [VMEM] * 4,
            [shape(2 * tokens, half, F32)],
            flops=4 * tokens * part * half,
            size=2 * 2**20,
            name="q_early",
        )[0]
        for pair in blocks
    ]
    kv_z = across(give, 1)
    kv_z, early[0] = lax.optimization_barrier((kv_z, early[0]))
    turn = call(
        kv_turn_kernel,
        (there, kv_z),
        [VMEM] * 2,
        [shape(4 * vis_here, 2 * head_dim)],
        name="kv_turn",
    )[0]
    kv_first = call(
        kv_join_kernel,
        (here, kv_z, across(turn, 2)),
        [VMEM] * 3,
        [shape(8 * vis_here, 2 * head_dim)],
        name="kv_join",
    )[0]
    kv_all = [kv_first] + [peer(kv_first, s) for s in steps]

    q_behind, _ = lax.optimization_barrier((q_other, shares[0]))
    q_corner = along_x(q_behind)

    o_early, _ = lax.optimization_barrier((o_weight[:half], here))
    q_corner, o_early = lax.optimization_barrier((q_corner, along_y(o_early)))
    early[1], kv_all[1] = lax.optimization_barrier((early[1], kv_all[1]))
    q_far, q_first = [
        call(
            late_kernel,
            (where, *blocks[k], q_side, q_corner, early[k]),
            [SMEM] + [VMEM] * 5,
            [shape(2 * tokens, half, kind)],
            flops=4 * tokens * part * half,
            size=2 * 2**20,
            name="q_late",
        )[0]
        for k, kind in ((0, BF16), (1, F32))
    ]
    landed = along_y(q_far)
    o_late, _ = lax.optimization_barrier((o_weight[half:], q_far))
    o_late = along_y(o_late)

    ids = jnp.concatenate((segment_ids, swap(segment_ids)))
    images = jnp.arange(image_slot.shape[0])
    slot_of = jnp.sum(
        jnp.where(seg_images[:, :, None] == images, image_slot[None, None, :], 0), axis=2
    )
    numbers = jnp.arange(seg_images.shape[0])
    own_slots = jnp.sum(
        jnp.where((ids[:, None] == numbers)[:, :, None], slot_of[None], 0), axis=1
    )
    key_rows = jnp.arange(CHIPS * CHIPS * 2 * vis_here)
    key_plane = plane ^ (key_rows // (2 * vis_here) % CHIPS)
    key_slot = key_plane * slots_here + key_rows // vt_dev % slots_here
    sees = jnp.any(own_slots[:, :, None] == key_slot, axis=1)
    bias = jnp.where(sees, 0.0, NEG).astype(F32)

    context = call(
        attend_kernel,
        (q_gain[None], q_first, landed, *kv_all, bias),
        [VMEM] * (4 + CHIPS),
        [shape(2 * tokens, half)],
        flops=8 * tokens * half * bias.shape[1],
        size=2 * 2**20,
        name="attend",
    )[0]

    context_x = along_x(context)
    shares = [
        call(
            out_kernel,
            (where, x, swap(x), o_weight, o_early, o_late),
            [SMEM] + [VMEM] * 5,
            [shape(tokens, 2 * half)] * 2,
            flops=8 * tokens * cols_plane * half,
            size=2 * 2**20,
            name="o_share",
        )
        for x in (context_x, context)
    ]
    summands = []
    for rows in (1, 0):
        picked = call(
            pick_kernel,
            (where, shares[1][rows], along_x(shares[0][rows])),
            [SMEM] + [VMEM] * 2,
            [shape(tokens, half)] * CHIPS,
            flops=2**20,
            size=2**20,
            name="pick",
        )
        summands.append([picked[0]] + [across(picked[t], t) for t in steps])
    gate = jnp.tanh(attn_gate)
    give = call(
        give_kernel,
        (gate, swap(text_give), *summands[0]),
        [SMEM] + [VMEM] * (1 + CHIPS),
        [shape(tokens, half)],
        flops=2**20,
        size=2**20,
        name="mix_give",
    )[0]
    return call(
        last_kernel,
        (where, gate, text_keep, swap(give), *summands[1]),
        [SMEM, SMEM] + [VMEM] * (2 + CHIPS),
        [shape(tokens, 2 * half)],
        flops=2**20,
        size=2**20,
        name="mix_keep",
    )[0]


def solution(mesh):
    fits = mesh.shape["img"] == 4 and mesh.shape["ctx"] == 8
    return jax.shard_map(
        paired if fits else general,
        mesh=mesh,
        in_specs=(
            P("ctx", None),
            P(),
            P("ctx", "img"),
            P("ctx", None),
            P("img", "ctx"),
            P(),
            P(),
            P(),
            P("img", "ctx", None),
            P("ctx"),
            P(),
            P(),
        ),
        out_specs=P("ctx", "img"),
        check_vma=False,
    )
```

```python
import jax
import jax.numpy as jnp
from jax import lax
from jax.experimental import pallas as pl
from jax.experimental.pallas import tpu as pltpu
from jax.sharding import PartitionSpec as P

KVH = 8


EPS = 1e-05
NEG = -1e30


def head_norm(values, gain):
    mean_sq = jnp.mean(values * values, axis=-1, keepdims=True)
    return values * lax.rsqrt(mean_sq + EPS) * gain


def attend(query, keys, values, mask):
    scale = query.shape[-1] ** (-0.5)
    scores = jnp.einsum("tkgd,nkd->tkgn", query, keys, preferred_element_type=jnp.float32) * scale
    live = mask[:, None, None, :]
    scores = jnp.where(live, scores, NEG)
    top = jnp.max(scores, axis=-1)
    weights = jnp.where(live, jnp.exp(scores - top[..., None]), 0.0)
    total = jnp.sum(weights, axis=-1)
    acc = jnp.einsum(
        "tkgn,nkd->tkgd", weights.astype(jnp.bfloat16), values, preferred_element_type=jnp.float32
    )
    return acc / total[..., None]


def general(
    text,
    input_gain,
    q_weight,
    kv_weight,
    o_weight,
    q_gain,
    k_gain,
    attn_gate,
    vision,
    segment_ids,
    seg_images,
    image_slot,
):
    tokens_here = text.shape[0]
    head_dim = q_gain.shape[0]
    ctx_count = lax.axis_size("ctx")
    img_count = lax.axis_size("img")
    heads_here = q_weight.shape[1] // head_dim
    kv_heads = max(1, KVH // img_count)
    group = heads_here // kv_heads
    slots_here, vt_dev = vision.shape[:2]
    rows_here = slots_here * vt_dev

    o_full = lax.all_gather(o_weight, "ctx", axis=1, tiled=True)
    vision_cols = lax.all_to_all(
        vision.reshape(rows_here, -1), "ctx", split_axis=1, concat_axis=0, tiled=True
    )
    hidden = head_norm(text.astype(jnp.float32), input_gain).astype(jnp.bfloat16)
    hidden_cols = lax.all_to_all(hidden, "ctx", split_axis=1, concat_axis=0, tiled=True)

    kv_share = jnp.dot(vision_cols, kv_weight, preferred_element_type=jnp.float32)
    kv_shares = lax.all_to_all(
        kv_share.reshape(ctx_count, rows_here, -1), "ctx", split_axis=0, concat_axis=0, tiled=True
    )
    projected = jnp.sum(kv_shares, axis=0).reshape(rows_here, KVH, 2, head_dim)
    keys = head_norm(projected[:, :, 0], k_gain).astype(jnp.bfloat16)
    values = projected[:, :, 1].astype(jnp.bfloat16)
    kv_rows = jnp.stack((keys, values), axis=2)
    owners = jnp.arange(img_count)[:, None] * KVH // img_count + jnp.arange(kv_heads)[None, :]
    kv_out = jnp.take(kv_rows, owners, axis=1).transpose(1, 0, 2, 3, 4)
    kv_in = lax.all_to_all(kv_out, "img", split_axis=0, concat_axis=0, tiled=True)
    kv_all = lax.all_gather(kv_in, "ctx", axis=0, tiled=False)

    q_share = jnp.dot(hidden_cols, q_weight, preferred_element_type=jnp.float32)
    q_shares = lax.all_to_all(
        q_share.astype(jnp.bfloat16).reshape(ctx_count, tokens_here, -1),
        "ctx",
        split_axis=0,
        concat_axis=0,
        tiled=True,
    )
    query = jnp.sum(q_shares.astype(jnp.float32), axis=0)
    query = head_norm(query.reshape(tokens_here, kv_heads, group, head_dim), q_gain).astype(
        jnp.bfloat16
    )

    slots = img_count * slots_here
    own_slots = jnp.take(image_slot, jnp.take(seg_images, segment_ids, axis=0), axis=0)
    slot_ids = jnp.arange(slots, dtype=jnp.int32)
    sees = jnp.any(own_slots[:, :, None] == slot_ids[None, None, :], axis=1)
    flat = kv_all.reshape(ctx_count * slots * vt_dev, kv_heads, 2, head_dim)
    mask = jnp.broadcast_to(
        sees[:, None, :, None], (tokens_here, ctx_count, slots, vt_dev)
    ).reshape(tokens_here, -1)
    context = attend(query, flat[:, :, 0], flat[:, :, 1], mask)
    context = context.astype(jnp.bfloat16).reshape(tokens_here, heads_here * head_dim)
    partial_terms = jnp.dot(context, o_full, preferred_element_type=jnp.float32)
    width = partial_terms.shape[1] // img_count
    shares = lax.all_to_all(
        partial_terms.astype(jnp.bfloat16).reshape(tokens_here, img_count, width),
        "img",
        split_axis=1,
        concat_axis=1,
        tiled=True,
    )
    update = jnp.sum(shares.astype(jnp.float32), axis=1)
    own_text = lax.dynamic_slice_in_dim(text, lax.axis_index("img") * width, width, 1)
    return (own_text.astype(jnp.float32) + jnp.tanh(attn_gate[0]) * update).astype(jnp.bfloat16)


BF16, F32 = jnp.bfloat16, jnp.float32
SMEM = pl.BlockSpec(memory_space=pltpu.SMEM)
VMEM = pl.BlockSpec(memory_space=pltpu.VMEM)
CHIPS = 4


def call(kernel, args, specs, outs, out_specs=None, scratch=(), flops=0, size=0, name=None, grid=(), limit=24):
    return pl.pallas_call(
        kernel,
        out_shape=outs,
        in_specs=specs,
        out_specs=[VMEM] * len(outs) if out_specs is None else out_specs,
        scratch_shapes=scratch,
        grid=grid,
        compiler_params=pltpu.CompilerParams(vmem_limit_bytes=limit * 2**20),
        cost_estimate=pl.CostEstimate(flops=flops, bytes_accessed=size, transcendentals=0),
        name=name,
    )(*args)


def block(index, size):
    return pl.ds(pl.multiple_of(index * size, size), size)


def row_scales(text, scale, step, ready=()):
    for k, r in enumerate(range(0, text.shape[0], step)):
        if ready:
            ready[k].wait()
        x = text[r : r + step, :].astype(F32)
        mean_sq = jnp.mean(x * x, axis=-1, keepdims=True)
        scale[r : r + step, :] = jnp.broadcast_to(lax.rsqrt(mean_sq + EPS), (step, 128))


def scaled(text, scale, gain, out, index, step):
    cols = block(index, out.shape[1])
    row_gain = gain[:, cols]
    for r in range(0, text.shape[0], step):
        x = text[r : r + step, cols].astype(F32)
        out[r : r + step, :] = (x * scale[r : r + step, 0:1] * row_gain).astype(BF16)


def start_kernel(where, text_hbm, gain, vis_hbm, q_hbm, *refs):
    pieces, refs = refs[:CHIPS], refs[CHIPS:]
    far, q_keep, q_give, text, vis, scale, sems = refs
    chip, core = where[0], where[1]
    tokens = text.shape[0]
    half = q_keep.shape[1]
    step = 16
    first = pltpu.make_async_copy(vis_hbm, vis, sems.at[0])
    first.start()
    copies = []
    for k, r in enumerate(range(0, tokens, step)):
        rows = pl.ds(r, step)
        copies.append(pltpu.make_async_copy(text_hbm.at[rows, :], text.at[rows, :], sems.at[3 + k]))
        copies[-1].start()
    cuts = [
        pltpu.make_async_copy(q_hbm.at[:, block(core, half)], q_keep, sems.at[1]),
        pltpu.make_async_copy(q_hbm.at[:, block(1 - core, half)], q_give, sems.at[2]),
    ]
    for copy in cuts:
        copy.start()
    first.wait()
    for s in range(CHIPS):
        pieces[s][...] = vis[:, block(chip ^ s, pieces[s].shape[1])]
    row_scales(text, scale, step, copies)
    scaled(text, scale, gain, far, 1 - chip // 2, step)
    for copy in cuts:
        copy.wait()


def near_kernel(where, text, gain, near, text_keep, text_give, scale):
    chip, core, plane = where[0], where[1], where[2]
    half = text_keep.shape[1]
    row_scales(text, scale, 16)
    scaled(text, scale, gain, near, chip // 2, 16)
    text_keep[...] = text[:, block(2 * plane + core, half)]
    text_give[...] = text[:, block(2 * plane + 1 - core, half)]


def kv_kernel(where, *refs):
    vis, vis_other, refs = refs[:CHIPS], refs[CHIPS : 2 * CHIPS], refs[2 * CHIPS :]
    (kv_own, kv_other), refs = refs[:2], refs[2:]
    shares, (other, near_total, sems) = refs[:CHIPS], refs[CHIPS:]
    core = where[1]
    rows = kv_own.shape[0]
    head = kv_own.shape[1] // (2 * CHIPS)
    copies = []
    for j in range(CHIPS):
        copies.append(
            pltpu.make_async_copy(
                kv_other.at[:, block(2 * j + core, head)],
                other.at[:, pl.ds(j * head, head)],
                sems.at[j],
            )
        )
        copies[-1].start()
    near, far = block(core, rows), block(1 - core, rows)
    x_near = jnp.concatenate([x[:, near] for x in vis + vis_other], axis=0)
    x_far = jnp.concatenate([x[:, far] for x in vis + vis_other], axis=0)
    count = vis[0].shape[0]
    total = CHIPS * count
    for j in range(CHIPS):
        near_total[:, j * head : (j + 1) * head] = jnp.dot(
            x_near, kv_own[:, block(2 * j + core, head)], preferred_element_type=F32
        )
    for j in range(CHIPS):
        copies[j].wait()
        cols = slice(j * head, (j + 1) * head)
        out = near_total[:, cols] + jnp.dot(x_far, other[:, cols], preferred_element_type=F32)
        for s in range(CHIPS):
            shares[s][:count, cols] = out[s * count : (s + 1) * count]
            shares[s][count:, cols] = out[total + s * count : total + (s + 1) * count]


def kv_norm_kernel(where, k_gain, *refs):
    shares, (here, there, give) = refs[:CHIPS], refs[CHIPS:]
    plane = where[2]
    lines, head = here.shape
    dim = head // 2
    for t, (out, row) in enumerate(((here, 0), (give, 0), (there, 0), (give, lines))):
        cols = block(plane ^ t, head)
        total = (shares[0][:, cols] + shares[1][:, cols]) + (shares[2][:, cols] + shares[3][:, cols])
        keys = head_norm(total[:, :dim], k_gain[...])
        out[row : row + lines, :dim] = keys.astype(BF16)
        out[row : row + lines, dim:] = total[:, dim:].astype(BF16)


def kv_turn_kernel(there, landed, out):
    lines = there.shape[0]
    out[:lines, :] = there[...]
    out[lines:, :] = landed[lines:, :]


def kv_join_kernel(here, landed, last, out):
    lines = here.shape[0]
    out[:lines, :] = here[...]
    out[lines : 2 * lines, :] = landed[:lines, :]
    out[2 * lines :, :] = last[...]


def query_share(index, own, other, first, second, flip):
    rows = first.shape[0]
    total = None
    for weight, k in ((first, index), (second, index ^ flip)):
        cols = block(k, rows)
        x = jnp.concatenate((own[:, cols], other[:, cols]), axis=0)
        share = jnp.dot(x, weight[...], preferred_element_type=F32)
        total = share if total is None else total + share
    return total


def early_kernel(where, own, other, q_keep, q_other, out):
    index = 2 * lax.rem(where[0], 2) + where[1]
    out[...] = query_share(index, own, other, q_keep, q_other, 1)


def late_kernel(where, own, other, q_side, q_corner, early, out):
    index = (2 * lax.rem(where[0], 2) + where[1]) ^ 2
    share = early[...] + query_share(index, own, other, q_side, q_corner, 1)
    out[...] = share.astype(out.dtype)


def attend_kernel(q_gain, first, landed, *refs):
    kv, (bias, context) = refs[:CHIPS], refs[CHIPS:]
    dim = q_gain.shape[1]
    rows, half = context.shape
    keys = jnp.concatenate([x[:, :dim] for x in kv], axis=0)
    values = jnp.concatenate([x[:, dim:] for x in kv], axis=0)
    step = 128
    for r in range(0, rows, step):
        for g in range(half // dim):
            cols = slice(g * dim, (g + 1) * dim)
            query = first[r : r + step, cols] + landed[r : r + step, cols].astype(F32)
            query = head_norm(query, q_gain[...]).astype(BF16)
            scores = lax.dot_general(
                query, keys, (((1,), (1,)), ((), ())), preferred_element_type=F32
            )
            scores = scores * dim ** (-0.5) + bias[r : r + step, :]
            weights = jnp.exp(scores - jnp.max(scores, axis=-1, keepdims=True))
            total = jnp.sum(weights, axis=-1, keepdims=True)
            acc = jnp.dot(weights.astype(BF16), values, preferred_element_type=F32)
            context[r : r + step, cols] = (acc / total).astype(BF16)


def out_kernel(where, near, far, o_own, o_early, o_late, own, other):
    core = where[1]
    tokens, width = own.shape
    half = near.shape[1]
    turned = jnp.concatenate((far[tokens:, :], far[:tokens, :]), axis=0)
    share = jnp.dot(near[...], o_own[block(core, half), :], preferred_element_type=F32)
    share += jnp.dot(turned, o_own[block(1 - core, half), :], preferred_element_type=F32)
    own[:, : width // 2] = share[:tokens].astype(BF16)
    other[:, : width // 2] = share[tokens:].astype(BF16)
    top = jnp.where(core == 0, near[...], turned)
    low = jnp.where(core == 0, turned, near[...])
    share = jnp.dot(top, o_early[...], preferred_element_type=F32)
    share += jnp.dot(low, o_late[...], preferred_element_type=F32)
    own[:, width // 2 :] = share[:tokens].astype(BF16)
    other[:, width // 2 :] = share[tokens:].astype(BF16)


def pick_kernel(where, own, landed, *outs):
    first = where[0] ^ where[2]
    half = outs[0].shape[1]
    for t in range(CHIPS):
        for s in range(CHIPS):

            @pl.when((first ^ t) == s)
            def _():
                outs[t][...] = (own, landed)[s % 2][:, (s // 2) * half : (s // 2 + 1) * half]


def mixed_rows(gate, text, shares):
    x = [share[...].astype(F32) for share in shares]
    update = (x[0] + x[1]) + (x[2] + x[3])
    return (text[...].astype(F32) + gate[0] * update).astype(BF16)


def give_kernel(gate, text, *refs):
    refs[CHIPS][...] = mixed_rows(gate, text, refs[:CHIPS])


def last_kernel(where, gate, text, back, *refs):
    shares, out = refs[:CHIPS], refs[CHIPS]
    core = where[1]
    half = text.shape[1]
    out[:, block(core, half)] = mixed_rows(gate, text, shares)
    out[:, block(1 - core, half)] = back[...]


def paired(
    text,
    input_gain,
    q_weight,
    kv_weight,
    o_weight,
    q_gain,
    k_gain,
    attn_gate,
    vision,
    segment_ids,
    seg_images,
    image_slot,
):
    ctx_count = lax.axis_size("ctx")
    place, plane = lax.axis_index("ctx"), lax.axis_index("img")
    chip, core = place // 2, place % 2
    where = jnp.stack((chip, core, plane)).astype(jnp.int32)
    tokens, width = text.shape
    head_dim = q_gain.shape[0]
    rows_dev, cols_plane = q_weight.shape
    half = cols_plane // 2
    part = 2 * rows_dev
    slots_here, vt_dev = vision.shape[:2]
    vis_here = slots_here * vt_dev
    kv_cols = kv_weight.shape[1] // 2

    def shape(rows, cols, kind=BF16):
        return jax.ShapeDtypeStruct((rows, cols), kind)

    def swap(x):
        return lax.ppermute(x, "ctx", [(k, k ^ 1) for k in range(ctx_count)])

    def peer(x, s):
        return lax.ppermute(x, "ctx", [(k, k ^ (2 * s)) for k in range(ctx_count)])

    def along_x(x):
        return peer(x, 1)

    def along_y(x):
        return peer(x, 2)

    def across(x, t):
        return lax.ppermute(x, "img", [(k, k ^ t) for k in range(CHIPS)])

    steps = range(1, CHIPS)
    vis = vision.reshape(vis_here, width)
    kv_other = swap(kv_weight)

    anywhere = pl.BlockSpec(memory_space=pl.ANY)
    *vis_pieces, far, q_keep, q_give = call(
        start_kernel,
        (where, text, input_gain[None], vis, q_weight),
        [SMEM, anywhere, VMEM, anywhere, anywhere],
        [shape(vis_here, part)] * CHIPS
        + [shape(tokens, width // 2)]
        + [shape(rows_dev, half)] * 2,
        scratch=[
            pltpu.VMEM((tokens, width), BF16),
            pltpu.VMEM((vis_here, width), BF16),
            pltpu.VMEM((tokens, 128), F32),
            pltpu.SemaphoreType.DMA((3 + tokens // 16,)),
        ],
        flops=8 * tokens * width,
        size=4 * 2**20,
        name="start",
        limit=60,
    )
    vis_own = [vis_pieces[0]] + [peer(vis_pieces[s], s) for s in steps]
    vis_other = [swap(x) for x in vis_own]
    q_keep_sent, far, _ = lax.optimization_barrier((q_keep, far, vis_own))
    q_side, q_other = along_x(q_keep_sent), swap(q_give)
    far = along_y(far)

    shares = call(
        kv_kernel,
        (where, *vis_own, *vis_other, kv_weight, kv_other),
        [SMEM] + [VMEM] * (1 + 2 * CHIPS) + [pl.BlockSpec(memory_space=pl.ANY)],
        [shape(2 * vis_here, kv_cols, F32)] * CHIPS,
        scratch=[
            pltpu.VMEM((rows_dev, kv_cols), BF16),
            pltpu.VMEM((8 * vis_here, kv_cols), F32),
            pltpu.SemaphoreType.DMA((CHIPS,)),
        ],
        flops=4 * vis_here * ctx_count * part * kv_cols,
        size=4 * 2**20,
        name="kv_shares",
    )
    where_near, _ = lax.optimization_barrier((where, shares[0]))
    near, text_keep, text_give = call(
        near_kernel,
        (where_near, text, input_gain[None]),
        [SMEM, VMEM, VMEM],
        [shape(tokens, width // 2)] + [shape(tokens, half)] * 2,
        scratch=[pltpu.VMEM((tokens, 128), F32)],
        flops=8 * tokens * width,
        size=4 * 2**20,
        name="near",
    )
    shares = [shares[0]] + [peer(shares[s], s) for s in steps]
    shares, q_side, far, near = lax.optimization_barrier((shares, q_side, far, near))
    here, there, give = call(
        kv_norm_kernel,
        (where, k_gain[None], *shares),
        [SMEM] + [VMEM] * (1 + CHIPS),
        [shape(2 * vis_here, 2 * head_dim)] * 2 + [shape(4 * vis_here, 2 * head_dim)],
        name="kv_norm",
    )
    blocks = ((far, swap(far)), (near, swap(near)))
    early = [
        call(
            early_kernel,
            (where, *pair, q_keep, q_other),
            [SMEM] + [VMEM] * 4,
            [shape(2 * tokens, half, F32)],
            flops=4 * tokens * part * half,
            size=2 * 2**20,
            name="q_early",
        )[0]
        for pair in blocks
    ]
    kv_z = across(give, 1)
    kv_z, early[0] = lax.optimization_barrier((kv_z, early[0]))
    turn = call(
        kv_turn_kernel,
        (there, kv_z),
        [VMEM] * 2,
        [shape(4 * vis_here, 2 * head_dim)],
        name="kv_turn",
    )[0]
    kv_first = call(
        kv_join_kernel,
        (here, kv_z, across(turn, 2)),
        [VMEM] * 3,
        [shape(8 * vis_here, 2 * head_dim)],
        name="kv_join",
    )[0]
    kv_all = [kv_first] + [peer(kv_first, s) for s in steps]

    q_behind, _ = lax.optimization_barrier((q_other, shares[0]))
    q_corner = along_x(q_behind)

    o_early, _ = lax.optimization_barrier((o_weight[:half], here))
    o_early = along_y(o_early)
    early[1], o_early = lax.optimization_barrier((early[1], o_early))
    q_far, q_first = [
        call(
            late_kernel,
            (where, *blocks[k], q_side, q_corner, early[k]),
            [SMEM] + [VMEM] * 5,
            [shape(2 * tokens, half, kind)],
            flops=4 * tokens * part * half,
            size=2 * 2**20,
            name="q_late",
        )[0]
        for k, kind in ((0, BF16), (1, F32))
    ]
    q_sent, kv_all[2] = lax.optimization_barrier((q_far, kv_all[2]))
    landed = along_y(q_sent)
    o_late, _ = lax.optimization_barrier((o_weight[half:], q_sent))
    o_late = along_y(o_late)

    ids = jnp.concatenate((segment_ids, swap(segment_ids)))
    images = jnp.arange(image_slot.shape[0])
    slot_of = jnp.sum(
        jnp.where(seg_images[:, :, None] == images, image_slot[None, None, :], 0), axis=2
    )
    numbers = jnp.arange(seg_images.shape[0])
    own_slots = jnp.sum(
        jnp.where((ids[:, None] == numbers)[:, :, None], slot_of[None], 0), axis=1
    )
    key_rows = jnp.arange(CHIPS * CHIPS * 2 * vis_here)
    key_plane = plane ^ (key_rows // (2 * vis_here) % CHIPS)
    key_slot = key_plane * slots_here + key_rows // vt_dev % slots_here
    sees = jnp.any(own_slots[:, :, None] == key_slot, axis=1)
    bias = jnp.where(sees, 0.0, NEG).astype(F32)

    context = call(
        attend_kernel,
        (q_gain[None], q_first, landed, *kv_all, bias),
        [VMEM] * (4 + CHIPS),
        [shape(2 * tokens, half)],
        flops=8 * tokens * half * bias.shape[1],
        size=2 * 2**20,
        name="attend",
    )[0]

    context_x = along_x(context)
    shares = [
        call(
            out_kernel,
            (where, x, swap(x), o_weight, o_early, o_late),
            [SMEM] + [VMEM] * 5,
            [shape(tokens, 2 * half)] * 2,
            flops=8 * tokens * cols_plane * half,
            size=2 * 2**20,
            name="o_share",
        )
        for x in (context_x, context)
    ]
    summands = []
    for rows in (1, 0):
        picked = call(
            pick_kernel,
            (where, shares[1][rows], along_x(shares[0][rows])),
            [SMEM] + [VMEM] * 2,
            [shape(tokens, half)] * CHIPS,
            flops=2**20,
            size=2**20,
            name="pick",
        )
        summands.append([picked[0]] + [across(picked[t], t) for t in steps])
    gate = jnp.tanh(attn_gate)
    give = call(
        give_kernel,
        (gate, swap(text_give), *summands[0]),
        [SMEM] + [VMEM] * (1 + CHIPS),
        [shape(tokens, half)],
        flops=2**20,
        size=2**20,
        name="mix_give",
    )[0]
    return call(
        last_kernel,
        (where, gate, text_keep, swap(give), *summands[1]),
        [SMEM, SMEM] + [VMEM] * (2 + CHIPS),
        [shape(tokens, 2 * half)],
        flops=2**20,
        size=2**20,
        name="mix_keep",
    )[0]


def solution(mesh):
    fits = mesh.shape["img"] == 4 and mesh.shape["ctx"] == 8
    return jax.shard_map(
        paired if fits else general,
        mesh=mesh,
        in_specs=(
            P("ctx", None),
            P(),
            P("ctx", "img"),
            P("ctx", None),
            P("img", "ctx"),
            P(),
            P(),
            P(),
            P("img", "ctx", None),
            P("ctx"),
            P(),
            P(),
        ),
        out_specs=P("ctx", "img"),
        check_vma=False,
    )
```

```python
import jax
import jax.numpy as jnp
from jax import lax
from jax.experimental import pallas as pl
from jax.experimental.pallas import tpu as pltpu
from jax.sharding import PartitionSpec as P

KVH = 8


EPS = 1e-05
NEG = -1e30


def head_norm(values, gain):
    mean_sq = jnp.mean(values * values, axis=-1, keepdims=True)
    return values * lax.rsqrt(mean_sq + EPS) * gain


def attend(query, keys, values, mask):
    scale = query.shape[-1] ** (-0.5)
    scores = jnp.einsum("tkgd,nkd->tkgn", query, keys, preferred_element_type=jnp.float32) * scale
    live = mask[:, None, None, :]
    scores = jnp.where(live, scores, NEG)
    top = jnp.max(scores, axis=-1)
    weights = jnp.where(live, jnp.exp(scores - top[..., None]), 0.0)
    total = jnp.sum(weights, axis=-1)
    acc = jnp.einsum(
        "tkgn,nkd->tkgd", weights.astype(jnp.bfloat16), values, preferred_element_type=jnp.float32
    )
    return acc / total[..., None]


def general(
    text,
    input_gain,
    q_weight,
    kv_weight,
    o_weight,
    q_gain,
    k_gain,
    attn_gate,
    vision,
    segment_ids,
    seg_images,
    image_slot,
):
    tokens_here = text.shape[0]
    head_dim = q_gain.shape[0]
    ctx_count = lax.axis_size("ctx")
    img_count = lax.axis_size("img")
    heads_here = q_weight.shape[1] // head_dim
    kv_heads = max(1, KVH // img_count)
    group = heads_here // kv_heads
    slots_here, vt_dev = vision.shape[:2]
    rows_here = slots_here * vt_dev

    o_full = lax.all_gather(o_weight, "ctx", axis=1, tiled=True)
    vision_cols = lax.all_to_all(
        vision.reshape(rows_here, -1), "ctx", split_axis=1, concat_axis=0, tiled=True
    )
    hidden = head_norm(text.astype(jnp.float32), input_gain).astype(jnp.bfloat16)
    hidden_cols = lax.all_to_all(hidden, "ctx", split_axis=1, concat_axis=0, tiled=True)

    kv_share = jnp.dot(vision_cols, kv_weight, preferred_element_type=jnp.float32)
    kv_shares = lax.all_to_all(
        kv_share.reshape(ctx_count, rows_here, -1), "ctx", split_axis=0, concat_axis=0, tiled=True
    )
    projected = jnp.sum(kv_shares, axis=0).reshape(rows_here, KVH, 2, head_dim)
    keys = head_norm(projected[:, :, 0], k_gain).astype(jnp.bfloat16)
    values = projected[:, :, 1].astype(jnp.bfloat16)
    kv_rows = jnp.stack((keys, values), axis=2)
    owners = jnp.arange(img_count)[:, None] * KVH // img_count + jnp.arange(kv_heads)[None, :]
    kv_out = jnp.take(kv_rows, owners, axis=1).transpose(1, 0, 2, 3, 4)
    kv_in = lax.all_to_all(kv_out, "img", split_axis=0, concat_axis=0, tiled=True)
    kv_all = lax.all_gather(kv_in, "ctx", axis=0, tiled=False)

    q_share = jnp.dot(hidden_cols, q_weight, preferred_element_type=jnp.float32)
    q_shares = lax.all_to_all(
        q_share.astype(jnp.bfloat16).reshape(ctx_count, tokens_here, -1),
        "ctx",
        split_axis=0,
        concat_axis=0,
        tiled=True,
    )
    query = jnp.sum(q_shares.astype(jnp.float32), axis=0)
    query = head_norm(query.reshape(tokens_here, kv_heads, group, head_dim), q_gain).astype(
        jnp.bfloat16
    )

    slots = img_count * slots_here
    own_slots = jnp.take(image_slot, jnp.take(seg_images, segment_ids, axis=0), axis=0)
    slot_ids = jnp.arange(slots, dtype=jnp.int32)
    sees = jnp.any(own_slots[:, :, None] == slot_ids[None, None, :], axis=1)
    flat = kv_all.reshape(ctx_count * slots * vt_dev, kv_heads, 2, head_dim)
    mask = jnp.broadcast_to(
        sees[:, None, :, None], (tokens_here, ctx_count, slots, vt_dev)
    ).reshape(tokens_here, -1)
    context = attend(query, flat[:, :, 0], flat[:, :, 1], mask)
    context = context.astype(jnp.bfloat16).reshape(tokens_here, heads_here * head_dim)
    partial_terms = jnp.dot(context, o_full, preferred_element_type=jnp.float32)
    width = partial_terms.shape[1] // img_count
    shares = lax.all_to_all(
        partial_terms.astype(jnp.bfloat16).reshape(tokens_here, img_count, width),
        "img",
        split_axis=1,
        concat_axis=1,
        tiled=True,
    )
    update = jnp.sum(shares.astype(jnp.float32), axis=1)
    own_text = lax.dynamic_slice_in_dim(text, lax.axis_index("img") * width, width, 1)
    return (own_text.astype(jnp.float32) + jnp.tanh(attn_gate[0]) * update).astype(jnp.bfloat16)


BF16, F32 = jnp.bfloat16, jnp.float32
SMEM = pl.BlockSpec(memory_space=pltpu.SMEM)
VMEM = pl.BlockSpec(memory_space=pltpu.VMEM)
CHIPS = 4


def call(kernel, args, specs, outs, out_specs=None, scratch=(), flops=0, size=0, name=None, grid=(), limit=24):
    return pl.pallas_call(
        kernel,
        out_shape=outs,
        in_specs=specs,
        out_specs=[VMEM] * len(outs) if out_specs is None else out_specs,
        scratch_shapes=scratch,
        grid=grid,
        compiler_params=pltpu.CompilerParams(vmem_limit_bytes=limit * 2**20),
        cost_estimate=pl.CostEstimate(flops=flops, bytes_accessed=size, transcendentals=0),
        name=name,
    )(*args)


def block(index, size):
    return pl.ds(pl.multiple_of(index * size, size), size)


def row_scales(text, scale, step):
    for r in range(0, text.shape[0], step):
        x = text[r : r + step, :].astype(F32)
        mean_sq = jnp.mean(x * x, axis=-1, keepdims=True)
        scale[r : r + step, :] = jnp.broadcast_to(lax.rsqrt(mean_sq + EPS), (step, 128))


def scaled(text, scale, gain, out, index, step):
    cols = block(index, out.shape[1])
    row_gain = gain[:, cols]
    for r in range(0, text.shape[0], step):
        x = text[r : r + step, cols].astype(F32)
        out[r : r + step, :] = (x * scale[r : r + step, 0:1] * row_gain).astype(BF16)


def spread_kernel(where, text, gain, near, far, text_keep, text_give, scale):
    chip, core, plane = where[0], where[1], where[2]
    half = text_keep.shape[1]
    row_scales(text, scale, 16)
    scaled(text, scale, gain, far, 1 - chip // 2, 16)
    scaled(text, scale, gain, near, chip // 2, 16)
    text_keep[...] = text[:, block(2 * plane + core, half)]
    text_give[...] = text[:, block(2 * plane + 1 - core, half)]


def kv_kernel(where, *refs):
    vis, vis_other, refs = refs[:CHIPS], refs[CHIPS : 2 * CHIPS], refs[2 * CHIPS :]
    (kv_own, kv_other), refs = refs[:2], refs[2:]
    shares, (other, near_total, sems) = refs[:CHIPS], refs[CHIPS:]
    core = where[1]
    rows = kv_own.shape[0]
    head = kv_own.shape[1] // (2 * CHIPS)
    copies = []
    for j in range(CHIPS):
        copies.append(
            pltpu.make_async_copy(
                kv_other.at[:, block(2 * j + core, head)],
                other.at[:, pl.ds(j * head, head)],
                sems.at[j],
            )
        )
        copies[-1].start()
    first = 2 * where[0]
    near, far = block(first + core, rows), block(first + 1 - core, rows)
    x_near = jnp.concatenate([x[:, near] for x in vis + vis_other], axis=0)
    x_far = jnp.concatenate([x[:, far] for x in vis + vis_other], axis=0)
    count = vis[0].shape[0]
    total = CHIPS * count
    for j in range(CHIPS):
        near_total[:, j * head : (j + 1) * head] = jnp.dot(
            x_near, kv_own[:, block(2 * j + core, head)], preferred_element_type=F32
        )
    for j in range(CHIPS):
        copies[j].wait()
        cols = slice(j * head, (j + 1) * head)
        out = near_total[:, cols] + jnp.dot(x_far, other[:, cols], preferred_element_type=F32)
        for s in range(CHIPS):
            shares[s][:count, cols] = out[s * count : (s + 1) * count]
            shares[s][count:, cols] = out[total + s * count : total + (s + 1) * count]


def kv_norm_kernel(where, k_gain, *refs):
    shares, (here, there, give) = refs[:CHIPS], refs[CHIPS:]
    plane = where[2]
    lines, head = here.shape
    dim = head // 2
    for t, (out, row) in enumerate(((here, 0), (give, 0), (there, 0), (give, lines))):
        cols = block(plane ^ t, head)
        total = (shares[0][:, cols] + shares[1][:, cols]) + (shares[2][:, cols] + shares[3][:, cols])
        keys = head_norm(total[:, :dim], k_gain[...])
        out[row : row + lines, :dim] = keys.astype(BF16)
        out[row : row + lines, dim:] = total[:, dim:].astype(BF16)


def kv_turn_kernel(there, landed, out):
    lines = there.shape[0]
    out[:lines, :] = there[...]
    out[lines:, :] = landed[lines:, :]


def kv_join_kernel(here, landed, last, out):
    lines = here.shape[0]
    out[:lines, :] = here[...]
    out[lines : 2 * lines, :] = landed[:lines, :]
    out[2 * lines :, :] = last[...]


def query_share(index, own, other, first, second, core):
    rows, width = first.shape
    half = block(core, width // 2)
    total = None
    for weight, k in ((first, index), (second, index ^ 1)):
        cols = block(k, rows)
        x = jnp.concatenate((own[:, cols], other[:, cols]), axis=0)
        share = jnp.dot(x, weight[:, half], preferred_element_type=F32)
        total = share if total is None else total + share
    return total


def early_kernel(where, own, other, q_own, q_other, out):
    index = 2 * lax.rem(where[0], 2) + where[1]
    out[...] = query_share(index, own, other, q_own, q_other, where[1])


def late_kernel(where, own, other, q_side, q_corner, early, out):
    index = (2 * lax.rem(where[0], 2) + where[1]) ^ 2
    share = early[...] + query_share(index, own, other, q_side, q_corner, where[1])
    out[...] = share.astype(out.dtype)


def attend_kernel(q_gain, first, landed, *refs):
    kv, (bias, context) = refs[:CHIPS], refs[CHIPS:]
    dim = q_gain.shape[1]
    rows, half = context.shape
    keys = jnp.concatenate([x[:, :dim] for x in kv], axis=0)
    values = jnp.concatenate([x[:, dim:] for x in kv], axis=0)
    step = 128
    for r in range(0, rows, step):
        for g in range(half // dim):
            cols = slice(g * dim, (g + 1) * dim)
            query = first[r : r + step, cols] + landed[r : r + step, cols].astype(F32)
            query = head_norm(query, q_gain[...]).astype(BF16)
            scores = lax.dot_general(
                query, keys, (((1,), (1,)), ((), ())), preferred_element_type=F32
            )
            scores = scores * dim ** (-0.5) + bias[r : r + step, :]
            weights = jnp.exp(scores - jnp.max(scores, axis=-1, keepdims=True))
            total = jnp.sum(weights, axis=-1, keepdims=True)
            acc = jnp.dot(weights.astype(BF16), values, preferred_element_type=F32)
            context[r : r + step, cols] = (acc / total).astype(BF16)


def out_kernel(where, near, far, o_own, o_early, o_late, own, other):
    core = where[1]
    tokens, width = own.shape
    half = near.shape[1]
    turned = jnp.concatenate((far[tokens:, :], far[:tokens, :]), axis=0)
    share = jnp.dot(near[...], o_own[block(core, half), :], preferred_element_type=F32)
    share += jnp.dot(turned, o_own[block(1 - core, half), :], preferred_element_type=F32)
    own[:, : width // 2] = share[:tokens].astype(BF16)
    other[:, : width // 2] = share[tokens:].astype(BF16)
    top = jnp.where(core == 0, near[...], turned)
    low = jnp.where(core == 0, turned, near[...])
    share = jnp.dot(top, o_early[...], preferred_element_type=F32)
    share += jnp.dot(low, o_late[...], preferred_element_type=F32)
    own[:, width // 2 :] = share[:tokens].astype(BF16)
    other[:, width // 2 :] = share[tokens:].astype(BF16)


def pick_kernel(where, own, landed, *outs):
    first = where[0] ^ where[2]
    half = outs[0].shape[1]
    for t in range(CHIPS):
        for s in range(CHIPS):

            @pl.when((first ^ t) == s)
            def _():
                outs[t][...] = (own, landed)[s // 2][:, (s % 2) * half : (s % 2 + 1) * half]


def mixed_rows(gate, text, shares):
    x = [share[...].astype(F32) for share in shares]
    update = (x[0] + x[1]) + (x[2] + x[3])
    return (text[...].astype(F32) + gate[0] * update).astype(BF16)


def give_kernel(gate, text, *refs):
    refs[CHIPS][...] = mixed_rows(gate, text, refs[:CHIPS])


def last_kernel(where, gate, text, back, *refs):
    shares, out = refs[:CHIPS], refs[CHIPS]
    core = where[1]
    half = text.shape[1]
    out[:, block(core, half)] = mixed_rows(gate, text, shares)
    out[:, block(1 - core, half)] = back[...]


def paired(
    text,
    input_gain,
    q_weight,
    kv_weight,
    o_weight,
    q_gain,
    k_gain,
    attn_gate,
    vision,
    segment_ids,
    seg_images,
    image_slot,
):
    ctx_count = lax.axis_size("ctx")
    place, plane = lax.axis_index("ctx"), lax.axis_index("img")
    chip, core = place // 2, place % 2
    where = jnp.stack((chip, core, plane)).astype(jnp.int32)
    tokens, width = text.shape
    head_dim = q_gain.shape[0]
    rows_dev, cols_plane = q_weight.shape
    half = cols_plane // 2
    part = 2 * rows_dev
    slots_here, vt_dev = vision.shape[:2]
    vis_here = slots_here * vt_dev
    kv_cols = kv_weight.shape[1] // 2

    def shape(rows, cols, kind=BF16):
        return jax.ShapeDtypeStruct((rows, cols), kind)

    def swap(x):
        return lax.ppermute(x, "ctx", [(k, k ^ 1) for k in range(ctx_count)])

    def peer(x, s):
        return lax.ppermute(x, "ctx", [(k, k ^ (2 * s)) for k in range(ctx_count)])

    def along_x(x):
        return peer(x, 1)

    def along_y(x):
        return peer(x, 2)

    def across(x, t):
        return lax.ppermute(x, "img", [(k, k ^ t) for k in range(CHIPS)])

    steps = range(1, CHIPS)
    vis = vision.reshape(vis_here, width)
    kv_other = swap(kv_weight)

    vis_own = [vis] + [peer(vis, s) for s in (1, 3, 2)]
    vis_own = [vis_own[0], vis_own[1], vis_own[3], vis_own[2]]
    vis_other = [swap(x) for x in vis_own]
    q_other = swap(q_weight)
    q_sent, _ = lax.optimization_barrier((q_weight, (vis_own[1], vis_own[3])))
    q_side = along_x(q_sent)

    where_text, _ = lax.optimization_barrier((where, vis_own[1]))
    near, far, text_keep, text_give = call(
        spread_kernel,
        (where_text, text, input_gain[None]),
        [SMEM] + [VMEM] * 2,
        [shape(tokens, width // 2)] * 2 + [shape(tokens, half)] * 2,
        scratch=[pltpu.VMEM((tokens, 128), F32)],
        flops=8 * tokens * width,
        size=4 * 2**20,
        name="spread",
    )
    far, _ = lax.optimization_barrier((far, vis_own[2]))
    far = along_y(far)

    shares = call(
        kv_kernel,
        (where, *vis_own, *vis_other, kv_weight, kv_other),
        [SMEM] + [VMEM] * (1 + 2 * CHIPS) + [pl.BlockSpec(memory_space=pl.ANY)],
        [shape(2 * vis_here, kv_cols, F32)] * CHIPS,
        scratch=[
            pltpu.VMEM((rows_dev, kv_cols), BF16),
            pltpu.VMEM((8 * vis_here, kv_cols), F32),
            pltpu.SemaphoreType.DMA((CHIPS,)),
        ],
        flops=4 * vis_here * ctx_count * part * kv_cols,
        size=4 * 2**20,
        name="kv_shares",
    )
    shares = [shares[0]] + [peer(shares[s], s) for s in steps]
    shares, far, q_side = lax.optimization_barrier((shares, far, q_side))
    q_corner = swap(q_side)
    here, there, give = call(
        kv_norm_kernel,
        (where, k_gain[None], *shares),
        [SMEM] + [VMEM] * (1 + CHIPS),
        [shape(2 * vis_here, 2 * head_dim)] * 2 + [shape(4 * vis_here, 2 * head_dim)],
        name="kv_norm",
    )
    blocks = ((far, swap(far)), (near, swap(near)))
    early = [
        call(
            early_kernel,
            (where, *pair, q_weight, q_other),
            [SMEM] + [VMEM] * 4,
            [shape(2 * tokens, half, F32)],
            flops=4 * tokens * part * half,
            size=2 * 2**20,
            name="q_early",
        )[0]
        for pair in blocks
    ]
    o_early, _ = lax.optimization_barrier((o_weight[:half], here))
    o_early = along_x(o_early)
    early[1], o_early = lax.optimization_barrier((early[1], o_early))
    q_far, q_first = [
        call(
            late_kernel,
            (where, *blocks[k], q_side, q_corner, early[k]),
            [SMEM] + [VMEM] * 5,
            [shape(2 * tokens, half, kind)],
            flops=4 * tokens * part * half,
            size=2 * 2**20,
            name="q_late",
        )[0]
        for k, kind in ((0, BF16), (1, F32))
    ]
    kv_z, q_far = lax.optimization_barrier((across(give, 1), q_far))
    turn = call(
        kv_turn_kernel,
        (there, kv_z),
        [VMEM] * 2,
        [shape(4 * vis_here, 2 * head_dim)],
        name="kv_turn",
    )[0]
    kv_first = call(
        kv_join_kernel,
        (here, kv_z, across(turn, 2)),
        [VMEM] * 3,
        [shape(8 * vis_here, 2 * head_dim)],
        name="kv_join",
    )[0]
    kv_all = [kv_first] + [peer(kv_first, s) for s in steps]


    landed = along_y(q_far)
    o_late, _ = lax.optimization_barrier((o_weight[half:], kv_all[1]))
    o_late = along_x(o_late)

    ids = jnp.concatenate((segment_ids, swap(segment_ids)))
    images = jnp.arange(image_slot.shape[0])
    slot_of = jnp.sum(
        jnp.where(seg_images[:, :, None] == images, image_slot[None, None, :], 0), axis=2
    )
    numbers = jnp.arange(seg_images.shape[0])
    own_slots = jnp.sum(
        jnp.where((ids[:, None] == numbers)[:, :, None], slot_of[None], 0), axis=1
    )
    key_rows = jnp.arange(CHIPS * CHIPS * 2 * vis_here)
    key_plane = plane ^ (key_rows // (2 * vis_here) % CHIPS)
    key_slot = key_plane * slots_here + key_rows // vt_dev % slots_here
    sees = jnp.any(own_slots[:, :, None] == key_slot, axis=1)
    bias = jnp.where(sees, 0.0, NEG).astype(F32)

    context = call(
        attend_kernel,
        (q_gain[None], q_first, landed, *kv_all, bias),
        [VMEM] * (4 + CHIPS),
        [shape(2 * tokens, half)],
        flops=8 * tokens * half * bias.shape[1],
        size=2 * 2**20,
        name="attend",
    )[0]

    context_y = along_y(context)
    shares = [
        call(
            out_kernel,
            (where, x, swap(x), o_weight, o_early, o_late),
            [SMEM] + [VMEM] * 5,
            [shape(tokens, 2 * half)] * 2,
            flops=8 * tokens * cols_plane * half,
            size=2 * 2**20,
            name="o_share",
        )
        for x in (context_y, context)
    ]
    summands = []
    for rows in (1, 0):
        picked = call(
            pick_kernel,
            (where, shares[1][rows], along_y(shares[0][rows])),
            [SMEM] + [VMEM] * 2,
            [shape(tokens, half)] * CHIPS,
            flops=2**20,
            size=2**20,
            name="pick",
        )
        summands.append([picked[0]] + [across(picked[t], t) for t in steps])
    gate = jnp.tanh(attn_gate)
    give = call(
        give_kernel,
        (gate, swap(text_give), *summands[0]),
        [SMEM] + [VMEM] * (1 + CHIPS),
        [shape(tokens, half)],
        flops=2**20,
        size=2**20,
        name="mix_give",
    )[0]
    return call(
        last_kernel,
        (where, gate, text_keep, swap(give), *summands[1]),
        [SMEM, SMEM] + [VMEM] * (2 + CHIPS),
        [shape(tokens, 2 * half)],
        flops=2**20,
        size=2**20,
        name="mix_keep",
    )[0]


def solution(mesh):
    fits = mesh.shape["img"] == 4 and mesh.shape["ctx"] == 8
    return jax.shard_map(
        paired if fits else general,
        mesh=mesh,
        in_specs=(
            P("ctx", None),
            P(),
            P("ctx", "img"),
            P("ctx", None),
            P("img", "ctx"),
            P(),
            P(),
            P(),
            P("img", "ctx", None),
            P("ctx"),
            P(),
            P(),
        ),
        out_specs=P("ctx", "img"),
        check_vma=False,
    )
```

```python
import jax
import jax.numpy as jnp
from jax import lax
from jax.experimental import pallas as pl
from jax.experimental.pallas import tpu as pltpu
from jax.sharding import PartitionSpec as P

KVH = 8


EPS = 1e-05
NEG = -1e30


def head_norm(values, gain):
    mean_sq = jnp.mean(values * values, axis=-1, keepdims=True)
    return values * lax.rsqrt(mean_sq + EPS) * gain


def attend(query, keys, values, mask):
    scale = query.shape[-1] ** (-0.5)
    scores = jnp.einsum("tkgd,nkd->tkgn", query, keys, preferred_element_type=jnp.float32) * scale
    live = mask[:, None, None, :]
    scores = jnp.where(live, scores, NEG)
    top = jnp.max(scores, axis=-1)
    weights = jnp.where(live, jnp.exp(scores - top[..., None]), 0.0)
    total = jnp.sum(weights, axis=-1)
    acc = jnp.einsum(
        "tkgn,nkd->tkgd", weights.astype(jnp.bfloat16), values, preferred_element_type=jnp.float32
    )
    return acc / total[..., None]


def general(
    text,
    input_gain,
    q_weight,
    kv_weight,
    o_weight,
    q_gain,
    k_gain,
    attn_gate,
    vision,
    segment_ids,
    seg_images,
    image_slot,
):
    tokens_here = text.shape[0]
    head_dim = q_gain.shape[0]
    ctx_count = lax.axis_size("ctx")
    img_count = lax.axis_size("img")
    heads_here = q_weight.shape[1] // head_dim
    kv_heads = max(1, KVH // img_count)
    group = heads_here // kv_heads
    slots_here, vt_dev = vision.shape[:2]
    rows_here = slots_here * vt_dev

    o_full = lax.all_gather(o_weight, "ctx", axis=1, tiled=True)
    vision_cols = lax.all_to_all(
        vision.reshape(rows_here, -1), "ctx", split_axis=1, concat_axis=0, tiled=True
    )
    hidden = head_norm(text.astype(jnp.float32), input_gain).astype(jnp.bfloat16)
    hidden_cols = lax.all_to_all(hidden, "ctx", split_axis=1, concat_axis=0, tiled=True)

    kv_share = jnp.dot(vision_cols, kv_weight, preferred_element_type=jnp.float32)
    kv_shares = lax.all_to_all(
        kv_share.reshape(ctx_count, rows_here, -1), "ctx", split_axis=0, concat_axis=0, tiled=True
    )
    projected = jnp.sum(kv_shares, axis=0).reshape(rows_here, KVH, 2, head_dim)
    keys = head_norm(projected[:, :, 0], k_gain).astype(jnp.bfloat16)
    values = projected[:, :, 1].astype(jnp.bfloat16)
    kv_rows = jnp.stack((keys, values), axis=2)
    owners = jnp.arange(img_count)[:, None] * KVH // img_count + jnp.arange(kv_heads)[None, :]
    kv_out = jnp.take(kv_rows, owners, axis=1).transpose(1, 0, 2, 3, 4)
    kv_in = lax.all_to_all(kv_out, "img", split_axis=0, concat_axis=0, tiled=True)
    kv_all = lax.all_gather(kv_in, "ctx", axis=0, tiled=False)

    q_share = jnp.dot(hidden_cols, q_weight, preferred_element_type=jnp.float32)
    q_shares = lax.all_to_all(
        q_share.astype(jnp.bfloat16).reshape(ctx_count, tokens_here, -1),
        "ctx",
        split_axis=0,
        concat_axis=0,
        tiled=True,
    )
    query = jnp.sum(q_shares.astype(jnp.float32), axis=0)
    query = head_norm(query.reshape(tokens_here, kv_heads, group, head_dim), q_gain).astype(
        jnp.bfloat16
    )

    slots = img_count * slots_here
    own_slots = jnp.take(image_slot, jnp.take(seg_images, segment_ids, axis=0), axis=0)
    slot_ids = jnp.arange(slots, dtype=jnp.int32)
    sees = jnp.any(own_slots[:, :, None] == slot_ids[None, None, :], axis=1)
    flat = kv_all.reshape(ctx_count * slots * vt_dev, kv_heads, 2, head_dim)
    mask = jnp.broadcast_to(
        sees[:, None, :, None], (tokens_here, ctx_count, slots, vt_dev)
    ).reshape(tokens_here, -1)
    context = attend(query, flat[:, :, 0], flat[:, :, 1], mask)
    context = context.astype(jnp.bfloat16).reshape(tokens_here, heads_here * head_dim)
    partial_terms = jnp.dot(context, o_full, preferred_element_type=jnp.float32)
    width = partial_terms.shape[1] // img_count
    shares = lax.all_to_all(
        partial_terms.astype(jnp.bfloat16).reshape(tokens_here, img_count, width),
        "img",
        split_axis=1,
        concat_axis=1,
        tiled=True,
    )
    update = jnp.sum(shares.astype(jnp.float32), axis=1)
    own_text = lax.dynamic_slice_in_dim(text, lax.axis_index("img") * width, width, 1)
    return (own_text.astype(jnp.float32) + jnp.tanh(attn_gate[0]) * update).astype(jnp.bfloat16)


BF16, F32 = jnp.bfloat16, jnp.float32
SMEM = pl.BlockSpec(memory_space=pltpu.SMEM)
VMEM = pl.BlockSpec(memory_space=pltpu.VMEM)
CHIPS = 4


def call(kernel, args, specs, outs, out_specs=None, scratch=(), flops=0, size=0, name=None, grid=(), limit=24):
    return pl.pallas_call(
        kernel,
        out_shape=outs,
        in_specs=specs,
        out_specs=[VMEM] * len(outs) if out_specs is None else out_specs,
        scratch_shapes=scratch,
        grid=grid,
        compiler_params=pltpu.CompilerParams(vmem_limit_bytes=limit * 2**20),
        cost_estimate=pl.CostEstimate(flops=flops, bytes_accessed=size, transcendentals=0),
        name=name,
    )(*args)


def block(index, size):
    return pl.ds(pl.multiple_of(index * size, size), size)


def start_kernel(where, text_hbm, gain, vis_hbm, q_hbm, *refs):
    pieces, refs = refs[:CHIPS], refs[CHIPS:]
    near, far, text_keep, text_give, q_keep, q_give, text, vis, scale, sems = refs
    chip, core, plane = where[0], where[1], where[2]
    tokens, width = text.shape
    part = width // 2
    half = text_keep.shape[1]
    step = 16
    first = pltpu.make_async_copy(vis_hbm, vis, sems.at[0])
    first.start()
    copies = []
    for k, r in enumerate(range(0, tokens, 2 * step)):
        rows = pl.ds(r, 2 * step)
        copies.append(pltpu.make_async_copy(text_hbm.at[rows, :], text.at[rows, :], sems.at[3 + k]))
        copies[-1].start()
    cuts = [
        pltpu.make_async_copy(q_hbm.at[:, block(core, half)], q_keep, sems.at[1]),
        pltpu.make_async_copy(q_hbm.at[:, block(1 - core, half)], q_give, sems.at[2]),
    ]
    for copy in cuts:
        copy.start()
    first.wait()
    for s in range(CHIPS):
        pieces[s][...] = vis[:, block(chip ^ s, pieces[s].shape[1])]
    for r in range(0, tokens, step):
        if r % (2 * step) == 0:
            copies[r // (2 * step)].wait()
        x = text[r : r + step, :].astype(F32)
        mean_sq = jnp.mean(x * x, axis=-1, keepdims=True)
        scale[r : r + step, :] = jnp.broadcast_to(lax.rsqrt(mean_sq + EPS), (step, 128))
    line = chip // 2
    for out, index in ((far, 1 - line), (near, line)):
        cols = block(index, part)
        row_gain = gain[:, cols]
        for r in range(0, tokens, step):
            x = text[r : r + step, cols].astype(F32)
            out[r : r + step, :] = (x * scale[r : r + step, 0:1] * row_gain).astype(BF16)
    text_keep[...] = text[:, block(2 * plane + core, half)]
    text_give[...] = text[:, block(2 * plane + 1 - core, half)]
    for copy in cuts:
        copy.wait()


def kv_kernel(where, vis, vis_other, kv_own, kv_other, *refs):
    shares, (other, near_total, sems) = refs[:CHIPS], refs[CHIPS:]
    core = where[1]
    rows = kv_own.shape[0]
    head = kv_own.shape[1] // (2 * CHIPS)
    copies = []
    for j in range(CHIPS):
        copies.append(
            pltpu.make_async_copy(
                kv_other.at[:, block(2 * j + core, head)],
                other.at[:, pl.ds(j * head, head)],
                sems.at[j],
            )
        )
        copies[-1].start()
    near, far = block(core, rows), block(1 - core, rows)
    x_near = jnp.concatenate((vis[:, near], vis_other[:, near]), axis=0)
    x_far = jnp.concatenate((vis[:, far], vis_other[:, far]), axis=0)
    total = vis.shape[0]
    count = total // CHIPS
    for j in range(CHIPS):
        near_total[:, j * head : (j + 1) * head] = jnp.dot(
            x_near, kv_own[:, block(2 * j + core, head)], preferred_element_type=F32
        )
    for j in range(CHIPS):
        copies[j].wait()
        cols = slice(j * head, (j + 1) * head)
        out = near_total[:, cols] + jnp.dot(x_far, other[:, cols], preferred_element_type=F32)
        for s in range(CHIPS):
            shares[s][:count, cols] = out[s * count : (s + 1) * count]
            shares[s][count:, cols] = out[total + s * count : total + (s + 1) * count]


def kv_norm_kernel(where, k_gain, *refs):
    shares, (here, there, give) = refs[:CHIPS], refs[CHIPS:]
    plane = where[2]
    lines, head = here.shape
    dim = head // 2
    for t, (out, row) in enumerate(((here, 0), (give, 0), (there, 0), (give, lines))):
        cols = block(plane ^ t, head)
        total = (shares[0][:, cols] + shares[1][:, cols]) + (shares[2][:, cols] + shares[3][:, cols])
        keys = head_norm(total[:, :dim], k_gain[...])
        out[row : row + lines, :dim] = keys.astype(BF16)
        out[row : row + lines, dim:] = total[:, dim:].astype(BF16)


def kv_turn_kernel(there, landed, out):
    lines = there.shape[0]
    out[:lines, :] = there[...]
    out[lines:, :] = landed[lines:, :]


def kv_join_kernel(here, landed, last, out):
    lines = here.shape[0]
    out[:lines, :] = here[...]
    out[lines : 2 * lines, :] = landed[:lines, :]
    out[2 * lines :, :] = last[...]


def query_share(index, own, other, first, second, flip):
    rows = first.shape[0]
    total = None
    for weight, k in ((first, index), (second, index ^ flip)):
        cols = block(k, rows)
        x = jnp.concatenate((own[:, cols], other[:, cols]), axis=0)
        share = jnp.dot(x, weight[...], preferred_element_type=F32)
        total = share if total is None else total + share
    return total


def early_kernel(where, own, other, q_keep, q_other, out):
    index = 2 * lax.rem(where[0], 2) + where[1]
    out[...] = query_share(index, own, other, q_keep, q_other, 1)


def late_kernel(where, own, other, q_side, q_corner, early, out):
    index = (2 * lax.rem(where[0], 2) + where[1]) ^ 2
    share = early[...] + query_share(index, own, other, q_side, q_corner, 1)
    out[...] = share.astype(out.dtype)


def attend_kernel(q_gain, first, landed, *refs):
    kv, (bias, context) = refs[:CHIPS], refs[CHIPS:]
    dim = q_gain.shape[1]
    rows, half = context.shape
    keys = jnp.concatenate([x[:, :dim] for x in kv], axis=0)
    values = jnp.concatenate([x[:, dim:] for x in kv], axis=0)
    step = 128
    for r in range(0, rows, step):
        for g in range(half // dim):
            cols = slice(g * dim, (g + 1) * dim)
            query = first[r : r + step, cols] + landed[r : r + step, cols].astype(F32)
            query = head_norm(query, q_gain[...]).astype(BF16)
            scores = lax.dot_general(
                query, keys, (((1,), (1,)), ((), ())), preferred_element_type=F32
            )
            scores = scores * dim ** (-0.5) + bias[r : r + step, :]
            weights = jnp.exp(scores - jnp.max(scores, axis=-1, keepdims=True))
            total = jnp.sum(weights, axis=-1, keepdims=True)
            acc = jnp.dot(weights.astype(BF16), values, preferred_element_type=F32)
            context[r : r + step, cols] = (acc / total).astype(BF16)


def out_kernel(where, near, far, o_own, o_early, o_late, own, other):
    core = where[1]
    tokens, width = own.shape
    half = near.shape[1]
    turned = jnp.concatenate((far[tokens:, :], far[:tokens, :]), axis=0)
    share = jnp.dot(near[...], o_own[block(core, half), :], preferred_element_type=F32)
    share += jnp.dot(turned, o_own[block(1 - core, half), :], preferred_element_type=F32)
    own[:, : width // 2] = share[:tokens].astype(BF16)
    other[:, : width // 2] = share[tokens:].astype(BF16)
    top = jnp.where(core == 0, near[...], turned)
    low = jnp.where(core == 0, turned, near[...])
    share = jnp.dot(top, o_early[...], preferred_element_type=F32)
    share += jnp.dot(low, o_late[...], preferred_element_type=F32)
    own[:, width // 2 :] = share[:tokens].astype(BF16)
    other[:, width // 2 :] = share[tokens:].astype(BF16)


def pick_kernel(where, own, landed, *outs):
    first = where[0] ^ where[2]
    half = outs[0].shape[1]
    for t in range(CHIPS):
        for s in range(CHIPS):

            @pl.when((first ^ t) == s)
            def _():
                outs[t][...] = (own, landed)[s % 2][:, (s // 2) * half : (s // 2 + 1) * half]


def mixed_rows(gate, text, shares):
    x = [share[...].astype(F32) for share in shares]
    update = (x[0] + x[1]) + (x[2] + x[3])
    return (text[...].astype(F32) + gate[0] * update).astype(BF16)


def give_kernel(gate, text, *refs):
    refs[CHIPS][...] = mixed_rows(gate, text, refs[:CHIPS])


def last_kernel(where, gate, text, back, *refs):
    shares, out = refs[:CHIPS], refs[CHIPS]
    core = where[1]
    half = text.shape[1]
    out[:, block(core, half)] = mixed_rows(gate, text, shares)
    out[:, block(1 - core, half)] = back[...]


def paired(
    text,
    input_gain,
    q_weight,
    kv_weight,
    o_weight,
    q_gain,
    k_gain,
    attn_gate,
    vision,
    segment_ids,
    seg_images,
    image_slot,
):
    ctx_count = lax.axis_size("ctx")
    place, plane = lax.axis_index("ctx"), lax.axis_index("img")
    chip, core = place // 2, place % 2
    where = jnp.stack((chip, core, plane)).astype(jnp.int32)
    tokens, width = text.shape
    head_dim = q_gain.shape[0]
    rows_dev, cols_plane = q_weight.shape
    half = cols_plane // 2
    part = 2 * rows_dev
    slots_here, vt_dev = vision.shape[:2]
    vis_here = slots_here * vt_dev
    kv_cols = kv_weight.shape[1] // 2

    def shape(rows, cols, kind=BF16):
        return jax.ShapeDtypeStruct((rows, cols), kind)

    def swap(x):
        return lax.ppermute(x, "ctx", [(k, k ^ 1) for k in range(ctx_count)])

    def peer(x, s):
        return lax.ppermute(x, "ctx", [(k, k ^ (2 * s)) for k in range(ctx_count)])

    def along_x(x):
        return peer(x, 1)

    def along_y(x):
        return peer(x, 2)

    def across(x, t):
        return lax.ppermute(x, "img", [(k, k ^ t) for k in range(CHIPS)])

    steps = range(1, CHIPS)
    vis = vision.reshape(vis_here, width)
    kv_other = swap(kv_weight)

    anywhere = pl.BlockSpec(memory_space=pl.ANY)
    *vis_pieces, near, far, text_keep, text_give, q_keep, q_give = call(
        start_kernel,
        (where, text, input_gain[None], vis, q_weight),
        [SMEM, anywhere, VMEM, anywhere, anywhere],
        [shape(vis_here, part)] * CHIPS
        + [shape(tokens, width // 2)] * 2
        + [shape(tokens, half)] * 2
        + [shape(rows_dev, half)] * 2,
        scratch=[
            pltpu.VMEM((tokens, width), BF16),
            pltpu.VMEM((vis_here, width), BF16),
            pltpu.VMEM((tokens, 128), F32),
            pltpu.SemaphoreType.DMA((3 + tokens // 32,)),
        ],
        flops=8 * tokens * width,
        size=4 * 2**20,
        name="start",
        limit=60,
    )
    vis_own = jnp.concatenate([vis_pieces[0]] + [peer(vis_pieces[s], s) for s in steps])
    vis_other = swap(vis_own)
    q_side, q_other = along_x(q_keep), swap(q_give)
    far = along_y(far)

    shares = call(
        kv_kernel,
        (where, vis_own, vis_other, kv_weight, kv_other),
        [SMEM] + [VMEM] * 3 + [pl.BlockSpec(memory_space=pl.ANY)],
        [shape(2 * vis_here, kv_cols, F32)] * CHIPS,
        scratch=[
            pltpu.VMEM((rows_dev, kv_cols), BF16),
            pltpu.VMEM((8 * vis_here, kv_cols), F32),
            pltpu.SemaphoreType.DMA((CHIPS,)),
        ],
        flops=4 * vis_here * ctx_count * part * kv_cols,
        size=4 * 2**20,
        name="kv_shares",
    )
    shares = [shares[0]] + [peer(shares[s], s) for s in steps]
    shares, q_side, far = lax.optimization_barrier((shares, q_side, far))
    here, there, give = call(
        kv_norm_kernel,
        (where, k_gain[None], *shares),
        [SMEM] + [VMEM] * (1 + CHIPS),
        [shape(2 * vis_here, 2 * head_dim)] * 2 + [shape(4 * vis_here, 2 * head_dim)],
        name="kv_norm",
    )
    blocks = ((far, swap(far)), (near, swap(near)))
    early = [
        call(
            early_kernel,
            (where, *pair, q_keep, q_other),
            [SMEM] + [VMEM] * 4,
            [shape(2 * tokens, half, F32)],
            flops=4 * tokens * part * half,
            size=2 * 2**20,
            name="q_early",
        )[0]
        for pair in blocks
    ]
    kv_z, early[0] = lax.optimization_barrier((across(give, 1), early[0]))
    turn = call(
        kv_turn_kernel,
        (there, kv_z),
        [VMEM] * 2,
        [shape(4 * vis_here, 2 * head_dim)],
        name="kv_turn",
    )[0]
    kv_first = call(
        kv_join_kernel,
        (here, kv_z, across(turn, 2)),
        [VMEM] * 3,
        [shape(8 * vis_here, 2 * head_dim)],
        name="kv_join",
    )[0]
    kv_all = [kv_first] + [peer(kv_first, s) for s in steps]
    q_behind, _ = lax.optimization_barrier((q_other, shares[0]))
    q_corner = along_x(q_behind)
    q_corner, kv_all[1] = lax.optimization_barrier((q_corner, kv_all[1]))

    o_early, _ = lax.optimization_barrier((o_weight[:half], here))
    early[1], o_early = lax.optimization_barrier((early[1], along_y(o_early)))
    q_far, q_first = [
        call(
            late_kernel,
            (where, *blocks[k], q_side, q_corner, early[k]),
            [SMEM] + [VMEM] * 5,
            [shape(2 * tokens, half, kind)],
            flops=4 * tokens * part * half,
            size=2 * 2**20,
            name="q_late",
        )[0]
        for k, kind in ((0, BF16), (1, F32))
    ]
    landed = along_y(q_far)
    o_late, _ = lax.optimization_barrier((o_weight[half:], q_far))
    o_late = along_y(o_late)

    ids = jnp.concatenate((segment_ids, swap(segment_ids)))
    images = jnp.arange(image_slot.shape[0])
    slot_of = jnp.sum(
        jnp.where(seg_images[:, :, None] == images, image_slot[None, None, :], 0), axis=2
    )
    numbers = jnp.arange(seg_images.shape[0])
    own_slots = jnp.sum(
        jnp.where((ids[:, None] == numbers)[:, :, None], slot_of[None], 0), axis=1
    )
    key_rows = jnp.arange(CHIPS * CHIPS * 2 * vis_here)
    key_plane = plane ^ (key_rows // (2 * vis_here) % CHIPS)
    key_slot = key_plane * slots_here + key_rows // vt_dev % slots_here
    sees = jnp.any(own_slots[:, :, None] == key_slot, axis=1)
    bias = jnp.where(sees, 0.0, NEG).astype(F32)

    context = call(
        attend_kernel,
        (q_gain[None], q_first, landed, *kv_all, bias),
        [VMEM] * (4 + CHIPS),
        [shape(2 * tokens, half)],
        flops=8 * tokens * half * bias.shape[1],
        size=2 * 2**20,
        name="attend",
    )[0]

    context_x = along_x(context)
    shares = [
        call(
            out_kernel,
            (where, x, swap(x), o_weight, o_early, o_late),
            [SMEM] + [VMEM] * 5,
            [shape(tokens, 2 * half)] * 2,
            flops=8 * tokens * cols_plane * half,
            size=2 * 2**20,
            name="o_share",
        )
        for x in (context_x, context)
    ]
    summands = []
    for rows in (1, 0):
        picked = call(
            pick_kernel,
            (where, shares[1][rows], along_x(shares[0][rows])),
            [SMEM] + [VMEM] * 2,
            [shape(tokens, half)] * CHIPS,
            flops=2**20,
            size=2**20,
            name="pick",
        )
        summands.append([picked[0]] + [across(picked[t], t) for t in steps])
    gate = jnp.tanh(attn_gate)
    give = call(
        give_kernel,
        (gate, swap(text_give), *summands[0]),
        [SMEM] + [VMEM] * (1 + CHIPS),
        [shape(tokens, half)],
        flops=2**20,
        size=2**20,
        name="mix_give",
    )[0]
    return call(
        last_kernel,
        (where, gate, text_keep, swap(give), *summands[1]),
        [SMEM, SMEM] + [VMEM] * (2 + CHIPS),
        [shape(tokens, 2 * half)],
        flops=2**20,
        size=2**20,
        name="mix_keep",
    )[0]


def solution(mesh):
    fits = mesh.shape["img"] == 4 and mesh.shape["ctx"] == 8
    return jax.shard_map(
        paired if fits else general,
        mesh=mesh,
        in_specs=(
            P("ctx", None),
            P(),
            P("ctx", "img"),
            P("ctx", None),
            P("img", "ctx"),
            P(),
            P(),
            P(),
            P("img", "ctx", None),
            P("ctx"),
            P(),
            P(),
        ),
        out_specs=P("ctx", "img"),
        check_vma=False,
    )
```

```python
import jax
import jax.numpy as jnp
from jax import lax
from jax.experimental import pallas as pl
from jax.experimental.pallas import tpu as pltpu
from jax.sharding import PartitionSpec as P

KVH = 8


EPS = 1e-05
NEG = -1e30


def head_norm(values, gain):
    mean_sq = jnp.mean(values * values, axis=-1, keepdims=True)
    return values * lax.rsqrt(mean_sq + EPS) * gain


def attend(query, keys, values, mask):
    scale = query.shape[-1] ** (-0.5)
    scores = jnp.einsum("tkgd,nkd->tkgn", query, keys, preferred_element_type=jnp.float32) * scale
    live = mask[:, None, None, :]
    scores = jnp.where(live, scores, NEG)
    top = jnp.max(scores, axis=-1)
    weights = jnp.where(live, jnp.exp(scores - top[..., None]), 0.0)
    total = jnp.sum(weights, axis=-1)
    acc = jnp.einsum(
        "tkgn,nkd->tkgd", weights.astype(jnp.bfloat16), values, preferred_element_type=jnp.float32
    )
    return acc / total[..., None]


def general(
    text,
    input_gain,
    q_weight,
    kv_weight,
    o_weight,
    q_gain,
    k_gain,
    attn_gate,
    vision,
    segment_ids,
    seg_images,
    image_slot,
):
    tokens_here = text.shape[0]
    head_dim = q_gain.shape[0]
    ctx_count = lax.axis_size("ctx")
    img_count = lax.axis_size("img")
    heads_here = q_weight.shape[1] // head_dim
    kv_heads = max(1, KVH // img_count)
    group = heads_here // kv_heads
    slots_here, vt_dev = vision.shape[:2]
    rows_here = slots_here * vt_dev

    o_full = lax.all_gather(o_weight, "ctx", axis=1, tiled=True)
    vision_cols = lax.all_to_all(
        vision.reshape(rows_here, -1), "ctx", split_axis=1, concat_axis=0, tiled=True
    )
    hidden = head_norm(text.astype(jnp.float32), input_gain).astype(jnp.bfloat16)
    hidden_cols = lax.all_to_all(hidden, "ctx", split_axis=1, concat_axis=0, tiled=True)

    kv_share = jnp.dot(vision_cols, kv_weight, preferred_element_type=jnp.float32)
    kv_shares = lax.all_to_all(
        kv_share.reshape(ctx_count, rows_here, -1), "ctx", split_axis=0, concat_axis=0, tiled=True
    )
    projected = jnp.sum(kv_shares, axis=0).reshape(rows_here, KVH, 2, head_dim)
    keys = head_norm(projected[:, :, 0], k_gain).astype(jnp.bfloat16)
    values = projected[:, :, 1].astype(jnp.bfloat16)
    kv_rows = jnp.stack((keys, values), axis=2)
    owners = jnp.arange(img_count)[:, None] * KVH // img_count + jnp.arange(kv_heads)[None, :]
    kv_out = jnp.take(kv_rows, owners, axis=1).transpose(1, 0, 2, 3, 4)
    kv_in = lax.all_to_all(kv_out, "img", split_axis=0, concat_axis=0, tiled=True)
    kv_all = lax.all_gather(kv_in, "ctx", axis=0, tiled=False)

    q_share = jnp.dot(hidden_cols, q_weight, preferred_element_type=jnp.float32)
    q_shares = lax.all_to_all(
        q_share.astype(jnp.bfloat16).reshape(ctx_count, tokens_here, -1),
        "ctx",
        split_axis=0,
        concat_axis=0,
        tiled=True,
    )
    query = jnp.sum(q_shares.astype(jnp.float32), axis=0)
    query = head_norm(query.reshape(tokens_here, kv_heads, group, head_dim), q_gain).astype(
        jnp.bfloat16
    )

    slots = img_count * slots_here
    own_slots = jnp.take(image_slot, jnp.take(seg_images, segment_ids, axis=0), axis=0)
    slot_ids = jnp.arange(slots, dtype=jnp.int32)
    sees = jnp.any(own_slots[:, :, None] == slot_ids[None, None, :], axis=1)
    flat = kv_all.reshape(ctx_count * slots * vt_dev, kv_heads, 2, head_dim)
    mask = jnp.broadcast_to(
        sees[:, None, :, None], (tokens_here, ctx_count, slots, vt_dev)
    ).reshape(tokens_here, -1)
    context = attend(query, flat[:, :, 0], flat[:, :, 1], mask)
    context = context.astype(jnp.bfloat16).reshape(tokens_here, heads_here * head_dim)
    partial_terms = jnp.dot(context, o_full, preferred_element_type=jnp.float32)
    width = partial_terms.shape[1] // img_count
    shares = lax.all_to_all(
        partial_terms.astype(jnp.bfloat16).reshape(tokens_here, img_count, width),
        "img",
        split_axis=1,
        concat_axis=1,
        tiled=True,
    )
    update = jnp.sum(shares.astype(jnp.float32), axis=1)
    own_text = lax.dynamic_slice_in_dim(text, lax.axis_index("img") * width, width, 1)
    return (own_text.astype(jnp.float32) + jnp.tanh(attn_gate[0]) * update).astype(jnp.bfloat16)


BF16, F32 = jnp.bfloat16, jnp.float32
SMEM = pl.BlockSpec(memory_space=pltpu.SMEM)
VMEM = pl.BlockSpec(memory_space=pltpu.VMEM)
CHIPS = 4


def call(kernel, args, specs, outs, out_specs=None, scratch=(), flops=0, size=0, name=None, grid=(), limit=24):
    return pl.pallas_call(
        kernel,
        out_shape=outs,
        in_specs=specs,
        out_specs=[VMEM] * len(outs) if out_specs is None else out_specs,
        scratch_shapes=scratch,
        grid=grid,
        compiler_params=pltpu.CompilerParams(vmem_limit_bytes=limit * 2**20),
        cost_estimate=pl.CostEstimate(flops=flops, bytes_accessed=size, transcendentals=0),
        name=name,
    )(*args)


def block(index, size):
    return pl.ds(pl.multiple_of(index * size, size), size)


def start_kernel(where, text_hbm, gain, vis_hbm, q_hbm, *refs):
    pieces, refs = refs[:CHIPS], refs[CHIPS:]
    near, far, text_keep, text_give, q_keep, q_give, text, vis, scale, sems = refs
    chip, core, plane = where[0], where[1], where[2]
    tokens, width = text.shape
    part = width // 2
    half = text_keep.shape[1]
    step = 16
    first = pltpu.make_async_copy(vis_hbm, vis, sems.at[0])
    first.start()
    copies = []
    for k, r in enumerate(range(0, tokens, 2 * step)):
        rows = pl.ds(r, 2 * step)
        copies.append(pltpu.make_async_copy(text_hbm.at[rows, :], text.at[rows, :], sems.at[3 + k]))
        copies[-1].start()
    cuts = [
        pltpu.make_async_copy(q_hbm.at[:, block(core, half)], q_keep, sems.at[1]),
        pltpu.make_async_copy(q_hbm.at[:, block(1 - core, half)], q_give, sems.at[2]),
    ]
    for copy in cuts:
        copy.start()
    first.wait()
    for s in range(CHIPS):
        pieces[s][...] = vis[:, block(chip ^ s, pieces[s].shape[1])]
    for r in range(0, tokens, step):
        if r % (2 * step) == 0:
            copies[r // (2 * step)].wait()
        x = text[r : r + step, :].astype(F32)
        mean_sq = jnp.mean(x * x, axis=-1, keepdims=True)
        scale[r : r + step, :] = jnp.broadcast_to(lax.rsqrt(mean_sq + EPS), (step, 128))
    line = chip // 2
    for out, index in ((far, 1 - line), (near, line)):
        cols = block(index, part)
        row_gain = gain[:, cols]
        for r in range(0, tokens, step):
            x = text[r : r + step, cols].astype(F32)
            out[r : r + step, :] = (x * scale[r : r + step, 0:1] * row_gain).astype(BF16)
    text_keep[...] = text[:, block(2 * plane + core, half)]
    text_give[...] = text[:, block(2 * plane + 1 - core, half)]
    for copy in cuts:
        copy.wait()


def kv_kernel(where, vis, vis_other, kv_own, kv_other, *refs):
    shares, (other, near_total, sems) = refs[:CHIPS], refs[CHIPS:]
    core = where[1]
    rows = kv_own.shape[0]
    head = kv_own.shape[1] // (2 * CHIPS)
    copies = []
    for j in range(CHIPS):
        copies.append(
            pltpu.make_async_copy(
                kv_other.at[:, block(2 * j + core, head)],
                other.at[:, pl.ds(j * head, head)],
                sems.at[j],
            )
        )
        copies[-1].start()
    near, far = block(core, rows), block(1 - core, rows)
    x_near = jnp.concatenate((vis[:, near], vis_other[:, near]), axis=0)
    x_far = jnp.concatenate((vis[:, far], vis_other[:, far]), axis=0)
    total = vis.shape[0]
    count = total // CHIPS
    for j in range(CHIPS):
        near_total[:, j * head : (j + 1) * head] = jnp.dot(
            x_near, kv_own[:, block(2 * j + core, head)], preferred_element_type=F32
        )
    for j in range(CHIPS):
        copies[j].wait()
        cols = slice(j * head, (j + 1) * head)
        out = near_total[:, cols] + jnp.dot(x_far, other[:, cols], preferred_element_type=F32)
        for s in range(CHIPS):
            shares[s][:count, cols] = out[s * count : (s + 1) * count]
            shares[s][count:, cols] = out[total + s * count : total + (s + 1) * count]


def kv_norm_kernel(where, k_gain, *refs):
    shares, (here, there, give) = refs[:CHIPS], refs[CHIPS:]
    plane = where[2]
    lines, head = here.shape
    dim = head // 2
    for t, (out, row) in enumerate(((here, 0), (give, 0), (there, 0), (give, lines))):
        cols = block(plane ^ t, head)
        total = (shares[0][:, cols] + shares[1][:, cols]) + (shares[2][:, cols] + shares[3][:, cols])
        keys = head_norm(total[:, :dim], k_gain[...])
        out[row : row + lines, :dim] = keys.astype(BF16)
        out[row : row + lines, dim:] = total[:, dim:].astype(BF16)


def kv_turn_kernel(there, landed, out):
    lines = there.shape[0]
    out[:lines, :] = there[...]
    out[lines:, :] = landed[lines:, :]


def kv_join_kernel(here, landed, last, out):
    lines = here.shape[0]
    out[:lines, :] = here[...]
    out[lines : 2 * lines, :] = landed[:lines, :]
    out[2 * lines :, :] = last[...]


def query_share(index, own, other, first, second, flip):
    rows = first.shape[0]
    total = None
    for weight, k in ((first, index), (second, index ^ flip)):
        cols = block(k, rows)
        x = jnp.concatenate((own[:, cols], other[:, cols]), axis=0)
        share = jnp.dot(x, weight[...], preferred_element_type=F32)
        total = share if total is None else total + share
    return total


def early_kernel(where, own, other, q_keep, q_other, out):
    index = 2 * lax.rem(where[0], 2) + where[1]
    out[...] = query_share(index, own, other, q_keep, q_other, 1)


def late_kernel(where, own, other, q_side, q_corner, early, out):
    index = (2 * lax.rem(where[0], 2) + where[1]) ^ 2
    share = early[...] + query_share(index, own, other, q_side, q_corner, 1)
    out[...] = share.astype(out.dtype)


def attend_kernel(q_gain, first, landed, *refs):
    kv, (bias, context) = refs[:CHIPS], refs[CHIPS:]
    dim = q_gain.shape[1]
    rows, half = context.shape
    keys = jnp.concatenate([x[:, :dim] for x in kv], axis=0)
    values = jnp.concatenate([x[:, dim:] for x in kv], axis=0)
    step = 128
    for r in range(0, rows, step):
        for g in range(half // dim):
            cols = slice(g * dim, (g + 1) * dim)
            query = first[r : r + step, cols] + landed[r : r + step, cols].astype(F32)
            query = head_norm(query, q_gain[...]).astype(BF16)
            scores = lax.dot_general(
                query, keys, (((1,), (1,)), ((), ())), preferred_element_type=F32
            )
            scores = scores * dim ** (-0.5) + bias[r : r + step, :]
            weights = jnp.exp(scores - jnp.max(scores, axis=-1, keepdims=True))
            total = jnp.sum(weights, axis=-1, keepdims=True)
            acc = jnp.dot(weights.astype(BF16), values, preferred_element_type=F32)
            context[r : r + step, cols] = (acc / total).astype(BF16)


def out_kernel(where, near, far, o_own, o_early, o_late, own, other):
    core = where[1]
    tokens, width = own.shape
    half = near.shape[1]
    turned = jnp.concatenate((far[tokens:, :], far[:tokens, :]), axis=0)
    share = jnp.dot(near[...], o_own[block(core, half), :], preferred_element_type=F32)
    share += jnp.dot(turned, o_own[block(1 - core, half), :], preferred_element_type=F32)
    own[:, : width // 2] = share[:tokens].astype(BF16)
    other[:, : width // 2] = share[tokens:].astype(BF16)
    top = jnp.where(core == 0, near[...], turned)
    low = jnp.where(core == 0, turned, near[...])
    share = jnp.dot(top, o_early[...], preferred_element_type=F32)
    share += jnp.dot(low, o_late[...], preferred_element_type=F32)
    own[:, width // 2 :] = share[:tokens].astype(BF16)
    other[:, width // 2 :] = share[tokens:].astype(BF16)


def pick_kernel(where, own, landed, *outs):
    first = where[0] ^ where[2]
    half = outs[0].shape[1]
    for t in range(CHIPS):
        for s in range(CHIPS):

            @pl.when((first ^ t) == s)
            def _():
                outs[t][...] = (own, landed)[s % 2][:, (s // 2) * half : (s // 2 + 1) * half]


def mixed_rows(gate, text, shares):
    x = [share[...].astype(F32) for share in shares]
    update = (x[0] + x[1]) + (x[2] + x[3])
    return (text[...].astype(F32) + gate[0] * update).astype(BF16)


def give_kernel(gate, text, *refs):
    refs[CHIPS][...] = mixed_rows(gate, text, refs[:CHIPS])


def last_kernel(where, gate, text, back, *refs):
    shares, out = refs[:CHIPS], refs[CHIPS]
    core = where[1]
    half = text.shape[1]
    out[:, block(core, half)] = mixed_rows(gate, text, shares)
    out[:, block(1 - core, half)] = back[...]


def paired(
    text,
    input_gain,
    q_weight,
    kv_weight,
    o_weight,
    q_gain,
    k_gain,
    attn_gate,
    vision,
    segment_ids,
    seg_images,
    image_slot,
):
    ctx_count = lax.axis_size("ctx")
    place, plane = lax.axis_index("ctx"), lax.axis_index("img")
    chip, core = place // 2, place % 2
    where = jnp.stack((chip, core, plane)).astype(jnp.int32)
    tokens, width = text.shape
    head_dim = q_gain.shape[0]
    rows_dev, cols_plane = q_weight.shape
    half = cols_plane // 2
    part = 2 * rows_dev
    slots_here, vt_dev = vision.shape[:2]
    vis_here = slots_here * vt_dev
    kv_cols = kv_weight.shape[1] // 2

    def shape(rows, cols, kind=BF16):
        return jax.ShapeDtypeStruct((rows, cols), kind)

    def swap(x):
        return lax.ppermute(x, "ctx", [(k, k ^ 1) for k in range(ctx_count)])

    def peer(x, s):
        return lax.ppermute(x, "ctx", [(k, k ^ (2 * s)) for k in range(ctx_count)])

    def along_x(x):
        return peer(x, 1)

    def along_y(x):
        return peer(x, 2)

    def across(x, t):
        return lax.ppermute(x, "img", [(k, k ^ t) for k in range(CHIPS)])

    steps = range(1, CHIPS)
    vis = vision.reshape(vis_here, width)
    kv_other = swap(kv_weight)

    anywhere = pl.BlockSpec(memory_space=pl.ANY)
    *vis_pieces, near, far, text_keep, text_give, q_keep, q_give = call(
        start_kernel,
        (where, text, input_gain[None], vis, q_weight),
        [SMEM, anywhere, VMEM, anywhere, anywhere],
        [shape(vis_here, part)] * CHIPS
        + [shape(tokens, width // 2)] * 2
        + [shape(tokens, half)] * 2
        + [shape(rows_dev, half)] * 2,
        scratch=[
            pltpu.VMEM((tokens, width), BF16),
            pltpu.VMEM((vis_here, width), BF16),
            pltpu.VMEM((tokens, 128), F32),
            pltpu.SemaphoreType.DMA((3 + tokens // 32,)),
        ],
        flops=8 * tokens * width,
        size=4 * 2**20,
        name="start",
        limit=60,
    )
    vis_own = jnp.concatenate([vis_pieces[0]] + [peer(vis_pieces[s], s) for s in steps])
    vis_other = swap(vis_own)
    q_side, q_other = along_x(q_keep), swap(q_give)
    far = along_y(far)

    shares = call(
        kv_kernel,
        (where, vis_own, vis_other, kv_weight, kv_other),
        [SMEM] + [VMEM] * 3 + [pl.BlockSpec(memory_space=pl.ANY)],
        [shape(2 * vis_here, kv_cols, F32)] * CHIPS,
        scratch=[
            pltpu.VMEM((rows_dev, kv_cols), BF16),
            pltpu.VMEM((8 * vis_here, kv_cols), F32),
            pltpu.SemaphoreType.DMA((CHIPS,)),
        ],
        flops=4 * vis_here * ctx_count * part * kv_cols,
        size=4 * 2**20,
        name="kv_shares",
    )
    shares = [shares[0]] + [peer(shares[s], s) for s in steps]
    own_share = shares[0]
    shares, q_side, far = lax.optimization_barrier((shares, q_side, far))
    here, there, give = call(
        kv_norm_kernel,
        (where, k_gain[None], *shares),
        [SMEM] + [VMEM] * (1 + CHIPS),
        [shape(2 * vis_here, 2 * head_dim)] * 2 + [shape(4 * vis_here, 2 * head_dim)],
        name="kv_norm",
    )
    blocks = ((far, swap(far)), (near, swap(near)))
    early = [
        call(
            early_kernel,
            (where, *pair, q_keep, q_other),
            [SMEM] + [VMEM] * 4,
            [shape(2 * tokens, half, F32)],
            flops=4 * tokens * part * half,
            size=2 * 2**20,
            name="q_early",
        )[0]
        for pair in blocks
    ]
    kv_z, early[0] = lax.optimization_barrier((across(give, 1), early[0]))
    turn = call(
        kv_turn_kernel,
        (there, kv_z),
        [VMEM] * 2,
        [shape(4 * vis_here, 2 * head_dim)],
        name="kv_turn",
    )[0]
    kv_first = call(
        kv_join_kernel,
        (here, kv_z, across(turn, 2)),
        [VMEM] * 3,
        [shape(8 * vis_here, 2 * head_dim)],
        name="kv_join",
    )[0]
    kv_all = [kv_first] + [peer(kv_first, s) for s in steps]
    q_behind, _ = lax.optimization_barrier((q_other, own_share))
    q_corner = along_x(q_behind)
    q_corner, kv_all[1] = lax.optimization_barrier((q_corner, kv_all[1]))

    o_early, _ = lax.optimization_barrier((o_weight[:half], here))
    q_corner, o_early = lax.optimization_barrier((q_corner, along_y(o_early)))
    q_far, q_first = [
        call(
            late_kernel,
            (where, *blocks[k], q_side, q_corner, early[k]),
            [SMEM] + [VMEM] * 5,
            [shape(2 * tokens, half, kind)],
            flops=4 * tokens * part * half,
            size=2 * 2**20,
            name="q_late",
        )[0]
        for k, kind in ((0, BF16), (1, F32))
    ]
    landed = along_y(q_far)
    o_late, _ = lax.optimization_barrier((o_weight[half:], q_far))
    o_late = along_y(o_late)

    ids = jnp.concatenate((segment_ids, swap(segment_ids)))
    images = jnp.arange(image_slot.shape[0])
    slot_of = jnp.sum(
        jnp.where(seg_images[:, :, None] == images, image_slot[None, None, :], 0), axis=2
    )
    numbers = jnp.arange(seg_images.shape[0])
    own_slots = jnp.sum(
        jnp.where((ids[:, None] == numbers)[:, :, None], slot_of[None], 0), axis=1
    )
    key_rows = jnp.arange(CHIPS * CHIPS * 2 * vis_here)
    key_plane = plane ^ (key_rows // (2 * vis_here) % CHIPS)
    key_slot = key_plane * slots_here + key_rows // vt_dev % slots_here
    sees = jnp.any(own_slots[:, :, None] == key_slot, axis=1)
    bias = jnp.where(sees, 0.0, NEG).astype(F32)

    context = call(
        attend_kernel,
        (q_gain[None], q_first, landed, *kv_all, bias),
        [VMEM] * (4 + CHIPS),
        [shape(2 * tokens, half)],
        flops=8 * tokens * half * bias.shape[1],
        size=2 * 2**20,
        name="attend",
    )[0]

    context_x = along_x(context)
    shares = [
        call(
            out_kernel,
            (where, x, swap(x), o_weight, o_early, o_late),
            [SMEM] + [VMEM] * 5,
            [shape(tokens, 2 * half)] * 2,
            flops=8 * tokens * cols_plane * half,
            size=2 * 2**20,
            name="o_share",
        )
        for x in (context_x, context)
    ]
    summands = []
    for rows in (1, 0):
        picked = call(
            pick_kernel,
            (where, shares[1][rows], along_x(shares[0][rows])),
            [SMEM] + [VMEM] * 2,
            [shape(tokens, half)] * CHIPS,
            flops=2**20,
            size=2**20,
            name="pick",
        )
        summands.append([picked[0]] + [across(picked[t], t) for t in steps])
    gate = jnp.tanh(attn_gate)
    give = call(
        give_kernel,
        (gate, swap(text_give), *summands[0]),
        [SMEM] + [VMEM] * (1 + CHIPS),
        [shape(tokens, half)],
        flops=2**20,
        size=2**20,
        name="mix_give",
    )[0]
    return call(
        last_kernel,
        (where, gate, text_keep, swap(give), *summands[1]),
        [SMEM, SMEM] + [VMEM] * (2 + CHIPS),
        [shape(tokens, 2 * half)],
        flops=2**20,
        size=2**20,
        name="mix_keep",
    )[0]


def solution(mesh):
    fits = mesh.shape["img"] == 4 and mesh.shape["ctx"] == 8
    return jax.shard_map(
        paired if fits else general,
        mesh=mesh,
        in_specs=(
            P("ctx", None),
            P(),
            P("ctx", "img"),
            P("ctx", None),
            P("img", "ctx"),
            P(),
            P(),
            P(),
            P("img", "ctx", None),
            P("ctx"),
            P(),
            P(),
        ),
        out_specs=P("ctx", "img"),
        check_vma=False,
    )
```

```python
import jax
import jax.numpy as jnp
from jax import lax
from jax.experimental import pallas as pl
from jax.experimental.pallas import tpu as pltpu
from jax.sharding import PartitionSpec as P

KVH = 8


EPS = 1e-05
NEG = -1e30


def head_norm(values, gain):
    mean_sq = jnp.mean(values * values, axis=-1, keepdims=True)
    return values * lax.rsqrt(mean_sq + EPS) * gain


def attend(query, keys, values, mask):
    scale = query.shape[-1] ** (-0.5)
    scores = jnp.einsum("tkgd,nkd->tkgn", query, keys, preferred_element_type=jnp.float32) * scale
    live = mask[:, None, None, :]
    scores = jnp.where(live, scores, NEG)
    top = jnp.max(scores, axis=-1)
    weights = jnp.where(live, jnp.exp(scores - top[..., None]), 0.0)
    total = jnp.sum(weights, axis=-1)
    acc = jnp.einsum(
        "tkgn,nkd->tkgd", weights.astype(jnp.bfloat16), values, preferred_element_type=jnp.float32
    )
    return acc / total[..., None]


def general(
    text,
    input_gain,
    q_weight,
    kv_weight,
    o_weight,
    q_gain,
    k_gain,
    attn_gate,
    vision,
    segment_ids,
    seg_images,
    image_slot,
):
    tokens_here = text.shape[0]
    head_dim = q_gain.shape[0]
    ctx_count = lax.axis_size("ctx")
    img_count = lax.axis_size("img")
    heads_here = q_weight.shape[1] // head_dim
    kv_heads = max(1, KVH // img_count)
    group = heads_here // kv_heads
    slots_here, vt_dev = vision.shape[:2]
    rows_here = slots_here * vt_dev

    o_full = lax.all_gather(o_weight, "ctx", axis=1, tiled=True)
    vision_cols = lax.all_to_all(
        vision.reshape(rows_here, -1), "ctx", split_axis=1, concat_axis=0, tiled=True
    )
    hidden = head_norm(text.astype(jnp.float32), input_gain).astype(jnp.bfloat16)
    hidden_cols = lax.all_to_all(hidden, "ctx", split_axis=1, concat_axis=0, tiled=True)

    kv_share = jnp.dot(vision_cols, kv_weight, preferred_element_type=jnp.float32)
    kv_shares = lax.all_to_all(
        kv_share.reshape(ctx_count, rows_here, -1), "ctx", split_axis=0, concat_axis=0, tiled=True
    )
    projected = jnp.sum(kv_shares, axis=0).reshape(rows_here, KVH, 2, head_dim)
    keys = head_norm(projected[:, :, 0], k_gain).astype(jnp.bfloat16)
    values = projected[:, :, 1].astype(jnp.bfloat16)
    kv_rows = jnp.stack((keys, values), axis=2)
    owners = jnp.arange(img_count)[:, None] * KVH // img_count + jnp.arange(kv_heads)[None, :]
    kv_out = jnp.take(kv_rows, owners, axis=1).transpose(1, 0, 2, 3, 4)
    kv_in = lax.all_to_all(kv_out, "img", split_axis=0, concat_axis=0, tiled=True)
    kv_all = lax.all_gather(kv_in, "ctx", axis=0, tiled=False)

    q_share = jnp.dot(hidden_cols, q_weight, preferred_element_type=jnp.float32)
    q_shares = lax.all_to_all(
        q_share.astype(jnp.bfloat16).reshape(ctx_count, tokens_here, -1),
        "ctx",
        split_axis=0,
        concat_axis=0,
        tiled=True,
    )
    query = jnp.sum(q_shares.astype(jnp.float32), axis=0)
    query = head_norm(query.reshape(tokens_here, kv_heads, group, head_dim), q_gain).astype(
        jnp.bfloat16
    )

    slots = img_count * slots_here
    own_slots = jnp.take(image_slot, jnp.take(seg_images, segment_ids, axis=0), axis=0)
    slot_ids = jnp.arange(slots, dtype=jnp.int32)
    sees = jnp.any(own_slots[:, :, None] == slot_ids[None, None, :], axis=1)
    flat = kv_all.reshape(ctx_count * slots * vt_dev, kv_heads, 2, head_dim)
    mask = jnp.broadcast_to(
        sees[:, None, :, None], (tokens_here, ctx_count, slots, vt_dev)
    ).reshape(tokens_here, -1)
    context = attend(query, flat[:, :, 0], flat[:, :, 1], mask)
    context = context.astype(jnp.bfloat16).reshape(tokens_here, heads_here * head_dim)
    partial_terms = jnp.dot(context, o_full, preferred_element_type=jnp.float32)
    width = partial_terms.shape[1] // img_count
    shares = lax.all_to_all(
        partial_terms.astype(jnp.bfloat16).reshape(tokens_here, img_count, width),
        "img",
        split_axis=1,
        concat_axis=1,
        tiled=True,
    )
    update = jnp.sum(shares.astype(jnp.float32), axis=1)
    own_text = lax.dynamic_slice_in_dim(text, lax.axis_index("img") * width, width, 1)
    return (own_text.astype(jnp.float32) + jnp.tanh(attn_gate[0]) * update).astype(jnp.bfloat16)


BF16, F32 = jnp.bfloat16, jnp.float32
SMEM = pl.BlockSpec(memory_space=pltpu.SMEM)
VMEM = pl.BlockSpec(memory_space=pltpu.VMEM)
CHIPS = 4


def call(kernel, args, specs, outs, out_specs=None, scratch=(), flops=0, size=0, name=None, grid=(), limit=24):
    return pl.pallas_call(
        kernel,
        out_shape=outs,
        in_specs=specs,
        out_specs=[VMEM] * len(outs) if out_specs is None else out_specs,
        scratch_shapes=scratch,
        grid=grid,
        compiler_params=pltpu.CompilerParams(vmem_limit_bytes=limit * 2**20),
        cost_estimate=pl.CostEstimate(flops=flops, bytes_accessed=size, transcendentals=0),
        name=name,
    )(*args)


def block(index, size):
    return pl.ds(pl.multiple_of(index * size, size), size)


def start_kernel(where, text_hbm, gain, vis_hbm, q_hbm, *refs):
    pieces, refs = refs[:CHIPS], refs[CHIPS:]
    near, far, text_keep, text_give, q_keep, q_give, text, vis, scale, sems = refs
    chip, core, plane = where[0], where[1], where[2]
    tokens, width = text.shape
    part = width // 2
    half = text_keep.shape[1]
    step = 16
    first = pltpu.make_async_copy(vis_hbm, vis, sems.at[0])
    first.start()
    copies = []
    for k, r in enumerate(range(0, tokens, 2 * step)):
        rows = pl.ds(r, 2 * step)
        copies.append(pltpu.make_async_copy(text_hbm.at[rows, :], text.at[rows, :], sems.at[3 + k]))
        copies[-1].start()
    cuts = [
        pltpu.make_async_copy(q_hbm.at[:, block(core, half)], q_keep, sems.at[1]),
        pltpu.make_async_copy(q_hbm.at[:, block(1 - core, half)], q_give, sems.at[2]),
    ]
    for copy in cuts:
        copy.start()
    first.wait()
    for s in range(CHIPS):
        pieces[s][...] = vis[:, block(chip ^ s, pieces[s].shape[1])]
    for r in range(0, tokens, step):
        if r % (2 * step) == 0:
            copies[r // (2 * step)].wait()
        x = text[r : r + step, :].astype(F32)
        mean_sq = jnp.mean(x * x, axis=-1, keepdims=True)
        scale[r : r + step, :] = jnp.broadcast_to(lax.rsqrt(mean_sq + EPS), (step, 128))
    line = chip // 2
    for out, index in ((far, 1 - line), (near, line)):
        cols = block(index, part)
        row_gain = gain[:, cols]
        for r in range(0, tokens, step):
            x = text[r : r + step, cols].astype(F32)
            out[r : r + step, :] = (x * scale[r : r + step, 0:1] * row_gain).astype(BF16)
    text_keep[...] = text[:, block(2 * plane + core, half)]
    text_give[...] = text[:, block(2 * plane + 1 - core, half)]
    for copy in cuts:
        copy.wait()


def kv_kernel(where, vis, vis_other, kv_own, kv_other, *refs):
    shares, (other, near_total, sems) = refs[:CHIPS], refs[CHIPS:]
    core = where[1]
    rows = kv_own.shape[0]
    head = kv_own.shape[1] // (2 * CHIPS)
    copies = []
    for j in range(CHIPS):
        copies.append(
            pltpu.make_async_copy(
                kv_other.at[:, block(2 * j + core, head)],
                other.at[:, pl.ds(j * head, head)],
                sems.at[j],
            )
        )
        copies[-1].start()
    near, far = block(core, rows), block(1 - core, rows)
    x_near = jnp.concatenate((vis[:, near], vis_other[:, near]), axis=0)
    x_far = jnp.concatenate((vis[:, far], vis_other[:, far]), axis=0)
    total = vis.shape[0]
    count = total // CHIPS
    for j in range(CHIPS):
        near_total[:, j * head : (j + 1) * head] = jnp.dot(
            x_near, kv_own[:, block(2 * j + core, head)], preferred_element_type=F32
        )
    for j in range(CHIPS):
        copies[j].wait()
        cols = slice(j * head, (j + 1) * head)
        out = near_total[:, cols] + jnp.dot(x_far, other[:, cols], preferred_element_type=F32)
        for s in range(CHIPS):
            shares[s][:count, cols] = out[s * count : (s + 1) * count]
            shares[s][count:, cols] = out[total + s * count : total + (s + 1) * count]


def kv_norm_kernel(where, k_gain, *refs):
    shares, (here, there, give) = refs[:CHIPS], refs[CHIPS:]
    plane = where[2]
    lines, head = here.shape
    dim = head // 2
    for t, (out, row) in enumerate(((here, 0), (give, 0), (there, 0), (give, lines))):
        cols = block(plane ^ t, head)
        total = (shares[0][:, cols] + shares[1][:, cols]) + (shares[2][:, cols] + shares[3][:, cols])
        keys = head_norm(total[:, :dim], k_gain[...])
        out[row : row + lines, :dim] = keys.astype(BF16)
        out[row : row + lines, dim:] = total[:, dim:].astype(BF16)


def kv_turn_kernel(there, landed, out):
    lines = there.shape[0]
    out[:lines, :] = there[...]
    out[lines:, :] = landed[lines:, :]


def kv_join_kernel(here, landed, last, out):
    lines = here.shape[0]
    out[:lines, :] = here[...]
    out[lines : 2 * lines, :] = landed[:lines, :]
    out[2 * lines :, :] = last[...]


def query_share(index, own, other, first, second, flip):
    rows = first.shape[0]
    total = None
    for weight, k in ((first, index), (second, index ^ flip)):
        cols = block(k, rows)
        x = jnp.concatenate((own[:, cols], other[:, cols]), axis=0)
        share = jnp.dot(x, weight[...], preferred_element_type=F32)
        total = share if total is None else total + share
    return total


def early_kernel(where, own, other, q_keep, q_other, out):
    index = 2 * lax.rem(where[0], 2) + where[1]
    out[...] = query_share(index, own, other, q_keep, q_other, 1)


def late_kernel(where, own, other, q_side, q_corner, early, out):
    index = (2 * lax.rem(where[0], 2) + where[1]) ^ 2
    share = early[...] + query_share(index, own, other, q_side, q_corner, 1)
    out[...] = share.astype(out.dtype)


def attend_kernel(q_gain, first, landed, *refs):
    kv, (bias, context) = refs[:CHIPS], refs[CHIPS:]
    dim = q_gain.shape[1]
    rows, half = context.shape
    keys = jnp.concatenate([x[:, :dim] for x in kv], axis=0)
    values = jnp.concatenate([x[:, dim:] for x in kv], axis=0)
    step = 128
    for r in range(0, rows, step):
        for g in range(half // dim):
            cols = slice(g * dim, (g + 1) * dim)
            query = first[r : r + step, cols] + landed[r : r + step, cols].astype(F32)
            query = head_norm(query, q_gain[...]).astype(BF16)
            scores = lax.dot_general(
                query, keys, (((1,), (1,)), ((), ())), preferred_element_type=F32
            )
            scores = scores * dim ** (-0.5) + bias[r : r + step, :]
            weights = jnp.exp(scores - jnp.max(scores, axis=-1, keepdims=True))
            total = jnp.sum(weights, axis=-1, keepdims=True)
            acc = jnp.dot(weights.astype(BF16), values, preferred_element_type=F32)
            context[r : r + step, cols] = (acc / total).astype(BF16)


def out_kernel(where, near, far, o_own, o_early, o_late, own, other):
    core = where[1]
    tokens, width = own.shape
    half = near.shape[1]
    turned = jnp.concatenate((far[tokens:, :], far[:tokens, :]), axis=0)
    share = jnp.dot(near[...], o_own[block(core, half), :], preferred_element_type=F32)
    share += jnp.dot(turned, o_own[block(1 - core, half), :], preferred_element_type=F32)
    own[:, : width // 2] = share[:tokens].astype(BF16)
    other[:, : width // 2] = share[tokens:].astype(BF16)
    top = jnp.where(core == 0, near[...], turned)
    low = jnp.where(core == 0, turned, near[...])
    share = jnp.dot(top, o_early[...], preferred_element_type=F32)
    share += jnp.dot(low, o_late[...], preferred_element_type=F32)
    own[:, width // 2 :] = share[:tokens].astype(BF16)
    other[:, width // 2 :] = share[tokens:].astype(BF16)


def pick_kernel(where, own, landed, *outs):
    first = where[0] ^ where[2]
    half = outs[0].shape[1]
    for t in range(CHIPS):
        for s in range(CHIPS):

            @pl.when((first ^ t) == s)
            def _():
                outs[t][...] = (own, landed)[s % 2][:, (s // 2) * half : (s // 2 + 1) * half]


def mixed_rows(gate, text, shares):
    x = [share[...].astype(F32) for share in shares]
    update = (x[0] + x[1]) + (x[2] + x[3])
    return (text[...].astype(F32) + gate[0] * update).astype(BF16)


def give_kernel(gate, text, *refs):
    refs[CHIPS][...] = mixed_rows(gate, text, refs[:CHIPS])


def last_kernel(where, gate, text, back, *refs):
    shares, out = refs[:CHIPS], refs[CHIPS]
    core = where[1]
    half = text.shape[1]
    out[:, block(core, half)] = mixed_rows(gate, text, shares)
    out[:, block(1 - core, half)] = back[...]


def paired(
    text,
    input_gain,
    q_weight,
    kv_weight,
    o_weight,
    q_gain,
    k_gain,
    attn_gate,
    vision,
    segment_ids,
    seg_images,
    image_slot,
):
    ctx_count = lax.axis_size("ctx")
    place, plane = lax.axis_index("ctx"), lax.axis_index("img")
    chip, core = place // 2, place % 2
    where = jnp.stack((chip, core, plane)).astype(jnp.int32)
    tokens, width = text.shape
    head_dim = q_gain.shape[0]
    rows_dev, cols_plane = q_weight.shape
    half = cols_plane // 2
    part = 2 * rows_dev
    slots_here, vt_dev = vision.shape[:2]
    vis_here = slots_here * vt_dev
    kv_cols = kv_weight.shape[1] // 2

    def shape(rows, cols, kind=BF16):
        return jax.ShapeDtypeStruct((rows, cols), kind)

    def swap(x):
        return lax.ppermute(x, "ctx", [(k, k ^ 1) for k in range(ctx_count)])

    def peer(x, s):
        return lax.ppermute(x, "ctx", [(k, k ^ (2 * s)) for k in range(ctx_count)])

    def along_x(x):
        return peer(x, 1)

    def along_y(x):
        return peer(x, 2)

    def across(x, t):
        return lax.ppermute(x, "img", [(k, k ^ t) for k in range(CHIPS)])

    steps = range(1, CHIPS)
    vis = vision.reshape(vis_here, width)
    kv_other = swap(kv_weight)

    anywhere = pl.BlockSpec(memory_space=pl.ANY)
    *vis_pieces, near, far, text_keep, text_give, q_keep, q_give = call(
        start_kernel,
        (where, text, input_gain[None], vis, q_weight),
        [SMEM, anywhere, VMEM, anywhere, anywhere],
        [shape(vis_here, part)] * CHIPS
        + [shape(tokens, width // 2)] * 2
        + [shape(tokens, half)] * 2
        + [shape(rows_dev, half)] * 2,
        scratch=[
            pltpu.VMEM((tokens, width), BF16),
            pltpu.VMEM((vis_here, width), BF16),
            pltpu.VMEM((tokens, 128), F32),
            pltpu.SemaphoreType.DMA((3 + tokens // 32,)),
        ],
        flops=8 * tokens * width,
        size=4 * 2**20,
        name="start",
        limit=60,
    )
    vis_own = jnp.concatenate([vis_pieces[0]] + [peer(vis_pieces[s], s) for s in steps])
    vis_other = swap(vis_own)
    q_side, q_other = along_x(q_keep), swap(q_give)
    far = along_y(far)

    shares = call(
        kv_kernel,
        (where, vis_own, vis_other, kv_weight, kv_other),
        [SMEM] + [VMEM] * 3 + [pl.BlockSpec(memory_space=pl.ANY)],
        [shape(2 * vis_here, kv_cols, F32)] * CHIPS,
        scratch=[
            pltpu.VMEM((rows_dev, kv_cols), BF16),
            pltpu.VMEM((8 * vis_here, kv_cols), F32),
            pltpu.SemaphoreType.DMA((CHIPS,)),
        ],
        flops=4 * vis_here * ctx_count * part * kv_cols,
        size=4 * 2**20,
        name="kv_shares",
    )
    shares = [shares[0]] + [peer(shares[s], s) for s in steps]
    own_share = shares[0]
    q_behind, _ = lax.optimization_barrier((q_other, (own_share, q_side)))
    q_corner = along_x(q_behind)
    shares, q_side, far = lax.optimization_barrier((shares, q_side, far))
    here, there, give = call(
        kv_norm_kernel,
        (where, k_gain[None], *shares),
        [SMEM] + [VMEM] * (1 + CHIPS),
        [shape(2 * vis_here, 2 * head_dim)] * 2 + [shape(4 * vis_here, 2 * head_dim)],
        name="kv_norm",
    )
    blocks = ((far, swap(far)), (near, swap(near)))
    early = [
        call(
            early_kernel,
            (where, *pair, q_keep, q_other),
            [SMEM] + [VMEM] * 4,
            [shape(2 * tokens, half, F32)],
            flops=4 * tokens * part * half,
            size=2 * 2**20,
            name="q_early",
        )[0]
        for pair in blocks
    ]
    kv_z, q_corner = lax.optimization_barrier((across(give, 1), q_corner))
    o_early, _ = lax.optimization_barrier((o_weight[:half], here))
    o_early = along_y(o_early)
    q_far, q_first = [
        call(
            late_kernel,
            (where, *blocks[k], q_side, q_corner, early[k]),
            [SMEM] + [VMEM] * 5,
            [shape(2 * tokens, half, kind)],
            flops=4 * tokens * part * half,
            size=2 * 2**20,
            name="q_late",
        )[0]
        for k, kind in ((0, BF16), (1, F32))
    ]
    turn = call(
        kv_turn_kernel,
        (there, kv_z),
        [VMEM] * 2,
        [shape(4 * vis_here, 2 * head_dim)],
        name="kv_turn",
    )[0]
    kv_last, o_early, q_far = lax.optimization_barrier((across(turn, 2), o_early, q_far))
    kv_first = call(
        kv_join_kernel,
        (here, kv_z, kv_last),
        [VMEM] * 3,
        [shape(8 * vis_here, 2 * head_dim)],
        name="kv_join",
    )[0]
    kv_first, _ = lax.optimization_barrier((kv_first, q_first))
    kv_all = [kv_first] + [peer(kv_first, s) for s in steps]

    landed = along_y(q_far)
    o_late, _ = lax.optimization_barrier((o_weight[half:], q_far))
    o_late = along_y(o_late)

    ids = jnp.concatenate((segment_ids, swap(segment_ids)))
    images = jnp.arange(image_slot.shape[0])
    slot_of = jnp.sum(
        jnp.where(seg_images[:, :, None] == images, image_slot[None, None, :], 0), axis=2
    )
    numbers = jnp.arange(seg_images.shape[0])
    own_slots = jnp.sum(
        jnp.where((ids[:, None] == numbers)[:, :, None], slot_of[None], 0), axis=1
    )
    key_rows = jnp.arange(CHIPS * CHIPS * 2 * vis_here)
    key_plane = plane ^ (key_rows // (2 * vis_here) % CHIPS)
    key_slot = key_plane * slots_here + key_rows // vt_dev % slots_here
    sees = jnp.any(own_slots[:, :, None] == key_slot, axis=1)
    bias = jnp.where(sees, 0.0, NEG).astype(F32)

    context = call(
        attend_kernel,
        (q_gain[None], q_first, landed, *kv_all, bias),
        [VMEM] * (4 + CHIPS),
        [shape(2 * tokens, half)],
        flops=8 * tokens * half * bias.shape[1],
        size=2 * 2**20,
        name="attend",
    )[0]

    context_x = along_x(context)
    shares = [
        call(
            out_kernel,
            (where, x, swap(x), o_weight, o_early, o_late),
            [SMEM] + [VMEM] * 5,
            [shape(tokens, 2 * half)] * 2,
            flops=8 * tokens * cols_plane * half,
            size=2 * 2**20,
            name="o_share",
        )
        for x in (context_x, context)
    ]
    summands = []
    for rows in (1, 0):
        picked = call(
            pick_kernel,
            (where, shares[1][rows], along_x(shares[0][rows])),
            [SMEM] + [VMEM] * 2,
            [shape(tokens, half)] * CHIPS,
            flops=2**20,
            size=2**20,
            name="pick",
        )
        summands.append([picked[0]] + [across(picked[t], t) for t in steps])
    gate = jnp.tanh(attn_gate)
    give = call(
        give_kernel,
        (gate, swap(text_give), *summands[0]),
        [SMEM] + [VMEM] * (1 + CHIPS),
        [shape(tokens, half)],
        flops=2**20,
        size=2**20,
        name="mix_give",
    )[0]
    return call(
        last_kernel,
        (where, gate, text_keep, swap(give), *summands[1]),
        [SMEM, SMEM] + [VMEM] * (2 + CHIPS),
        [shape(tokens, 2 * half)],
        flops=2**20,
        size=2**20,
        name="mix_keep",
    )[0]


def solution(mesh):
    fits = mesh.shape["img"] == 4 and mesh.shape["ctx"] == 8
    return jax.shard_map(
        paired if fits else general,
        mesh=mesh,
        in_specs=(
            P("ctx", None),
            P(),
            P("ctx", "img"),
            P("ctx", None),
            P("img", "ctx"),
            P(),
            P(),
            P(),
            P("img", "ctx", None),
            P("ctx"),
            P(),
            P(),
        ),
        out_specs=P("ctx", "img"),
        check_vma=False,
    )
```

```python
import jax
import jax.numpy as jnp
from jax import lax
from jax.experimental import pallas as pl
from jax.experimental.pallas import tpu as pltpu
from jax.sharding import PartitionSpec as P

KVH = 8


EPS = 1e-05
NEG = -1e30


def head_norm(values, gain):
    mean_sq = jnp.mean(values * values, axis=-1, keepdims=True)
    return values * lax.rsqrt(mean_sq + EPS) * gain


def attend(query, keys, values, mask):
    scale = query.shape[-1] ** (-0.5)
    scores = jnp.einsum("tkgd,nkd->tkgn", query, keys, preferred_element_type=jnp.float32) * scale
    live = mask[:, None, None, :]
    scores = jnp.where(live, scores, NEG)
    top = jnp.max(scores, axis=-1)
    weights = jnp.where(live, jnp.exp(scores - top[..., None]), 0.0)
    total = jnp.sum(weights, axis=-1)
    acc = jnp.einsum(
        "tkgn,nkd->tkgd", weights.astype(jnp.bfloat16), values, preferred_element_type=jnp.float32
    )
    return acc / total[..., None]


def general(
    text,
    input_gain,
    q_weight,
    kv_weight,
    o_weight,
    q_gain,
    k_gain,
    attn_gate,
    vision,
    segment_ids,
    seg_images,
    image_slot,
):
    tokens_here = text.shape[0]
    head_dim = q_gain.shape[0]
    ctx_count = lax.axis_size("ctx")
    img_count = lax.axis_size("img")
    heads_here = q_weight.shape[1] // head_dim
    kv_heads = max(1, KVH // img_count)
    group = heads_here // kv_heads
    slots_here, vt_dev = vision.shape[:2]
    rows_here = slots_here * vt_dev

    o_full = lax.all_gather(o_weight, "ctx", axis=1, tiled=True)
    vision_cols = lax.all_to_all(
        vision.reshape(rows_here, -1), "ctx", split_axis=1, concat_axis=0, tiled=True
    )
    hidden = head_norm(text.astype(jnp.float32), input_gain).astype(jnp.bfloat16)
    hidden_cols = lax.all_to_all(hidden, "ctx", split_axis=1, concat_axis=0, tiled=True)

    kv_share = jnp.dot(vision_cols, kv_weight, preferred_element_type=jnp.float32)
    kv_shares = lax.all_to_all(
        kv_share.reshape(ctx_count, rows_here, -1), "ctx", split_axis=0, concat_axis=0, tiled=True
    )
    projected = jnp.sum(kv_shares, axis=0).reshape(rows_here, KVH, 2, head_dim)
    keys = head_norm(projected[:, :, 0], k_gain).astype(jnp.bfloat16)
    values = projected[:, :, 1].astype(jnp.bfloat16)
    kv_rows = jnp.stack((keys, values), axis=2)
    owners = jnp.arange(img_count)[:, None] * KVH // img_count + jnp.arange(kv_heads)[None, :]
    kv_out = jnp.take(kv_rows, owners, axis=1).transpose(1, 0, 2, 3, 4)
    kv_in = lax.all_to_all(kv_out, "img", split_axis=0, concat_axis=0, tiled=True)
    kv_all = lax.all_gather(kv_in, "ctx", axis=0, tiled=False)

    q_share = jnp.dot(hidden_cols, q_weight, preferred_element_type=jnp.float32)
    q_shares = lax.all_to_all(
        q_share.astype(jnp.bfloat16).reshape(ctx_count, tokens_here, -1),
        "ctx",
        split_axis=0,
        concat_axis=0,
        tiled=True,
    )
    query = jnp.sum(q_shares.astype(jnp.float32), axis=0)
    query = head_norm(query.reshape(tokens_here, kv_heads, group, head_dim), q_gain).astype(
        jnp.bfloat16
    )

    slots = img_count * slots_here
    own_slots = jnp.take(image_slot, jnp.take(seg_images, segment_ids, axis=0), axis=0)
    slot_ids = jnp.arange(slots, dtype=jnp.int32)
    sees = jnp.any(own_slots[:, :, None] == slot_ids[None, None, :], axis=1)
    flat = kv_all.reshape(ctx_count * slots * vt_dev, kv_heads, 2, head_dim)
    mask = jnp.broadcast_to(
        sees[:, None, :, None], (tokens_here, ctx_count, slots, vt_dev)
    ).reshape(tokens_here, -1)
    context = attend(query, flat[:, :, 0], flat[:, :, 1], mask)
    context = context.astype(jnp.bfloat16).reshape(tokens_here, heads_here * head_dim)
    partial_terms = jnp.dot(context, o_full, preferred_element_type=jnp.float32)
    width = partial_terms.shape[1] // img_count
    shares = lax.all_to_all(
        partial_terms.astype(jnp.bfloat16).reshape(tokens_here, img_count, width),
        "img",
        split_axis=1,
        concat_axis=1,
        tiled=True,
    )
    update = jnp.sum(shares.astype(jnp.float32), axis=1)
    own_text = lax.dynamic_slice_in_dim(text, lax.axis_index("img") * width, width, 1)
    return (own_text.astype(jnp.float32) + jnp.tanh(attn_gate[0]) * update).astype(jnp.bfloat16)


BF16, F32 = jnp.bfloat16, jnp.float32
SMEM = pl.BlockSpec(memory_space=pltpu.SMEM)
VMEM = pl.BlockSpec(memory_space=pltpu.VMEM)
CHIPS = 4


def call(kernel, args, specs, outs, out_specs=None, scratch=(), flops=0, size=0, name=None, grid=(), limit=24):
    return pl.pallas_call(
        kernel,
        out_shape=outs,
        in_specs=specs,
        out_specs=[VMEM] * len(outs) if out_specs is None else out_specs,
        scratch_shapes=scratch,
        grid=grid,
        compiler_params=pltpu.CompilerParams(vmem_limit_bytes=limit * 2**20),
        cost_estimate=pl.CostEstimate(flops=flops, bytes_accessed=size, transcendentals=0),
        name=name,
    )(*args)


def block(index, size):
    return pl.ds(pl.multiple_of(index * size, size), size)


def start_kernel(where, text_hbm, gain, vis_hbm, q_hbm, *refs):
    pieces, refs = refs[:CHIPS], refs[CHIPS:]
    near, far, text_keep, text_give, q_keep, q_give, text, vis, scale, sems = refs
    chip, core, plane = where[0], where[1], where[2]
    tokens, width = text.shape
    part = width // 2
    half = text_keep.shape[1]
    step = 16
    first = pltpu.make_async_copy(vis_hbm, vis, sems.at[0])
    first.start()
    copies = []
    for k, r in enumerate(range(0, tokens, 2 * step)):
        rows = pl.ds(r, 2 * step)
        copies.append(pltpu.make_async_copy(text_hbm.at[rows, :], text.at[rows, :], sems.at[3 + k]))
        copies[-1].start()
    cuts = [
        pltpu.make_async_copy(q_hbm.at[:, block(core, half)], q_keep, sems.at[1]),
        pltpu.make_async_copy(q_hbm.at[:, block(1 - core, half)], q_give, sems.at[2]),
    ]
    for copy in cuts:
        copy.start()
    first.wait()
    for s in range(CHIPS):
        pieces[s][...] = vis[:, block(chip ^ s, pieces[s].shape[1])]
    for r in range(0, tokens, step):
        if r % (2 * step) == 0:
            copies[r // (2 * step)].wait()
        x = text[r : r + step, :].astype(F32)
        mean_sq = jnp.mean(x * x, axis=-1, keepdims=True)
        scale[r : r + step, :] = jnp.broadcast_to(lax.rsqrt(mean_sq + EPS), (step, 128))
    line = chip // 2
    for out, index in ((far, 1 - line), (near, line)):
        cols = block(index, part)
        row_gain = gain[:, cols]
        for r in range(0, tokens, step):
            x = text[r : r + step, cols].astype(F32)
            out[r : r + step, :] = (x * scale[r : r + step, 0:1] * row_gain).astype(BF16)
    text_keep[...] = text[:, block(2 * plane + core, half)]
    text_give[...] = text[:, block(2 * plane + 1 - core, half)]
    for copy in cuts:
        copy.wait()


def kv_kernel(where, vis, vis_other, kv_own, kv_other, *refs):
    shares, (other, near_total, sems) = refs[:CHIPS], refs[CHIPS:]
    core = where[1]
    rows = kv_own.shape[0]
    head = kv_own.shape[1] // (2 * CHIPS)
    copies = []
    for j in range(CHIPS):
        copies.append(
            pltpu.make_async_copy(
                kv_other.at[:, block(2 * j + core, head)],
                other.at[:, pl.ds(j * head, head)],
                sems.at[j],
            )
        )
        copies[-1].start()
    near, far = block(core, rows), block(1 - core, rows)
    x_near = jnp.concatenate((vis[:, near], vis_other[:, near]), axis=0)
    x_far = jnp.concatenate((vis[:, far], vis_other[:, far]), axis=0)
    total = vis.shape[0]
    count = total // CHIPS
    for j in range(CHIPS):
        near_total[:, j * head : (j + 1) * head] = jnp.dot(
            x_near, kv_own[:, block(2 * j + core, head)], preferred_element_type=F32
        )
    for j in range(CHIPS):
        copies[j].wait()
        cols = slice(j * head, (j + 1) * head)
        out = near_total[:, cols] + jnp.dot(x_far, other[:, cols], preferred_element_type=F32)
        for s in range(CHIPS):
            shares[s][:count, cols] = out[s * count : (s + 1) * count]
            shares[s][count:, cols] = out[total + s * count : total + (s + 1) * count]


def kv_norm_kernel(where, k_gain, *refs):
    shares, (here, there, give) = refs[:CHIPS], refs[CHIPS:]
    plane = where[2]
    lines, head = here.shape
    dim = head // 2
    for t, (out, row) in enumerate(((here, 0), (give, 0), (there, 0), (give, lines))):
        cols = block(plane ^ t, head)
        total = (shares[0][:, cols] + shares[1][:, cols]) + (shares[2][:, cols] + shares[3][:, cols])
        keys = head_norm(total[:, :dim], k_gain[...])
        out[row : row + lines, :dim] = keys.astype(BF16)
        out[row : row + lines, dim:] = total[:, dim:].astype(BF16)


def kv_turn_kernel(there, landed, out):
    lines = there.shape[0]
    out[:lines, :] = there[...]
    out[lines:, :] = landed[lines:, :]


def kv_join_kernel(here, landed, last, out):
    lines = here.shape[0]
    out[:lines, :] = here[...]
    out[lines : 2 * lines, :] = landed[:lines, :]
    out[2 * lines :, :] = last[...]


def query_share(index, own, other, first, second, flip):
    rows = first.shape[0]
    total = None
    for weight, k in ((first, index), (second, index ^ flip)):
        cols = block(k, rows)
        x = jnp.concatenate((own[:, cols], other[:, cols]), axis=0)
        share = jnp.dot(x, weight[...], preferred_element_type=F32)
        total = share if total is None else total + share
    return total


def early_kernel(where, own, other, q_keep, q_other, out):
    index = 2 * lax.rem(where[0], 2) + where[1]
    out[...] = query_share(index, own, other, q_keep, q_other, 1)


def late_kernel(where, own, other, q_side, q_corner, early, out):
    index = (2 * lax.rem(where[0], 2) + where[1]) ^ 2
    share = early[...] + query_share(index, own, other, q_side, q_corner, 1)
    out[...] = share.astype(out.dtype)


def attend_kernel(q_gain, first, landed, *refs):
    kv, (bias, context) = refs[:CHIPS], refs[CHIPS:]
    dim = q_gain.shape[1]
    rows, half = context.shape
    keys = jnp.concatenate([x[:, :dim] for x in kv], axis=0)
    values = jnp.concatenate([x[:, dim:] for x in kv], axis=0)
    step = 128
    for r in range(0, rows, step):
        for g in range(half // dim):
            cols = slice(g * dim, (g + 1) * dim)
            query = first[r : r + step, cols] + landed[r : r + step, cols].astype(F32)
            query = head_norm(query, q_gain[...]).astype(BF16)
            scores = lax.dot_general(
                query, keys, (((1,), (1,)), ((), ())), preferred_element_type=F32
            )
            scores = scores * dim ** (-0.5) + bias[r : r + step, :]
            weights = jnp.exp(scores - jnp.max(scores, axis=-1, keepdims=True))
            total = jnp.sum(weights, axis=-1, keepdims=True)
            acc = jnp.dot(weights.astype(BF16), values, preferred_element_type=F32)
            context[r : r + step, cols] = (acc / total).astype(BF16)


def out_kernel(where, near, far, o_own, o_early, o_late, own, other):
    core = where[1]
    tokens, width = own.shape
    half = near.shape[1]
    turned = jnp.concatenate((far[tokens:, :], far[:tokens, :]), axis=0)
    share = jnp.dot(near[...], o_own[block(core, half), :], preferred_element_type=F32)
    share += jnp.dot(turned, o_own[block(1 - core, half), :], preferred_element_type=F32)
    own[:, : width // 2] = share[:tokens].astype(BF16)
    other[:, : width // 2] = share[tokens:].astype(BF16)
    top = jnp.where(core == 0, near[...], turned)
    low = jnp.where(core == 0, turned, near[...])
    share = jnp.dot(top, o_early[...], preferred_element_type=F32)
    share += jnp.dot(low, o_late[...], preferred_element_type=F32)
    own[:, width // 2 :] = share[:tokens].astype(BF16)
    other[:, width // 2 :] = share[tokens:].astype(BF16)


def pick_kernel(where, own, landed, *outs):
    first = where[0] ^ where[2]
    half = outs[0].shape[1]
    for t in range(CHIPS):
        for s in range(CHIPS):

            @pl.when((first ^ t) == s)
            def _():
                outs[t][...] = (own, landed)[s % 2][:, (s // 2) * half : (s // 2 + 1) * half]


def mixed_rows(gate, text, shares):
    x = [share[...].astype(F32) for share in shares]
    update = (x[0] + x[1]) + (x[2] + x[3])
    return (text[...].astype(F32) + gate[0] * update).astype(BF16)


def give_kernel(gate, text, *refs):
    refs[CHIPS][...] = mixed_rows(gate, text, refs[:CHIPS])


def last_kernel(where, gate, text, back, *refs):
    shares, out = refs[:CHIPS], refs[CHIPS]
    core = where[1]
    half = text.shape[1]
    out[:, block(core, half)] = mixed_rows(gate, text, shares)
    out[:, block(1 - core, half)] = back[...]


def paired(
    text,
    input_gain,
    q_weight,
    kv_weight,
    o_weight,
    q_gain,
    k_gain,
    attn_gate,
    vision,
    segment_ids,
    seg_images,
    image_slot,
):
    ctx_count = lax.axis_size("ctx")
    place, plane = lax.axis_index("ctx"), lax.axis_index("img")
    chip, core = place // 2, place % 2
    where = jnp.stack((chip, core, plane)).astype(jnp.int32)
    tokens, width = text.shape
    head_dim = q_gain.shape[0]
    rows_dev, cols_plane = q_weight.shape
    half = cols_plane // 2
    part = 2 * rows_dev
    slots_here, vt_dev = vision.shape[:2]
    vis_here = slots_here * vt_dev
    kv_cols = kv_weight.shape[1] // 2

    def shape(rows, cols, kind=BF16):
        return jax.ShapeDtypeStruct((rows, cols), kind)

    def swap(x):
        return lax.ppermute(x, "ctx", [(k, k ^ 1) for k in range(ctx_count)])

    def peer(x, s):
        return lax.ppermute(x, "ctx", [(k, k ^ (2 * s)) for k in range(ctx_count)])

    def along_x(x):
        return peer(x, 1)

    def along_y(x):
        return peer(x, 2)

    def across(x, t):
        return lax.ppermute(x, "img", [(k, k ^ t) for k in range(CHIPS)])

    steps = range(1, CHIPS)
    vis = vision.reshape(vis_here, width)
    kv_other = swap(kv_weight)

    anywhere = pl.BlockSpec(memory_space=pl.ANY)
    *vis_pieces, near, far, text_keep, text_give, q_keep, q_give = call(
        start_kernel,
        (where, text, input_gain[None], vis, q_weight),
        [SMEM, anywhere, VMEM, anywhere, anywhere],
        [shape(vis_here, part)] * CHIPS
        + [shape(tokens, width // 2)] * 2
        + [shape(tokens, half)] * 2
        + [shape(rows_dev, half)] * 2,
        scratch=[
            pltpu.VMEM((tokens, width), BF16),
            pltpu.VMEM((vis_here, width), BF16),
            pltpu.VMEM((tokens, 128), F32),
            pltpu.SemaphoreType.DMA((3 + tokens // 32,)),
        ],
        flops=8 * tokens * width,
        size=4 * 2**20,
        name="start",
        limit=60,
    )
    vis_own = jnp.concatenate([vis_pieces[0]] + [peer(vis_pieces[s], s) for s in steps])
    vis_other = swap(vis_own)
    q_side, q_other = along_x(q_keep), swap(q_give)
    far = along_y(far)

    shares = call(
        kv_kernel,
        (where, vis_own, vis_other, kv_weight, kv_other),
        [SMEM] + [VMEM] * 3 + [pl.BlockSpec(memory_space=pl.ANY)],
        [shape(2 * vis_here, kv_cols, F32)] * CHIPS,
        scratch=[
            pltpu.VMEM((rows_dev, kv_cols), BF16),
            pltpu.VMEM((8 * vis_here, kv_cols), F32),
            pltpu.SemaphoreType.DMA((CHIPS,)),
        ],
        flops=4 * vis_here * ctx_count * part * kv_cols,
        size=4 * 2**20,
        name="kv_shares",
    )
    shares = [shares[0]] + [peer(shares[s], s) for s in steps]
    own_share = shares[0]
    q_behind, _ = lax.optimization_barrier((q_other, (own_share, q_side)))
    q_corner = along_x(q_behind)
    shares, q_side, far = lax.optimization_barrier((shares, q_side, far))
    here, there, give = call(
        kv_norm_kernel,
        (where, k_gain[None], *shares),
        [SMEM] + [VMEM] * (1 + CHIPS),
        [shape(2 * vis_here, 2 * head_dim)] * 2 + [shape(4 * vis_here, 2 * head_dim)],
        name="kv_norm",
    )
    blocks = ((far, swap(far)), (near, swap(near)))
    early = [
        call(
            early_kernel,
            (where, *pair, q_keep, q_other),
            [SMEM] + [VMEM] * 4,
            [shape(2 * tokens, half, F32)],
            flops=4 * tokens * part * half,
            size=2 * 2**20,
            name="q_early",
        )[0]
        for pair in blocks
    ]
    kv_z = across(give, 1)
    o_early, _ = lax.optimization_barrier((o_weight[:half], here))
    o_early = along_y(o_early)
    q_far, q_first = [
        call(
            late_kernel,
            (where, *blocks[k], q_side, q_corner, early[k]),
            [SMEM] + [VMEM] * 5,
            [shape(2 * tokens, half, kind)],
            flops=40 * tokens * part * half,
            size=2 * 2**20,
            name="q_late",
        )[0]
        for k, kind in ((0, BF16), (1, F32))
    ]
    turn = call(
        kv_turn_kernel,
        (there, kv_z),
        [VMEM] * 2,
        [shape(4 * vis_here, 2 * head_dim)],
        name="kv_turn",
    )[0]
    kv_last, o_early, q_far = lax.optimization_barrier((across(turn, 2), o_early, q_far))
    kv_first = call(
        kv_join_kernel,
        (here, kv_z, kv_last),
        [VMEM] * 3,
        [shape(8 * vis_here, 2 * head_dim)],
        name="kv_join",
    )[0]
    kv_first, _ = lax.optimization_barrier((kv_first, q_first))
    kv_all = [kv_first] + [peer(kv_first, s) for s in steps]

    landed = along_y(q_far)
    o_late, _ = lax.optimization_barrier((o_weight[half:], q_far))
    o_late = along_y(o_late)

    ids = jnp.concatenate((segment_ids, swap(segment_ids)))
    images = jnp.arange(image_slot.shape[0])
    slot_of = jnp.sum(
        jnp.where(seg_images[:, :, None] == images, image_slot[None, None, :], 0), axis=2
    )
    numbers = jnp.arange(seg_images.shape[0])
    own_slots = jnp.sum(
        jnp.where((ids[:, None] == numbers)[:, :, None], slot_of[None], 0), axis=1
    )
    key_rows = jnp.arange(CHIPS * CHIPS * 2 * vis_here)
    key_plane = plane ^ (key_rows // (2 * vis_here) % CHIPS)
    key_slot = key_plane * slots_here + key_rows // vt_dev % slots_here
    sees = jnp.any(own_slots[:, :, None] == key_slot, axis=1)
    bias = jnp.where(sees, 0.0, NEG).astype(F32)

    context = call(
        attend_kernel,
        (q_gain[None], q_first, landed, *kv_all, bias),
        [VMEM] * (4 + CHIPS),
        [shape(2 * tokens, half)],
        flops=8 * tokens * half * bias.shape[1],
        size=2 * 2**20,
        name="attend",
    )[0]

    context_x = along_x(context)
    shares = [
        call(
            out_kernel,
            (where, x, swap(x), o_weight, o_early, o_late),
            [SMEM] + [VMEM] * 5,
            [shape(tokens, 2 * half)] * 2,
            flops=8 * tokens * cols_plane * half,
            size=2 * 2**20,
            name="o_share",
        )
        for x in (context_x, context)
    ]
    summands = []
    for rows in (1, 0):
        picked = call(
            pick_kernel,
            (where, shares[1][rows], along_x(shares[0][rows])),
            [SMEM] + [VMEM] * 2,
            [shape(tokens, half)] * CHIPS,
            flops=2**20,
            size=2**20,
            name="pick",
        )
        summands.append([picked[0]] + [across(picked[t], t) for t in steps])
    gate = jnp.tanh(attn_gate)
    give = call(
        give_kernel,
        (gate, swap(text_give), *summands[0]),
        [SMEM] + [VMEM] * (1 + CHIPS),
        [shape(tokens, half)],
        flops=2**20,
        size=2**20,
        name="mix_give",
    )[0]
    return call(
        last_kernel,
        (where, gate, text_keep, swap(give), *summands[1]),
        [SMEM, SMEM] + [VMEM] * (2 + CHIPS),
        [shape(tokens, 2 * half)],
        flops=2**20,
        size=2**20,
        name="mix_keep",
    )[0]


def solution(mesh):
    fits = mesh.shape["img"] == 4 and mesh.shape["ctx"] == 8
    return jax.shard_map(
        paired if fits else general,
        mesh=mesh,
        in_specs=(
            P("ctx", None),
            P(),
            P("ctx", "img"),
            P("ctx", None),
            P("img", "ctx"),
            P(),
            P(),
            P(),
            P("img", "ctx", None),
            P("ctx"),
            P(),
            P(),
        ),
        out_specs=P("ctx", "img"),
        check_vma=False,
    )
```

```python
import jax
import jax.numpy as jnp
from jax import lax
from jax.experimental import pallas as pl
from jax.experimental.pallas import tpu as pltpu
from jax.sharding import PartitionSpec as P

KVH = 8


EPS = 1e-05
NEG = -1e30


def head_norm(values, gain):
    mean_sq = jnp.mean(values * values, axis=-1, keepdims=True)
    return values * lax.rsqrt(mean_sq + EPS) * gain


def attend(query, keys, values, mask):
    scale = query.shape[-1] ** (-0.5)
    scores = jnp.einsum("tkgd,nkd->tkgn", query, keys, preferred_element_type=jnp.float32) * scale
    live = mask[:, None, None, :]
    scores = jnp.where(live, scores, NEG)
    top = jnp.max(scores, axis=-1)
    weights = jnp.where(live, jnp.exp(scores - top[..., None]), 0.0)
    total = jnp.sum(weights, axis=-1)
    acc = jnp.einsum(
        "tkgn,nkd->tkgd", weights.astype(jnp.bfloat16), values, preferred_element_type=jnp.float32
    )
    return acc / total[..., None]


def general(
    text,
    input_gain,
    q_weight,
    kv_weight,
    o_weight,
    q_gain,
    k_gain,
    attn_gate,
    vision,
    segment_ids,
    seg_images,
    image_slot,
):
    tokens_here = text.shape[0]
    head_dim = q_gain.shape[0]
    ctx_count = lax.axis_size("ctx")
    img_count = lax.axis_size("img")
    heads_here = q_weight.shape[1] // head_dim
    kv_heads = max(1, KVH // img_count)
    group = heads_here // kv_heads
    slots_here, vt_dev = vision.shape[:2]
    rows_here = slots_here * vt_dev

    o_full = lax.all_gather(o_weight, "ctx", axis=1, tiled=True)
    vision_cols = lax.all_to_all(
        vision.reshape(rows_here, -1), "ctx", split_axis=1, concat_axis=0, tiled=True
    )
    hidden = head_norm(text.astype(jnp.float32), input_gain).astype(jnp.bfloat16)
    hidden_cols = lax.all_to_all(hidden, "ctx", split_axis=1, concat_axis=0, tiled=True)

    kv_share = jnp.dot(vision_cols, kv_weight, preferred_element_type=jnp.float32)
    kv_shares = lax.all_to_all(
        kv_share.reshape(ctx_count, rows_here, -1), "ctx", split_axis=0, concat_axis=0, tiled=True
    )
    projected = jnp.sum(kv_shares, axis=0).reshape(rows_here, KVH, 2, head_dim)
    keys = head_norm(projected[:, :, 0], k_gain).astype(jnp.bfloat16)
    values = projected[:, :, 1].astype(jnp.bfloat16)
    kv_rows = jnp.stack((keys, values), axis=2)
    owners = jnp.arange(img_count)[:, None] * KVH // img_count + jnp.arange(kv_heads)[None, :]
    kv_out = jnp.take(kv_rows, owners, axis=1).transpose(1, 0, 2, 3, 4)
    kv_in = lax.all_to_all(kv_out, "img", split_axis=0, concat_axis=0, tiled=True)
    kv_all = lax.all_gather(kv_in, "ctx", axis=0, tiled=False)

    q_share = jnp.dot(hidden_cols, q_weight, preferred_element_type=jnp.float32)
    q_shares = lax.all_to_all(
        q_share.astype(jnp.bfloat16).reshape(ctx_count, tokens_here, -1),
        "ctx",
        split_axis=0,
        concat_axis=0,
        tiled=True,
    )
    query = jnp.sum(q_shares.astype(jnp.float32), axis=0)
    query = head_norm(query.reshape(tokens_here, kv_heads, group, head_dim), q_gain).astype(
        jnp.bfloat16
    )

    slots = img_count * slots_here
    own_slots = jnp.take(image_slot, jnp.take(seg_images, segment_ids, axis=0), axis=0)
    slot_ids = jnp.arange(slots, dtype=jnp.int32)
    sees = jnp.any(own_slots[:, :, None] == slot_ids[None, None, :], axis=1)
    flat = kv_all.reshape(ctx_count * slots * vt_dev, kv_heads, 2, head_dim)
    mask = jnp.broadcast_to(
        sees[:, None, :, None], (tokens_here, ctx_count, slots, vt_dev)
    ).reshape(tokens_here, -1)
    context = attend(query, flat[:, :, 0], flat[:, :, 1], mask)
    context = context.astype(jnp.bfloat16).reshape(tokens_here, heads_here * head_dim)
    partial_terms = jnp.dot(context, o_full, preferred_element_type=jnp.float32)
    width = partial_terms.shape[1] // img_count
    shares = lax.all_to_all(
        partial_terms.astype(jnp.bfloat16).reshape(tokens_here, img_count, width),
        "img",
        split_axis=1,
        concat_axis=1,
        tiled=True,
    )
    update = jnp.sum(shares.astype(jnp.float32), axis=1)
    own_text = lax.dynamic_slice_in_dim(text, lax.axis_index("img") * width, width, 1)
    return (own_text.astype(jnp.float32) + jnp.tanh(attn_gate[0]) * update).astype(jnp.bfloat16)


BF16, F32 = jnp.bfloat16, jnp.float32
SMEM = pl.BlockSpec(memory_space=pltpu.SMEM)
VMEM = pl.BlockSpec(memory_space=pltpu.VMEM)
CHIPS = 4


def call(kernel, args, specs, outs, out_specs=None, scratch=(), flops=0, size=0, name=None, grid=(), limit=24):
    return pl.pallas_call(
        kernel,
        out_shape=outs,
        in_specs=specs,
        out_specs=[VMEM] * len(outs) if out_specs is None else out_specs,
        scratch_shapes=scratch,
        grid=grid,
        compiler_params=pltpu.CompilerParams(vmem_limit_bytes=limit * 2**20),
        cost_estimate=pl.CostEstimate(flops=flops, bytes_accessed=size, transcendentals=0),
        name=name,
    )(*args)


def block(index, size):
    return pl.ds(pl.multiple_of(index * size, size), size)


def start_kernel(where, text_hbm, gain, vis_hbm, q_hbm, *refs):
    pieces, refs = refs[:CHIPS], refs[CHIPS:]
    near, far, text_keep, text_give, q_keep, q_give, text, vis, scale, sems = refs
    chip, core, plane = where[0], where[1], where[2]
    tokens, width = text.shape
    part = width // 2
    half = text_keep.shape[1]
    step = 16
    first = pltpu.make_async_copy(vis_hbm, vis, sems.at[0])
    first.start()
    copies = []
    for k, r in enumerate(range(0, tokens, 2 * step)):
        rows = pl.ds(r, 2 * step)
        copies.append(pltpu.make_async_copy(text_hbm.at[rows, :], text.at[rows, :], sems.at[3 + k]))
        copies[-1].start()
    cuts = [
        pltpu.make_async_copy(q_hbm.at[:, block(core, half)], q_keep, sems.at[1]),
        pltpu.make_async_copy(q_hbm.at[:, block(1 - core, half)], q_give, sems.at[2]),
    ]
    for copy in cuts:
        copy.start()
    first.wait()
    for s in range(CHIPS):
        pieces[s][...] = vis[:, block(chip ^ s, pieces[s].shape[1])]
    for r in range(0, tokens, step):
        if r % (2 * step) == 0:
            copies[r // (2 * step)].wait()
        x = text[r : r + step, :].astype(F32)
        mean_sq = jnp.mean(x * x, axis=-1, keepdims=True)
        scale[r : r + step, :] = jnp.broadcast_to(lax.rsqrt(mean_sq + EPS), (step, 128))
    line = chip // 2
    for out, index in ((far, 1 - line), (near, line)):
        cols = block(index, part)
        row_gain = gain[:, cols]
        for r in range(0, tokens, step):
            x = text[r : r + step, cols].astype(F32)
            out[r : r + step, :] = (x * scale[r : r + step, 0:1] * row_gain).astype(BF16)
    text_keep[...] = text[:, block(2 * plane + core, half)]
    text_give[...] = text[:, block(2 * plane + 1 - core, half)]
    for copy in cuts:
        copy.wait()


def kv_kernel(where, vis, vis_other, kv_own, kv_other, *refs):
    shares, (other, near_total, sems) = refs[:CHIPS], refs[CHIPS:]
    core = where[1]
    rows = kv_own.shape[0]
    head = kv_own.shape[1] // (2 * CHIPS)
    copies = []
    for j in range(CHIPS):
        copies.append(
            pltpu.make_async_copy(
                kv_other.at[:, block(2 * j + core, head)],
                other.at[:, pl.ds(j * head, head)],
                sems.at[j],
            )
        )
        copies[-1].start()
    near, far = block(core, rows), block(1 - core, rows)
    x_near = jnp.concatenate((vis[:, near], vis_other[:, near]), axis=0)
    x_far = jnp.concatenate((vis[:, far], vis_other[:, far]), axis=0)
    total = vis.shape[0]
    count = total // CHIPS
    for j in range(CHIPS):
        near_total[:, j * head : (j + 1) * head] = jnp.dot(
            x_near, kv_own[:, block(2 * j + core, head)], preferred_element_type=F32
        )
    for j in range(CHIPS):
        copies[j].wait()
        cols = slice(j * head, (j + 1) * head)
        out = near_total[:, cols] + jnp.dot(x_far, other[:, cols], preferred_element_type=F32)
        for s in range(CHIPS):
            shares[s][:count, cols] = out[s * count : (s + 1) * count]
            shares[s][count:, cols] = out[total + s * count : total + (s + 1) * count]


def kv_norm_kernel(where, k_gain, *refs):
    shares, (here, there, give) = refs[:CHIPS], refs[CHIPS:]
    plane = where[2]
    lines, head = here.shape
    dim = head // 2
    for t, (out, row) in enumerate(((here, 0), (give, 0), (there, 0), (give, lines))):
        cols = block(plane ^ t, head)
        total = (shares[0][:, cols] + shares[1][:, cols]) + (shares[2][:, cols] + shares[3][:, cols])
        keys = head_norm(total[:, :dim], k_gain[...])
        out[row : row + lines, :dim] = keys.astype(BF16)
        out[row : row + lines, dim:] = total[:, dim:].astype(BF16)


def kv_turn_kernel(there, landed, out):
    lines = there.shape[0]
    out[:lines, :] = there[...]
    out[lines:, :] = landed[lines:, :]


def kv_join_kernel(here, landed, last, out):
    lines = here.shape[0]
    out[:lines, :] = here[...]
    out[lines : 2 * lines, :] = landed[:lines, :]
    out[2 * lines :, :] = last[...]


def query_share(index, own, other, first, second, flip):
    rows = first.shape[0]
    total = None
    for weight, k in ((first, index), (second, index ^ flip)):
        cols = block(k, rows)
        x = jnp.concatenate((own[:, cols], other[:, cols]), axis=0)
        share = jnp.dot(x, weight[...], preferred_element_type=F32)
        total = share if total is None else total + share
    return total


def early_kernel(where, own, other, q_keep, q_other, out):
    index = 2 * lax.rem(where[0], 2) + where[1]
    out[...] = query_share(index, own, other, q_keep, q_other, 1)


def late_kernel(where, own, other, q_side, q_corner, early, out):
    index = (2 * lax.rem(where[0], 2) + where[1]) ^ 2
    share = early[...] + query_share(index, own, other, q_side, q_corner, 1)
    out[...] = share.astype(out.dtype)


def attend_kernel(q_gain, first, landed, *refs):
    kv, (bias, context) = refs[:CHIPS], refs[CHIPS:]
    dim = q_gain.shape[1]
    rows, half = context.shape
    keys = jnp.concatenate([x[:, :dim] for x in kv], axis=0)
    values = jnp.concatenate([x[:, dim:] for x in kv], axis=0)
    step = 128
    for r in range(0, rows, step):
        for g in range(half // dim):
            cols = slice(g * dim, (g + 1) * dim)
            query = first[r : r + step, cols] + landed[r : r + step, cols].astype(F32)
            query = head_norm(query, q_gain[...]).astype(BF16)
            scores = lax.dot_general(
                query, keys, (((1,), (1,)), ((), ())), preferred_element_type=F32
            )
            scores = scores * dim ** (-0.5) + bias[r : r + step, :]
            weights = jnp.exp(scores - jnp.max(scores, axis=-1, keepdims=True))
            total = jnp.sum(weights, axis=-1, keepdims=True)
            acc = jnp.dot(weights.astype(BF16), values, preferred_element_type=F32)
            context[r : r + step, cols] = (acc / total).astype(BF16)


def out_kernel(where, near, far, o_own, o_early, o_late, own, other):
    core = where[1]
    tokens, width = own.shape
    half = near.shape[1]
    turned = jnp.concatenate((far[tokens:, :], far[:tokens, :]), axis=0)
    share = jnp.dot(near[...], o_own[block(core, half), :], preferred_element_type=F32)
    share += jnp.dot(turned, o_own[block(1 - core, half), :], preferred_element_type=F32)
    own[:, : width // 2] = share[:tokens].astype(BF16)
    other[:, : width // 2] = share[tokens:].astype(BF16)
    top = jnp.where(core == 0, near[...], turned)
    low = jnp.where(core == 0, turned, near[...])
    share = jnp.dot(top, o_early[...], preferred_element_type=F32)
    share += jnp.dot(low, o_late[...], preferred_element_type=F32)
    own[:, width // 2 :] = share[:tokens].astype(BF16)
    other[:, width // 2 :] = share[tokens:].astype(BF16)


def pick_kernel(where, own, landed, *outs):
    first = where[0] ^ where[2]
    half = outs[0].shape[1]
    for t in range(CHIPS):
        for s in range(CHIPS):

            @pl.when((first ^ t) == s)
            def _():
                outs[t][...] = (own, landed)[s % 2][:, (s // 2) * half : (s // 2 + 1) * half]


def mixed_rows(gate, text, shares):
    x = [share[...].astype(F32) for share in shares]
    update = (x[0] + x[1]) + (x[2] + x[3])
    return (text[...].astype(F32) + gate[0] * update).astype(BF16)


def give_kernel(gate, text, *refs):
    refs[CHIPS][...] = mixed_rows(gate, text, refs[:CHIPS])


def last_kernel(where, gate, text, back, *refs):
    shares, out = refs[:CHIPS], refs[CHIPS]
    core = where[1]
    half = text.shape[1]
    out[:, block(core, half)] = mixed_rows(gate, text, shares)
    out[:, block(1 - core, half)] = back[...]


def paired(
    text,
    input_gain,
    q_weight,
    kv_weight,
    o_weight,
    q_gain,
    k_gain,
    attn_gate,
    vision,
    segment_ids,
    seg_images,
    image_slot,
):
    ctx_count = lax.axis_size("ctx")
    place, plane = lax.axis_index("ctx"), lax.axis_index("img")
    chip, core = place // 2, place % 2
    where = jnp.stack((chip, core, plane)).astype(jnp.int32)
    tokens, width = text.shape
    head_dim = q_gain.shape[0]
    rows_dev, cols_plane = q_weight.shape
    half = cols_plane // 2
    part = 2 * rows_dev
    slots_here, vt_dev = vision.shape[:2]
    vis_here = slots_here * vt_dev
    kv_cols = kv_weight.shape[1] // 2

    def shape(rows, cols, kind=BF16):
        return jax.ShapeDtypeStruct((rows, cols), kind)

    def swap(x):
        return lax.ppermute(x, "ctx", [(k, k ^ 1) for k in range(ctx_count)])

    def peer(x, s):
        return lax.ppermute(x, "ctx", [(k, k ^ (2 * s)) for k in range(ctx_count)])

    def along_x(x):
        return peer(x, 1)

    def along_y(x):
        return peer(x, 2)

    def across(x, t):
        return lax.ppermute(x, "img", [(k, k ^ t) for k in range(CHIPS)])

    steps = range(1, CHIPS)
    vis = vision.reshape(vis_here, width)
    kv_other = swap(kv_weight)

    anywhere = pl.BlockSpec(memory_space=pl.ANY)
    *vis_pieces, near, far, text_keep, text_give, q_keep, q_give = call(
        start_kernel,
        (where, text, input_gain[None], vis, q_weight),
        [SMEM, anywhere, VMEM, anywhere, anywhere],
        [shape(vis_here, part)] * CHIPS
        + [shape(tokens, width // 2)] * 2
        + [shape(tokens, half)] * 2
        + [shape(rows_dev, half)] * 2,
        scratch=[
            pltpu.VMEM((tokens, width), BF16),
            pltpu.VMEM((vis_here, width), BF16),
            pltpu.VMEM((tokens, 128), F32),
            pltpu.SemaphoreType.DMA((3 + tokens // 32,)),
        ],
        flops=8 * tokens * width,
        size=4 * 2**20,
        name="start",
        limit=60,
    )
    vis_own = jnp.concatenate([vis_pieces[0]] + [peer(vis_pieces[s], s) for s in steps])
    vis_other = swap(vis_own)
    q_side, q_other = along_x(q_keep), swap(q_give)
    far = along_y(far)

    shares = call(
        kv_kernel,
        (where, vis_own, vis_other, kv_weight, kv_other),
        [SMEM] + [VMEM] * 3 + [pl.BlockSpec(memory_space=pl.ANY)],
        [shape(2 * vis_here, kv_cols, F32)] * CHIPS,
        scratch=[
            pltpu.VMEM((rows_dev, kv_cols), BF16),
            pltpu.VMEM((8 * vis_here, kv_cols), F32),
            pltpu.SemaphoreType.DMA((CHIPS,)),
        ],
        flops=4 * vis_here * ctx_count * part * kv_cols,
        size=4 * 2**20,
        name="kv_shares",
    )
    shares = [shares[0]] + [peer(shares[s], s) for s in steps]
    own_share = shares[0]
    q_behind, _ = lax.optimization_barrier((q_other, (own_share, q_side)))
    q_corner = along_x(q_behind)
    shares, q_side, far = lax.optimization_barrier((shares, q_side, far))
    here, there, give = call(
        kv_norm_kernel,
        (where, k_gain[None], *shares),
        [SMEM] + [VMEM] * (1 + CHIPS),
        [shape(2 * vis_here, 2 * head_dim)] * 2 + [shape(4 * vis_here, 2 * head_dim)],
        name="kv_norm",
    )
    blocks = ((far, swap(far)), (near, swap(near)))
    early = [
        call(
            early_kernel,
            (where, *pair, q_keep, q_other),
            [SMEM] + [VMEM] * 4,
            [shape(2 * tokens, half, F32)],
            flops=4 * tokens * part * half,
            size=2 * 2**20,
            name="q_early",
        )[0]
        for pair in blocks
    ]
    kv_z = across(give, 1)
    o_early, _ = lax.optimization_barrier((o_weight[:half], here))
    o_early = along_y(o_early)
    q_far, q_first = [
        call(
            late_kernel,
            (where, *blocks[k], q_side, q_corner, early[k]),
            [SMEM] + [VMEM] * 5,
            [shape(2 * tokens, half, kind)],
            flops=40 * tokens * part * half,
            size=2 * 2**20,
            name="q_late",
        )[0]
        for k, kind in ((0, BF16), (1, F32))
    ]
    turn = call(
        kv_turn_kernel,
        (there, kv_z),
        [VMEM] * 2,
        [shape(4 * vis_here, 2 * head_dim)],
        name="kv_turn",
    )[0]
    kv_last, o_early, _ = lax.optimization_barrier((across(turn, 2), o_early, q_far))
    kv_first = call(
        kv_join_kernel,
        (here, kv_z, kv_last),
        [VMEM] * 3,
        [shape(8 * vis_here, 2 * head_dim)],
        name="kv_join",
    )[0]
    kv_first, _ = lax.optimization_barrier((kv_first, q_first))
    kv_all = [kv_first] + [peer(kv_first, s) for s in steps]

    landed = along_y(q_far)
    o_late, _ = lax.optimization_barrier((o_weight[half:], q_far))
    o_late = along_y(o_late)

    ids = jnp.concatenate((segment_ids, swap(segment_ids)))
    images = jnp.arange(image_slot.shape[0])
    slot_of = jnp.sum(
        jnp.where(seg_images[:, :, None] == images, image_slot[None, None, :], 0), axis=2
    )
    numbers = jnp.arange(seg_images.shape[0])
    own_slots = jnp.sum(
        jnp.where((ids[:, None] == numbers)[:, :, None], slot_of[None], 0), axis=1
    )
    key_rows = jnp.arange(CHIPS * CHIPS * 2 * vis_here)
    key_plane = plane ^ (key_rows // (2 * vis_here) % CHIPS)
    key_slot = key_plane * slots_here + key_rows // vt_dev % slots_here
    sees = jnp.any(own_slots[:, :, None] == key_slot, axis=1)
    bias = jnp.where(sees, 0.0, NEG).astype(F32)

    context = call(
        attend_kernel,
        (q_gain[None], q_first, landed, *kv_all, bias),
        [VMEM] * (4 + CHIPS),
        [shape(2 * tokens, half)],
        flops=8 * tokens * half * bias.shape[1],
        size=2 * 2**20,
        name="attend",
    )[0]

    context_x = along_x(context)
    shares = [
        call(
            out_kernel,
            (where, x, swap(x), o_weight, o_early, o_late),
            [SMEM] + [VMEM] * 5,
            [shape(tokens, 2 * half)] * 2,
            flops=8 * tokens * cols_plane * half,
            size=2 * 2**20,
            name="o_share",
        )
        for x in (context_x, context)
    ]
    summands = []
    for rows in (1, 0):
        picked = call(
            pick_kernel,
            (where, shares[1][rows], along_x(shares[0][rows])),
            [SMEM] + [VMEM] * 2,
            [shape(tokens, half)] * CHIPS,
            flops=2**20,
            size=2**20,
            name="pick",
        )
        summands.append([picked[0]] + [across(picked[t], t) for t in steps])
    gate = jnp.tanh(attn_gate)
    give = call(
        give_kernel,
        (gate, swap(text_give), *summands[0]),
        [SMEM] + [VMEM] * (1 + CHIPS),
        [shape(tokens, half)],
        flops=2**20,
        size=2**20,
        name="mix_give",
    )[0]
    return call(
        last_kernel,
        (where, gate, text_keep, swap(give), *summands[1]),
        [SMEM, SMEM] + [VMEM] * (2 + CHIPS),
        [shape(tokens, 2 * half)],
        flops=2**20,
        size=2**20,
        name="mix_keep",
    )[0]


def solution(mesh):
    fits = mesh.shape["img"] == 4 and mesh.shape["ctx"] == 8
    return jax.shard_map(
        paired if fits else general,
        mesh=mesh,
        in_specs=(
            P("ctx", None),
            P(),
            P("ctx", "img"),
            P("ctx", None),
            P("img", "ctx"),
            P(),
            P(),
            P(),
            P("img", "ctx", None),
            P("ctx"),
            P(),
            P(),
        ),
        out_specs=P("ctx", "img"),
        check_vma=False,
    )
```
